512 devices in a mesh: ta: 4 (over y), gx: 16 (over z), gy: 8 (over x, core).
Axes of the slice: x: 4, y: 4, z: 16, core: 2. Of those that a mesh axis runs over, the one named last changes fastest.
Arguments:
- links: float32 [3, 2, 3, 3, 128, 128, 512], P(None, None, None, None, 'gx', 'gy', 'ta'), parts along dimension 6, may hold values from -1 to 1, as said below
Outputs:
- gauge: float32 [2, 2, 3, 128, 128, 512], P(None, None, None, 'gx', 'gy', 'ta'), parts along dimension 5
- divergence: float32 [8, 128, 128, 512], P(None, 'gx', 'gy', 'ta'), parts along dimension 3
- theta: float32 [12], P('ta'), parts along dimension 0
The draws below stay inside these ranges and needn't reach their ends.
There are 4 independent parts, one for each index of `ta`. The reference program is written for one: setup_inputs(seed, part) draws one part's arguments, and reference() takes and returns one part's arrays. A program takes and returns all parts, laid end to end along the dimension named above; each array names one. Nothing has to cross between parts.
Inputs may be any that keep to these rules, and one draw needn't show every extreme that they name: `links`: each link matrix is special unitary.
All inputs are finite; a program needn't handle non-finite values.
Results may differ from the reference program's by a relative error of at most 0.0003.
Values sent between devices are 32-bit elements; how exact they have to be, the bound alone decides.
No kernel may reach another device: no remote copies, remote signals or barrier semaphores. Data moves between devices by JAX's collectives and lax.ppermute only.
A program may use at most 128 MiB of HBM per device.

```python
import math
import jax
import jax.numpy as jnp
from jax import lax

LS = 128
NZ = 128
ITERS = 2


def normed_row(row):
    size = jnp.sqrt(jnp.sum(row[0] * row[0] + row[1] * row[1], axis=0))
    return row / size


def special_rows(matrix):
    first = normed_row(matrix[:, 0])
    second = matrix[:, 1]
    proj_re = jnp.sum(first[0] * second[0] + first[1] * second[1], axis=0)
    proj_im = jnp.sum(first[0] * second[1] - first[1] * second[0], axis=0)
    second = jnp.stack([second[0] - (proj_re * first[0] - proj_im * first[1]), second[1] - (proj_re * first[1] + proj_im * first[0])])
    second = normed_row(second)
    cross_re = []
    cross_im = []
    for entry in range(3):
        after = (entry + 1) % 3
        later = (entry + 2) % 3
        part_re = first[0, after] * second[0, later] - first[1, after] * second[1, later]
        part_re = part_re - (first[0, later] * second[0, after] - first[1, later] * second[1, after])
        part_im = first[0, after] * second[1, later] + first[1, after] * second[0, later]
        part_im = part_im - (first[0, later] * second[1, after] + first[1, later] * second[0, after])
        cross_re.append(part_re)
        cross_im.append(-part_im)
    third = jnp.stack([jnp.stack(cross_re), jnp.stack(cross_im)])
    return jnp.stack([first, second, third], axis=1)


def draw_links(key, part):
    key = jax.random.fold_in(key, 7)
    low_amp = 0.3
    high_amp = 3.0
    place = jnp.arange(LS).astype(jnp.float32) / (LS - 1.0)
    amp = jnp.exp(jnp.log(low_amp) + (jnp.log(high_amp) - jnp.log(low_amp)) * place).reshape(LS, 1, 1)
    raw = jax.random.normal(key, (3, 2, 3, 3, LS, LS, NZ), jnp.float32)
    eye = jnp.eye(3, dtype=jnp.float32).reshape(3, 3, 1, 1, 1)
    made = []
    for mu in range(3):
        matrix = jnp.stack([amp * raw[mu, 0] + eye, amp * raw[mu, 1]])
        made.append(special_rows(matrix))
    return jnp.stack(made)


def setup_inputs(seed: int = 0, part: int = 0) -> dict:
    streams_of = jax.random.split(jax.random.key(seed), 2)
    own_keys = jax.random.split(jax.random.fold_in(streams_of[1], part), 2)
    links = draw_links(jax.random.fold_in(jax.random.fold_in(streams_of[1], part), 71), part)
    return {"links": links}


STEP_SIZE = 0.08
PEAK_MOMENTUM = 12.0

def prod_three(left, right):
    return lax.optimization_barrier(jnp.sum(left[:, :, None] * right[None, :, :], axis=1))

def complex_product(left, right):
    real = prod_three(left[0], right[0]) - prod_three(left[1], right[1])
    imag = prod_three(left[0], right[1]) + prod_three(left[1], right[0])
    return jnp.stack([real, imag])

def dagger(matrix):
    return jnp.stack([jnp.swapaxes(matrix[0], 0, 1), -jnp.swapaxes(matrix[1], 0, 1)])

def algebra(matrix):
    mreal, mimag = (matrix[0], matrix[1])
    middle = (mimag[0, 0] + mimag[1, 1] + mimag[2, 2]) / 3.0
    return jnp.stack([mimag[0, 0] - middle, mimag[1, 1] - middle, (mreal[0, 1] - mreal[1, 0]) / 2.0, (mimag[0, 1] + mimag[1, 0]) / 2.0, (mreal[0, 2] - mreal[2, 0]) / 2.0, (mimag[0, 2] + mimag[2, 0]) / 2.0, (mreal[1, 2] - mreal[2, 1]) / 2.0, (mimag[1, 2] + mimag[2, 1]) / 2.0])

def squares(comps):
    third = comps[0] + comps[1]
    rest = lax.optimization_barrier(jnp.sum(comps[2:] * comps[2:], axis=0))
    return comps[0] * comps[0] + comps[1] * comps[1] + third * third + 2.0 * rest

def to_matrix(comps):
    zero = jnp.zeros_like(comps[0])
    real = jnp.stack([jnp.stack([zero, comps[2], comps[4]]), jnp.stack([-comps[2], zero, comps[6]]), jnp.stack([-comps[4], -comps[6], zero])])
    imag = jnp.stack([jnp.stack([comps[0], comps[3], comps[5]]), jnp.stack([comps[3], comps[1], comps[7]]), jnp.stack([comps[5], comps[7], -comps[0] - comps[1]])])
    return jnp.stack([real, imag])

def identity_like(tail):
    eye = jnp.eye(3, dtype=jnp.float32).reshape((3, 3) + (1,) * len(tail))
    real = jnp.broadcast_to(eye, (3, 3) + tuple(tail))
    return jnp.stack([real, jnp.zeros_like(real)])

def normed(row):
    size = jnp.sqrt(lax.optimization_barrier(jnp.sum(row[0] * row[0] + row[1] * row[1], axis=0)))
    return row / size

def unitarize(matrix):
    first = normed(matrix[:, 0])
    second = matrix[:, 1]
    proj_re = lax.optimization_barrier(jnp.sum(first[0] * second[0] + first[1] * second[1], axis=0))
    proj_im = lax.optimization_barrier(jnp.sum(first[0] * second[1] - first[1] * second[0], axis=0))
    second = jnp.stack([second[0] - (proj_re * first[0] - proj_im * first[1]), second[1] - (proj_re * first[1] + proj_im * first[0])])
    second = normed(second)
    cross_re = []
    cross_im = []
    for entry in range(3):
        after = (entry + 1) % 3
        later = (entry + 2) % 3
        part_re = first[0, after] * second[0, later] - first[1, after] * second[1, later]
        part_re = part_re - (first[0, later] * second[0, after] - first[1, later] * second[1, after])
        part_im = first[0, after] * second[1, later] + first[1, after] * second[0, later]
        part_im = part_im - (first[0, later] * second[1, after] + first[1, later] * second[0, after])
        cross_re.append(part_re)
        cross_im.append(-part_im)
    third = jnp.stack([jnp.stack(cross_re), jnp.stack(cross_im)])
    return jnp.stack([first, second, third], axis=1)

def exponent(comps):
    step = to_matrix(comps)
    series = identity_like(comps.shape[1:]) + step + 0.5 * complex_product(step, step)
    return unitarize(series)

def divergence_of(links):
    backs = [jnp.roll(links[mu], 1, axis=3 + mu) for mu in range(3)]
    total = backs[0] + backs[1] + backs[2] - links[0] - links[1] - links[2]
    return algebra(total)

def filter_table():
    kx = jnp.arange(LS).astype(jnp.float32)
    kz = jnp.arange(NZ).astype(jnp.float32)
    sx = jnp.sin(kx * (math.pi / LS))
    sz = jnp.sin(kz * (math.pi / NZ))
    total = 4.0 * sx[:, None, None] ** 2 + 4.0 * sx[None, :, None] ** 2 + 4.0 * sz[None, None, :] ** 2
    anchor = ((jnp.arange(LS)[:, None, None] == 0) & (jnp.arange(LS)[None, :, None] == 0) & (jnp.arange(NZ)[None, None, :] == 0)).astype(jnp.float32)
    return PEAK_MOMENTUM / (total + anchor) * (1.0 - anchor)

def accelerate(comps):
    spectrum = jnp.fft.fftn(comps, axes=(1, 2, 3))
    back = jnp.fft.ifftn(spectrum * filter_table(), axes=(1, 2, 3))
    return jnp.real(back).astype(jnp.float32)

def reference(links):
    gauge = identity_like(links.shape[4:])
    thetas = []
    comps = divergence_of(links)
    for step in range(ITERS + 1):
        comps = divergence_of(links)
        thetas.append(jnp.sum(squares(comps)) / (3.0 * LS * LS * NZ))
        if step == ITERS:
            break
        transform = exponent(STEP_SIZE * accelerate(comps))
        moved = []
        for mu in range(3):
            ahead = jnp.roll(transform, -1, axis=3 + mu)
            moved.append(complex_product(complex_product(transform, links[mu]), dagger(ahead)))
        links = jnp.stack(moved)
        gauge = complex_product(transform, gauge)
    return (gauge[:, :2], comps, jnp.stack(thetas))
```

```python
import math

import jax
import jax.numpy as jnp
import numpy as np
from jax import lax
from jax.experimental import pallas as pl
from jax.experimental.pallas import tpu as pltpu
from jax.sharding import PartitionSpec as P

LS = 128
NZ = 128
STEP_SIZE = 0.08
PEAK_MOMENTUM = 12.0
NGX = 16
NGY = 8
F32 = jnp.float32
BF16 = jnp.bfloat16
MEGA = 1024 * 1024


def real_basis(length):
    site = np.arange(length)[:, None]
    freq = np.arange(length)
    freq = np.where(freq <= length // 2, freq, freq - length // 2)
    phase = 2.0 * np.pi * ((site * freq[None, :]) % length) / length
    index = np.arange(length)[None, :]
    basis = np.where(index <= length // 2, np.cos(phase), np.sin(phase)) * np.sqrt(2.0 / length)
    basis[:, 0] = 1.0 / np.sqrt(length)
    basis[:, length // 2] = np.cos(np.pi * np.arange(length)) / np.sqrt(length)
    return basis, freq


def halves(table):
    high = table.astype(np.float32).astype(jnp.bfloat16)
    low = (table - high.astype(np.float64)).astype(np.float32).astype(jnp.bfloat16)
    return high, low


def right_table(table):
    high, low = halves(table)
    return np.concatenate([high, high, low], axis=0)


def left_table(table):
    high, low = halves(table)
    return np.concatenate([high, high, low], axis=1)


def ring_table(squares_y, squares_z):
    mass = squares_y[:, None] + squares_z[None, :]
    weight = np.zeros_like(mass)
    product = np.ones_like(mass)
    for _ in range(7):
        weight = 1.0 / (2.0 + mass - weight)
        product = product * weight
    diag = 2.0 + mass - 2.0 * weight
    out = np.zeros((9,) + mass.shape)
    for mode in range(16):
        eigen = diag - 2.0 * product * math.cos(2.0 * math.pi * mode / 16)
        if mode == 0:
            eigen[0, 0] = np.inf
        for dist in range(9):
            out[dist] += math.cos(2.0 * math.pi * mode * dist / 16) / eigen / 16.0
    return out


BASIS, FREQ = real_basis(128)
SQUARES = 4.0 * np.sin(np.pi * FREQ / 128.0) ** 2
Z_FORWARD = right_table(BASIS)
Z_BACK = right_table(BASIS.T)
Y_FORWARD = left_table(BASIS.T * (STEP_SIZE * PEAK_MOMENTUM))
Y_BACK = left_table(BASIS)
RING = ring_table(SQUARES, SQUARES).astype(np.float32)


def three_lanes(value):
    high = value.astype(BF16)
    low = (value - high.astype(F32)).astype(BF16)
    return jnp.concatenate([high, low, high], axis=1)


def three_rows(value):
    high = value.astype(BF16)
    low = (value - high.astype(F32)).astype(BF16)
    return jnp.concatenate([high, low, high], axis=0)


def swap_blocks(tiles):
    tiles = list(tiles)
    group = lax.broadcasted_iota(jnp.int32, tiles[0].shape, 1) // 16
    for bit in (1, 2, 4):
        upper = (group & bit) != 0
        for i in range(8):
            if i & bit:
                continue
            low, high = tiles[i], tiles[i | bit]
            tiles[i] = jnp.where(upper, pltpu.roll(high, 16 * bit, 1), low)
            tiles[i | bit] = jnp.where(upper, high, pltpu.roll(low, 128 - 16 * bit, 1))
    return tiles


def algebra(mreal, mimag):
    i00, i11, i22 = mimag(0, 0), mimag(1, 1), mimag(2, 2)
    middle = (i00 + i11 + i22) * (1.0 / 3.0)
    return [
        i00 - middle,
        i11 - middle,
        (mreal(0, 1) - mreal(1, 0)) * 0.5,
        (mimag(0, 1) + mimag(1, 0)) * 0.5,
        (mreal(0, 2) - mreal(2, 0)) * 0.5,
        (mimag(0, 2) + mimag(2, 0)) * 0.5,
        (mreal(1, 2) - mreal(2, 1)) * 0.5,
        (mimag(1, 2) + mimag(2, 1)) * 0.5,
    ]


def squares(c):
    third = c[0] + c[1]
    rest = c[2] * c[2] + c[3] * c[3] + c[4] * c[4] + c[5] * c[5] + c[6] * c[6] + c[7] * c[7]
    return c[0] * c[0] + c[1] * c[1] + third * third + 2.0 * rest


def entry(row, col):
    return row * 3 + col


def cross_row(first_re, first_im, second_re, second_im):
    out_re, out_im = [], []
    for k in range(3):
        a, b = (k + 1) % 3, (k + 2) % 3
        out_re.append(
            first_re[a] * second_re[b]
            - first_im[a] * second_im[b]
            - first_re[b] * second_re[a]
            + first_im[b] * second_im[a]
        )
        out_im.append(
            first_re[b] * second_im[a]
            + first_im[b] * second_re[a]
            - first_re[a] * second_im[b]
            - first_im[a] * second_re[b]
        )
    return out_re, out_im


def exponent_rows(c):
    c0, c1, c2, c3, c4, c5, c6, c7 = c
    n01 = c2 * c2 + c3 * c3
    n02 = c4 * c4 + c5 * c5
    n12 = c6 * c6 + c7 * c7
    s00 = 1.0 - 0.5 * (c0 * c0 + n01 + n02)
    s11 = 1.0 - 0.5 * (c1 * c1 + n01 + n12)
    d01 = c0 + c1
    p01r = -(d01 * c3) - (c4 * c6 + c5 * c7)
    p01i = d01 * c2 - (c5 * c6 - c4 * c7)
    p02r = c1 * c5 + (c2 * c6 - c3 * c7)
    p02i = -(c1 * c4) + (c2 * c7 + c3 * c6)
    p12r = -(c2 * c4 + c3 * c5) + c0 * c7
    p12i = -(c2 * c5 - c3 * c4) - c0 * c6
    r0 = [s00, c2 + 0.5 * p01r, c4 + 0.5 * p02r]
    i0 = [c0, c3 + 0.5 * p01i, c5 + 0.5 * p02i]
    r1 = [-c2 + 0.5 * p01r, s11, c6 + 0.5 * p12r]
    i1 = [c3 - 0.5 * p01i, c1, c7 + 0.5 * p12i]
    size = sum(r0[k] * r0[k] + i0[k] * i0[k] for k in range(3))
    scale = 1.0 / jnp.sqrt(size)
    r0 = [v * scale for v in r0]
    i0 = [v * scale for v in i0]
    pr = sum(r0[k] * r1[k] + i0[k] * i1[k] for k in range(3))
    pi = sum(r0[k] * i1[k] - i0[k] * r1[k] for k in range(3))
    r1, i1 = (
        [r1[k] - (pr * r0[k] - pi * i0[k]) for k in range(3)],
        [i1[k] - (pr * i0[k] + pi * r0[k]) for k in range(3)],
    )
    size = sum(r1[k] * r1[k] + i1[k] * i1[k] for k in range(3))
    scale = 1.0 / jnp.sqrt(size)
    r1 = [v * scale for v in r1]
    i1 = [v * scale for v in i1]
    return r0 + r1, i0 + i1


def full_matrix(re6, im6):
    re3, im3 = cross_row(re6[:3], im6[:3], re6[3:], im6[3:])
    return list(re6) + re3 + list(im6) + im3


def times_rows(gre, gim, hre, him):
    out_re, out_im = [], []
    for i in range(2):
        for j in range(3):
            acc_re = acc_im = None
            for k in range(3):
                ar, ai = gre[entry(i, k)], gim[entry(i, k)]
                br, bi = hre[entry(k, j)], him[entry(k, j)]
                pr, pi = ar * br - ai * bi, ar * bi + ai * br
                acc_re = pr if acc_re is None else acc_re + pr
                acc_im = pi if acc_im is None else acc_im + pi
            out_re.append(acc_re)
            out_im.append(acc_im)
    return out_re, out_im


def moved_algebra(g, link, ahead):
    gre, gim = g[:9], g[9:]
    are, aim = ahead[:9], ahead[9:]
    vre, vim = [None] * 9, [None] * 9
    for i in range(3):
        ur = [link(0, i, k) for k in range(3)]
        ui = [link(1, i, k) for k in range(3)]
        for j in range(3):
            br = [are[entry(j, k)] for k in range(3)]
            bi = [aim[entry(j, k)] for k in range(3)]
            vre[entry(i, j)] = (ur[0] * br[0] + ui[0] * bi[0]) + (
                (ur[1] * br[1] + ui[1] * bi[1]) + (ur[2] * br[2] + ui[2] * bi[2])
            )
            vim[entry(i, j)] = (ui[0] * br[0] - ur[0] * bi[0]) + (
                (ui[1] * br[1] - ur[1] * bi[1]) + (ui[2] * br[2] - ur[2] * bi[2])
            )

    def mreal(i, j):
        return sum(
            gre[entry(i, k)] * vre[entry(k, j)] - gim[entry(i, k)] * vim[entry(k, j)]
            for k in range(3)
        )

    def mimag(i, j):
        return sum(
            gre[entry(i, k)] * vim[entry(k, j)] + gim[entry(i, k)] * vre[entry(k, j)]
            for k in range(3)
        )

    return algebra(mreal, mimag)


def first_kernel(links, face_x, face_y, table, out, theta, prev, rows_in, spectrum):
    step = pl.program_id(0)

    @pl.when(step == 0)
    def _():
        prev[...] = face_x[...]
        theta[...] = jnp.zeros_like(theta)

    def of(mu):
        return algebra(
            lambda i, j: links[mu, 0, i, j, 0], lambda i, j: links[mu, 1, i, j, 0]
        )

    top = lax.broadcasted_iota(jnp.int32, (16, 128), 0) == 0
    ax, ay, az = of(0), of(1), of(2)
    comps = []
    for c in range(8):
        edge = face_y[c, pl.ds(step, 1), :]
        back_y = jnp.where(top, edge, pltpu.roll(ay[c], 1, 0))
        back_z = pltpu.roll(az[c], 1, 1)
        comps.append((prev[c] + back_y + back_z) - ax[c] - ay[c] - az[c])
        prev[c] = ax[c]
        rows_in[pl.ds(16 * c, 16), :] = comps[c]
    sq = squares(comps)
    theta[...] += sq[:8] + sq[8:]
    spectrum[step] = jnp.dot(
        three_lanes(rows_in[...]), table[...], preferred_element_type=F32
    )

    @pl.when(step == 7)
    def _():
        scatter_blocks(spectrum, out)


def scatter_blocks(spectrum, out):
    for c in range(8):
        tiles = swap_blocks([spectrum[x, pl.ds(16 * c, 16), :] for x in range(8)])
        for d in range(8):
            out[d, c] = tiles[d]


def weights_of(mass):
    base = mass + 2.0
    weights = [None, 1.0 / base]
    for _ in range(6):
        weights.append(1.0 / (base - weights[-1]))
    return weights


def forward_kernel(recv, table, mass, spectrum, moments, work):
    for c in range(8):
        block = recv[:, c].reshape(128, 128)
        work[c] = jnp.dot(table[...], three_rows(block), preferred_element_type=F32)
    for group in range(8):
        rows = pl.ds(16 * group, 16)
        tiles = swap_blocks([work[c, rows, :] for c in range(8)])
        for x in range(8):
            spectrum[x, rows, :] = tiles[x]
        w = weights_of(mass[rows, :])
        low = w[1] * tiles[7]
        for k in range(6, 0, -1):
            low = w[8 - k] * (tiles[k] + low)
        low = low + tiles[0]
        high = w[1] * tiles[1]
        for k in range(2, 8):
            high = w[k] * (tiles[k] + high)
        for half in range(2):
            part = slice(8 * half, 8 * half + 8)
            moments[2 * group + half, 0] = low[part]
            moments[2 * group + half, 1] = high[part]
            moments[2 * group + half, 2] = jnp.zeros((8, 128), F32)
        if group == 0:
            total = 3.5 * (tiles[1] + tiles[7]) + 6.0 * (tiles[2] + tiles[6])
            total = total + 7.5 * (tiles[3] + tiles[5]) + 8.0 * tiles[4]
            moments[0, 2] = total[:8]


def ring_kernel(recv, ring, zero, out):
    rhs = [recv[j, 0] + recv[(j + 15) % 16, 1] for j in range(16)]
    shift = recv[0, 2]
    for j in range(1, 16):
        shift = shift + recv[j, 2]
    shift = shift * zero[...]
    coef = [ring[n] for n in range(9)]
    for j in range(16):
        acc = coef[0] * rhs[j] + coef[8] * rhs[(j + 8) % 16]
        for n in range(1, 8):
            acc = acc + coef[n] * (rhs[(j + n) % 16] + rhs[(j - n) % 16])
        acc = acc + shift
        out[j, 0] = acc
        out[(j + 15) % 16, 1] = acc


def back_kernel(spectrum, faces, table, mass, out, work, edges, done):
    for group in range(8):
        rows = pl.ds(16 * group, 16)
        tiles = [spectrum[x, rows, :] for x in range(8)]
        near = jnp.concatenate([faces[2 * group, 0], faces[2 * group + 1, 0]], axis=0)
        far = jnp.concatenate([faces[2 * group, 1], faces[2 * group + 1, 1]], axis=0)
        m = mass[rows, :]
        w = weights_of(m)
        partial = [near]
        for k in range(1, 8):
            partial.append(w[k] * (tiles[k] + partial[-1]))
        value = [None] * 8
        value[0] = near
        last = far
        for k in range(7, 0, -1):
            last = partial[k] + w[k] * last
            value[k] = last
        edges[0, rows, :] = (m + 2.0) * near - value[1] - tiles[0]
        edges[1, rows, :] = far
        value = swap_blocks(value)
        for c in range(8):
            work[c, rows, :] = value[c]
    for c in range(8):
        res = jnp.dot(table[...], three_rows(work[c]), preferred_element_type=F32)
        done[pl.ds(128 * c, 128), :] = res
        out[:, c] = res.reshape(8, 16, 128)
    for side in range(2):
        res = jnp.dot(table[...], three_rows(edges[side]), preferred_element_type=F32)
        out[:, 8 + side] = res.reshape(8, 16, 128)
    for d in range(8):
        before = (16 * d + 127) % 128
        after = (16 * d + 16) % 128
        out[d, 10, pl.ds(0, 8), :] = done[pl.ds(before, 8, stride=128), :]
        out[d, 10, pl.ds(8, 8), :] = done[pl.ds(after, 8, stride=128), :]


PLANE = 18 * 32


def update_body(last, refs):
    if last:
        (recv, links_hbm, face_x, face_y, table_back, prior, prior_y, div, gauge, theta) = refs[:10]
        table = out = gout = gout_y = spectrum = None
        (links, sem, packed, comps_in, gs, edge_g, ay, prev, rows_in) = refs[10:]
    else:
        (recv, links_hbm, face_x, face_y, table_back, table, out, theta, gout, gout_y) = refs[:10]
        prior = prior_y = div = gauge = None
        (links, sem, packed, comps_in, gs, edge_g, ay, prev, rows_in, spectrum) = refs[10:]
    copy = pltpu.make_async_copy(links_hbm, links, sem)
    copy.start()
    theta[...] = jnp.zeros_like(theta)

    for r in range(11):
        tiles = swap_blocks([recv[s, r] for s in range(8)])
        for x in range(8):
            packed[x, pl.ds(16 * r, 16), :] = tiles[x]
    for x in range(8):
        comps_in[pl.ds(176 * x, 176), :] = jnp.dot(
            three_lanes(packed[x]), table_back[...], preferred_element_type=F32
        )

    def make(c, before):
        re6, im6 = exponent_rows(c)
        if before is not None:
            re6, im6 = times_rows(re6, im6, before[:9], before[9:])
        return full_matrix(re6, im6)

    def plane(index, c_of, rows):
        before = None
        if last:
            before = [prior[index, k, rows, :] for k in range(18)]
        g = make(c_of(rows), before)
        start = rows.start + 8
        for k in range(18):
            gs[pl.ds(index * PLANE + 32 * k + start, 8), :] = g[k]
            if not last:
                gout[index, k, rows, :] = g[k]
        if last and isinstance(index, int) is False:
            for p in range(2):
                for i in range(2):
                    for j in range(3):
                        gauge[p, i, j, index - 1, rows, :] = g[9 * p + entry(i, j)]

    def inner(x, carry):
        for half in range(2):
            rows = pl.ds(8 * half, 8)
            plane(
                x + 1,
                lambda rr: [
                    comps_in[pl.ds(176 * x + 16 * c + rr.start, 8), :] for c in range(8)
                ],
                rows,
            )
        return carry

    lax.fori_loop(0, 8, inner, 0)
    for side in range(2):
        for half in range(2):
            rows = pl.ds(8 * half, 8)
            plane(
                9 * side,
                lambda rr: [
                    comps_in[pl.ds(176 * c + 128 + 16 * side + rr.start, 8), :] for c in range(8)
                ],
                rows,
            )
    for side in range(2):
        c = [comps_in[pl.ds(160 + 8 * side + k, 8, stride=176), :] for k in range(8)]
        before = [prior_y[side, k] for k in range(18)] if last else None
        g = make(c, before)
        for k in range(18):
            if not last:
                gout_y[side, k] = g[k]
            if side == 0:
                edge_g[k] = g[k]
            else:
                gs[pl.ds(PLANE + 32 * k + 24, 8, stride=PLANE), :] = g[k]

    g = [edge_g[k] for k in range(18)]
    ahead = [gs[pl.ds(PLANE + 32 * k + 8, 8, stride=PLANE), :] for k in range(18)]
    edge = moved_algebra(g, lambda p, i, j: face_y[p, i, j], ahead)
    for c in range(8):
        ay[pl.ds(24 * c + 7, 8, stride=192), :] = edge[c]
    for half in range(2):
        rows = pl.ds(8 * half, 8)
        start = 8 * half + 8
        g = [gs[pl.ds(32 * k + start, 8), :] for k in range(18)]
        ahead = [gs[pl.ds(PLANE + 32 * k + start, 8), :] for k in range(18)]
        edge = moved_algebra(g, lambda p, i, j: face_x[p, i, j, rows, :], ahead)
        for c in range(8):
            prev[c, rows, :] = edge[c]

    copy.wait()

    def sites(x, carry):
        base = (x + 1) * PLANE
        for half in range(2):
            rows = pl.ds(8 * half, 8)
            start = 8 * half + 8
            total = [None] * 8

            def load_g():
                return [gs[pl.ds(base + 32 * k + start, 8), :] for k in range(18)]

            def link_of(mu):
                return lambda p, i, j: links[mu, p, i, j, x, rows, :]

            g = load_g()
            ahead = [gs[pl.ds(base + PLANE + 32 * k + start, 8), :] for k in range(18)]
            a = moved_algebra(g, link_of(0), ahead)
            for c in range(8):
                total[c] = prev[c, rows, :] - a[c]
                prev[c, rows, :] = a[c]
            ahead = [gs[pl.ds(base + 32 * k + start + 1, 8), :] for k in range(18)]
            a = moved_algebra(g, link_of(1), ahead)
            for c in range(8):
                ay[pl.ds(x * 192 + 24 * c + start, 8), :] = a[c]
            for c in range(8):
                total[c] = total[c] + (ay[pl.ds(x * 192 + 24 * c + start - 1, 8), :] - a[c])
            ahead = [pltpu.roll(v, 127, 1) for v in g]
            a = moved_algebra(g, link_of(2), ahead)
            for c in range(8):
                total[c] = total[c] + (pltpu.roll(a[c], 1, 1) - a[c])
                if last:
                    div[c, x, rows, :] = total[c]
                else:
                    rows_in[pl.ds(16 * c + 8 * half, 8), :] = total[c]
            theta[...] += squares(total)
        if not last:
            spectrum[x] = jnp.dot(
                three_lanes(rows_in[...]), table[...], preferred_element_type=F32
            )
        return carry

    lax.fori_loop(0, 8, sites, 0)
    if not last:
        scatter_blocks(spectrum, out)


def update_kernel(*refs):
    update_body(False, refs)


def last_kernel(*refs):
    update_body(True, refs)


def struct(*shape):
    return jax.ShapeDtypeStruct(shape, F32)


def vmem(*shape):
    return pltpu.VMEM(shape, F32)


def whole():
    return pl.BlockSpec(memory_space=pltpu.VMEM)


def params(size):
    return pltpu.CompilerParams(vmem_limit_bytes=size * MEGA)


def first_call(links, face_x, face_y):
    spec = pl.BlockSpec((3, 2, 3, 3, 1, 16, 128), lambda i: (0, 0, 0, 0, i, 0, 0))

    def fixed(*shape):
        return pl.BlockSpec(shape, lambda i: (0,) * len(shape))

    return pl.pallas_call(
        first_kernel,
        grid=(8,),
        in_specs=[spec, fixed(8, 16, 128), fixed(8, 8, 128), fixed(384, 128)],
        out_specs=[fixed(8, 8, 16, 128), fixed(8, 128)],
        out_shape=[struct(8, 8, 16, 128), struct(8, 128)],
        scratch_shapes=[vmem(8, 16, 128), vmem(128, 128), vmem(8, 128, 128)],
        compiler_params=params(16),
        name="first_divergence",
    )(links, face_x, face_y, jnp.asarray(Z_FORWARD))


def forward_call(recv, mass):
    return pl.pallas_call(
        forward_kernel,
        in_specs=[whole()] * 3,
        out_specs=[whole()] * 2,
        out_shape=[struct(8, 128, 128), struct(16, 3, 8, 128)],
        scratch_shapes=[vmem(8, 128, 128)],
        compiler_params=params(16),
        name="forward_y",
    )(recv, jnp.asarray(Y_FORWARD), mass)


def ring_call(recv, ring, zero):
    return pl.pallas_call(
        ring_kernel,
        in_specs=[whole()] * 3,
        out_specs=whole(),
        out_shape=struct(16, 2, 8, 128),
        compiler_params=params(8),
        name="ring_solve",
    )(recv, ring, zero)


def back_call(spectrum, faces, mass):
    return pl.pallas_call(
        back_kernel,
        in_specs=[whole()] * 4,
        out_specs=whole(),
        out_shape=struct(8, 11, 16, 128),
        scratch_shapes=[vmem(8, 128, 128), vmem(2, 128, 128), vmem(1024, 128)],
        compiler_params=params(16),
        name="back_y",
    )(spectrum, faces, jnp.asarray(Y_BACK), mass)


def update_call(recv, links, face_x, face_y, prior):
    last = prior is not None
    specs = [whole(), pl.BlockSpec(memory_space=pl.ANY), whole(), whole(), whole()]
    scratch = [
        vmem(3, 2, 3, 3, 8, 16, 128),
        pltpu.SemaphoreType.DMA,
        vmem(8, 176, 128),
        vmem(8 * 176, 128),
        vmem(10 * PLANE, 128),
        vmem(18, 8, 128),
        vmem(8 * 192, 128),
        vmem(8, 16, 128),
        vmem(128, 128),
    ]
    operands = [recv, links, face_x, face_y, jnp.asarray(Z_BACK)]
    if last:
        shapes = [struct(8, 8, 16, 128), struct(2, 2, 3, 8, 16, 128), struct(8, 128)]
        operands += list(prior)
        specs += [whole()] * 2
    else:
        shapes = [
            struct(8, 8, 16, 128),
            struct(8, 128),
            struct(10, 18, 16, 128),
            struct(2, 18, 8, 128),
        ]
        operands += [jnp.asarray(Z_FORWARD)]
        specs += [whole()]
        scratch += [vmem(8, 128, 128)]
    return pl.pallas_call(
        last_kernel if last else update_kernel,
        in_specs=specs,
        out_specs=[whole()] * len(shapes),
        out_shape=shapes,
        scratch_shapes=scratch,
        compiler_params=params(32),
        name="last_update" if last else "update",
    )(*operands)


def shifted(value, axis, steps):
    count = lax.axis_size(axis)
    pairs = [(source, (source + steps) % count) for source in range(count)]
    return lax.ppermute(value, axis, pairs)


def exchange(value, axis):
    return lax.all_to_all(value, axis, split_axis=0, concat_axis=0, tiled=True)


def face_algebra(link):
    return jnp.stack(algebra(lambda i, j: link[0, i, j], lambda i, j: link[1, i, j]))


def per_device(links):
    gx, gy = lax.axis_index("gx"), lax.axis_index("gy")
    own_x = links[0, :, :, :, 7]
    own_y = links[1, :, :, :, :, 15]
    near_x = shifted(face_algebra(own_x), "gx", 1)
    near_y = shifted(face_algebra(own_y), "gy", 1)
    face_x = shifted(own_x, "gx", 1)
    face_y = shifted(own_y, "gy", 1)

    squares_y = jnp.asarray(SQUARES.astype(np.float32))[:, None]
    squares_z = jnp.asarray(np.tile(SQUARES.astype(np.float32).reshape(8, 1, 16), (1, 8, 1)).reshape(8, 128))
    mass = squares_y + lax.dynamic_slice(squares_z, (gy, 0), (1, 128))
    ring = lax.dynamic_slice(jnp.asarray(RING), (0, gx * 8, gy * 16), (9, 8, 16))
    ring = jnp.tile(ring, (1, 1, 8))
    lane = lax.broadcasted_iota(jnp.int32, (8, 128), 1)
    row = lax.broadcasted_iota(jnp.int32, (8, 128), 0)
    zero = jnp.where((row + gx + gy == 0) & (lane % 16 == 0), -1.0 / 128.0, 0.0).astype(F32)

    packed, theta0 = first_call(links, near_x, near_y)
    thetas = [theta0]
    prior = None
    for step in range(2):
        spectrum, moments = forward_call(exchange(packed, "gy"), mass)
        faces = exchange(ring_call(exchange(moments, "gx"), ring, zero), "gx")
        back = exchange(back_call(spectrum, faces, mass), "gy")
        if step == 0:
            packed, theta, gout, gout_y = update_call(back, links, face_x, face_y, None)
            prior = (gout, gout_y)
        else:
            div, gauge, theta = update_call(back, links, face_x, face_y, prior)
        thetas.append(theta)
    sums = jnp.sum(jnp.stack(thetas), axis=(1, 2))
    sums = jnp.pad(sums, (0, 125)).reshape(1, 1, 128)
    sums = exchange(jnp.broadcast_to(sums, (8, 1, 128)), "gy")
    sums = jnp.sum(sums, axis=0, keepdims=True)
    sums = exchange(jnp.broadcast_to(sums, (16, 1, 128)), "gx")
    sums = jnp.sum(sums, axis=(0, 1))[:3] / (3.0 * LS * LS * NZ)
    return (gauge, div, sums)


def solution(mesh):
    in_specs = (P(None, None, None, None, "gx", "gy", "ta"),)
    out_specs = (P(None, None, None, "gx", "gy", "ta"), P(None, "gx", "gy", "ta"), P("ta"))
    return jax.shard_map(
        per_device, mesh=mesh, in_specs=in_specs, out_specs=out_specs, check_vma=False
    )
```

```python
import math

import jax
import jax.numpy as jnp
import numpy as np
from jax import lax
from jax.experimental import pallas as pl
from jax.experimental.pallas import tpu as pltpu
from jax.sharding import PartitionSpec as P

LS = 128
NZ = 128
STEP_SIZE = 0.08
PEAK_MOMENTUM = 12.0
F32 = jnp.float32
BF16 = jnp.bfloat16
MEGA = 1024 * 1024


def real_basis(length):
    site = np.arange(length)[:, None]
    freq = np.arange(length)
    freq = np.where(freq <= length // 2, freq, freq - length // 2)
    phase = 2.0 * np.pi * ((site * freq[None, :]) % length) / length
    index = np.arange(length)[None, :]
    basis = np.where(index <= length // 2, np.cos(phase), np.sin(phase)) * np.sqrt(2.0 / length)
    basis[:, 0] = 1.0 / np.sqrt(length)
    basis[:, length // 2] = np.cos(np.pi * np.arange(length)) / np.sqrt(length)
    return basis, freq


def halves(table):
    high = table.astype(np.float32).astype(jnp.bfloat16)
    low = (table - high.astype(np.float64)).astype(np.float32).astype(jnp.bfloat16)
    return high, low


def right_table(table):
    high, low = halves(table)
    return np.concatenate([high, high, low], axis=0)


def left_table(table):
    high, low = halves(table)
    return np.concatenate([high, high, low], axis=1)


def sine_table():
    x, y = np.arange(8), np.arange(16)
    sx = np.sin(np.pi * np.outer(x, x) / 8.0) * np.sqrt(2.0 / 8.0)
    sy = np.sin(np.pi * np.outer(y, y) / 16.0) * np.sqrt(2.0 / 16.0)
    table = np.kron(sx, sy)
    keep = np.kron(x > 0, y > 0)
    table = table * np.outer(keep, keep)
    eigen = (4.0 * np.sin(np.pi * x / 16.0) ** 2)[:, None] + (4.0 * np.sin(np.pi * y / 32.0) ** 2)[None, :]
    return table, eigen.reshape(128), keep


BASIS, FREQ = real_basis(128)
SQUARES = 4.0 * np.sin(np.pi * FREQ / 128.0) ** 2
SINE, EIGEN, INNER = sine_table()


def node(x, y):
    return 16 * x + y


def reduce_table():
    out = np.zeros((48, 256))
    for y in range(16):
        out[y, node(0, y)] = 1.0
        if y > 0:
            out[y, 128:] = SINE[node(1, y)]
            out[16 + y, 128:] = SINE[node(7, y)]
    out[32, 128:] = SINE[INNER].sum(0)
    for x in range(1, 8):
        out[32 + x, node(x, 0)] = 1.0
        out[32 + x, 128:] = SINE[node(x, 1)]
        out[40 + x, 128:] = SINE[node(x, 15)]
    return out


def source_table():
    out = np.zeros((128, 48))
    for y in range(1, 16):
        out[:, y] = SINE[node(1, y)]
        out[:, 16 + y] = SINE[node(7, y)]
    for x in range(1, 8):
        out[:, 32 + x] = SINE[node(x, 1)]
        out[:, 40 + x] = SINE[node(x, 15)]
    return out


def expand_table():
    out = np.zeros((176, 224))
    val, mass = 128, 176

    def line_x(x):
        return 0 if x == 0 else (16 if x == 8 else 32 + x)

    def line_y(y):
        return 40 if y == 16 else y

    for x in range(1, 8):
        for y in range(1, 16):
            out[node(x, y), :128] = SINE[node(x, y)]
    for y in range(16):
        out[node(0, y), val + y] = 1.0
        out[128 + y, val + 16 + y] = 1.0
    for x in range(1, 8):
        out[node(x, 0), val + 32 + x] = 1.0
    for x in range(8):
        out[160 + x, val + 40 + x] = 1.0
    out[144, val + 32] = 1.0
    for y in range(1, 16):
        row = out[144 + y]
        row[val + y] += 4.0
        row[mass + y] += 1.0
        row[:128] -= SINE[node(1, y)]
        row[val + line_y(y - 1)] -= 1.0
        row[val + line_y(y + 1)] -= 1.0
    for x in range(1, 8):
        row = out[168 + x]
        row[val + line_x(x)] += 4.0
        row[mass + line_x(x)] += 1.0
        row[:128] -= SINE[node(x, 1)]
        row[val + line_x(x - 1)] -= 1.0
        row[val + line_x(x + 1)] -= 1.0
    row = out[168]
    row[val] += 4.0
    row[mass] += 1.0
    row[val + 33] -= 1.0
    row[val + 32] -= 1.0
    row[val + 1] -= 1.0
    return out


def lines_in():
    out = np.zeros((128, 128))
    for g in range(8):
        out[16 * g : 16 * g + 16] = BASIS[16 * g]
    return out


def lines_out():
    out = np.zeros((128, 128))
    for g in range(8):
        out[:, 16 * g : 16 * g + 8] = BASIS[16 * g][:, None]
        out[:, 16 * g + 8 : 16 * g + 16] = BASIS[(16 * g + 16) % 128][:, None]
    return out


SCALE = STEP_SIZE * PEAK_MOMENTUM
ORDER = np.array([8 * j + x for x in range(8) for j in range(16)])


def pack_tables():
    out = np.zeros((864, 768), jnp.bfloat16)
    rights = (BASIS * SCALE, BASIS.T, BASIS, lines_in(), lines_out())
    for k, table in enumerate(rights):
        out[:384, 128 * k : 128 * k + 128] = right_table(table)
    out[384:512, :384] = left_table(SINE)
    out[384:512, 384:] = left_table(BASIS[ORDER].T)
    out[512:640, :384] = left_table(BASIS[ORDER])
    out[512:640, 384:528] = left_table(source_table())
    out[640:688, :] = left_table(reduce_table())
    out[688:864, :672] = left_table(expand_table())
    return out


COARSE = pack_tables()
INVERSE = INNER[:, None] / (np.where(INNER, EIGEN, 1.0)[:, None] + SQUARES[None, :])
PLANE_SUM = SQUARES[:, None] + SQUARES[None, :]
FINE = np.concatenate([INVERSE, PLANE_SUM]).astype(np.float32)
Z_IN, Z_OUT, Y_IN, LINES_IN, LINES_OUT = [(slice(0, 384), slice(128 * k, 128 * k + 128)) for k in range(5)]
MODES = (slice(384, 512), slice(0, 384))
X_IN = (slice(384, 512), slice(384, 768))
X_OUT = (slice(512, 640), slice(0, 384))
SOURCE = (slice(512, 640), slice(384, 528))
REDUCE = (slice(640, 688), slice(0, 768))
EXPAND = (slice(688, 864), slice(0, 672))
ZERO_ROW = 128


def three_lanes(value):
    high = value.astype(BF16)
    low = (value - high.astype(F32)).astype(BF16)
    return jnp.concatenate([high, low, high], axis=1)


def three_rows(value):
    high = value.astype(BF16)
    low = (value - high.astype(F32)).astype(BF16)
    return jnp.concatenate([high, low, high], axis=0)


def swap_blocks(tiles):
    tiles = list(tiles)
    group = lax.broadcasted_iota(jnp.int32, tiles[0].shape, 1) // 16
    for bit in (1, 2, 4):
        upper = (group & bit) != 0
        for i in range(8):
            if i & bit:
                continue
            low, high = tiles[i], tiles[i | bit]
            tiles[i] = jnp.where(upper, pltpu.roll(high, 16 * bit, 1), low)
            tiles[i | bit] = jnp.where(upper, high, pltpu.roll(low, 128 - 16 * bit, 1))
    return tiles


def algebra(mreal, mimag):
    i00, i11, i22 = mimag(0, 0), mimag(1, 1), mimag(2, 2)
    middle = (i00 + i11 + i22) * (1.0 / 3.0)
    return [
        i00 - middle,
        i11 - middle,
        (mreal(0, 1) - mreal(1, 0)) * 0.5,
        (mimag(0, 1) + mimag(1, 0)) * 0.5,
        (mreal(0, 2) - mreal(2, 0)) * 0.5,
        (mimag(0, 2) + mimag(2, 0)) * 0.5,
        (mreal(1, 2) - mreal(2, 1)) * 0.5,
        (mimag(1, 2) + mimag(2, 1)) * 0.5,
    ]


def squares(c):
    third = c[0] + c[1]
    rest = c[2] * c[2] + c[3] * c[3] + c[4] * c[4] + c[5] * c[5] + c[6] * c[6] + c[7] * c[7]
    return c[0] * c[0] + c[1] * c[1] + third * third + 2.0 * rest


def entry(row, col):
    return row * 3 + col


def cross_row(first_re, first_im, second_re, second_im):
    out_re, out_im = [], []
    for k in range(3):
        a, b = (k + 1) % 3, (k + 2) % 3
        out_re.append(
            first_re[a] * second_re[b]
            - first_im[a] * second_im[b]
            - first_re[b] * second_re[a]
            + first_im[b] * second_im[a]
        )
        out_im.append(
            first_re[b] * second_im[a]
            + first_im[b] * second_re[a]
            - first_re[a] * second_im[b]
            - first_im[a] * second_re[b]
        )
    return out_re, out_im


def exponent_rows(c):
    c0, c1, c2, c3, c4, c5, c6, c7 = c
    n01 = c2 * c2 + c3 * c3
    n02 = c4 * c4 + c5 * c5
    n12 = c6 * c6 + c7 * c7
    s00 = 1.0 - 0.5 * (c0 * c0 + n01 + n02)
    s11 = 1.0 - 0.5 * (c1 * c1 + n01 + n12)
    d01 = c0 + c1
    p01r = -(d01 * c3) - (c4 * c6 + c5 * c7)
    p01i = d01 * c2 - (c5 * c6 - c4 * c7)
    p02r = c1 * c5 + (c2 * c6 - c3 * c7)
    p02i = -(c1 * c4) + (c2 * c7 + c3 * c6)
    p12r = -(c2 * c4 + c3 * c5) + c0 * c7
    p12i = -(c2 * c5 - c3 * c4) - c0 * c6
    r0 = [s00, c2 + 0.5 * p01r, c4 + 0.5 * p02r]
    i0 = [c0, c3 + 0.5 * p01i, c5 + 0.5 * p02i]
    r1 = [-c2 + 0.5 * p01r, s11, c6 + 0.5 * p12r]
    i1 = [c3 - 0.5 * p01i, c1, c7 + 0.5 * p12i]
    size = sum(r0[k] * r0[k] + i0[k] * i0[k] for k in range(3))
    scale = 1.0 / jnp.sqrt(size)
    r0 = [v * scale for v in r0]
    i0 = [v * scale for v in i0]
    pr = sum(r0[k] * r1[k] + i0[k] * i1[k] for k in range(3))
    pi = sum(r0[k] * i1[k] - i0[k] * r1[k] for k in range(3))
    r1, i1 = (
        [r1[k] - (pr * r0[k] - pi * i0[k]) for k in range(3)],
        [i1[k] - (pr * i0[k] + pi * r0[k]) for k in range(3)],
    )
    size = sum(r1[k] * r1[k] + i1[k] * i1[k] for k in range(3))
    scale = 1.0 / jnp.sqrt(size)
    r1 = [v * scale for v in r1]
    i1 = [v * scale for v in i1]
    return r0 + r1, i0 + i1


def full_matrix(re6, im6):
    re3, im3 = cross_row(re6[:3], im6[:3], re6[3:], im6[3:])
    return list(re6) + re3 + list(im6) + im3


def times_rows(gre, gim, hre, him):
    out_re, out_im = [], []
    for i in range(2):
        for j in range(3):
            acc_re = acc_im = None
            for k in range(3):
                ar, ai = gre[entry(i, k)], gim[entry(i, k)]
                br, bi = hre[entry(k, j)], him[entry(k, j)]
                pr, pi = ar * br - ai * bi, ar * bi + ai * br
                acc_re = pr if acc_re is None else acc_re + pr
                acc_im = pi if acc_im is None else acc_im + pi
            out_re.append(acc_re)
            out_im.append(acc_im)
    return out_re, out_im


def moved_algebra(g, link, ahead):
    gre, gim = g[:9], g[9:]
    are, aim = ahead[:9], ahead[9:]
    vre, vim = [None] * 9, [None] * 9
    for i in range(3):
        ur = [link(0, i, k) for k in range(3)]
        ui = [link(1, i, k) for k in range(3)]
        for j in range(3):
            br = [are[entry(j, k)] for k in range(3)]
            bi = [aim[entry(j, k)] for k in range(3)]
            vre[entry(i, j)] = (ur[0] * br[0] + ui[0] * bi[0]) + (
                (ur[1] * br[1] + ui[1] * bi[1]) + (ur[2] * br[2] + ui[2] * bi[2])
            )
            vim[entry(i, j)] = (ui[0] * br[0] - ur[0] * bi[0]) + (
                (ui[1] * br[1] - ur[1] * bi[1]) + (ui[2] * br[2] - ur[2] * bi[2])
            )

    def mreal(i, j):
        return sum(
            gre[entry(i, k)] * vre[entry(k, j)] - gim[entry(i, k)] * vim[entry(k, j)]
            for k in range(3)
        )

    def mimag(i, j):
        return sum(
            gre[entry(i, k)] * vim[entry(k, j)] + gim[entry(i, k)] * vre[entry(k, j)]
            for k in range(3)
        )

    return algebra(mreal, mimag)


PLANE = 18 * 32


def dot(left, right):
    return jnp.dot(left, right, preferred_element_type=F32)


def wide(pieces):
    return jnp.concatenate([three_rows(piece) for piece in pieces], axis=1)


def tile(value, c):
    return value[:, 128 * c : 128 * c + 128]


def encode(sources, stride, coarse, fine, modes, packed, out):
    spectrum = dot(three_lanes(sources[...]), coarse[Z_IN])
    parts = [spectrum[stride * c : stride * c + stride] for c in range(8)]
    mode = dot(coarse[MODES], wide([part[:128] for part in parts]))
    scaled = []
    for c in range(8):
        scaled.append(fine[pl.ds(0, 128), :] * tile(mode, c))
        modes[c] = scaled[c]
    both = [jnp.concatenate([parts[c][:128], scaled[c]], axis=0) for c in range(8)]
    reduced = dot(coarse[REDUCE], wide(both))
    for c in range(8):
        values = tile(reduced, c)
        groups = [values[0:16], values[16:32], values[32:48]]
        if stride > 128:
            groups[1] = groups[1] + parts[c][128:144]
            groups[2] = jnp.concatenate([groups[2][:8], groups[2][8:] + parts[c][144:152]], axis=0)
        for t in range(3):
            packed[pl.ds(128 * t + 16 * c, 16), :] = groups[t]
    for t in range(3):
        out[:, pl.ds(128 * t, 128)] = packed[pl.ds(128 * t, 128), :].T


def first_kernel(links, coarse, fine, out, modes, edge_x, edge_y, theta, prev, sources, packed):
    prev[...] = jnp.zeros_like(prev)
    theta[...] = jnp.zeros_like(theta)
    row = lax.broadcasted_iota(jnp.int32, (16, 128), 0)

    def planes(x, carry):
        def of(mu):
            return algebra(
                lambda i, j: links[18 * mu + entry(i, j), x],
                lambda i, j: links[18 * mu + 9 + entry(i, j), x],
            )

        ax, ay, az = of(0), of(1), of(2)
        comps = []
        for c in range(8):
            back_y = jnp.where(row == 0, 0.0, pltpu.roll(ay[c], 1, 0))
            value = (prev[c] + back_y + pltpu.roll(az[c], 1, 1)) - ax[c] - ay[c] - az[c]
            prev[c] = ax[c]
            comps.append(value)
            sources[pl.ds(152 * c + 16 * x, 16), :] = value
            sources[pl.ds(152 * c + 144 + x, 1), :] = ay[c][15:16]
        inner = jnp.where((row > 0) & (x > 0), squares(comps), 0.0)
        theta[...] += inner[:8] + inner[8:]
        return carry

    lax.fori_loop(0, 8, planes, 0)
    for c in range(8):
        sources[pl.ds(152 * c + 128, 16), :] = prev[c]
        edge_x[c] = sources[pl.ds(152 * c, 16), :]
        edge_y[c] = sources[pl.ds(152 * c, 8, stride=16), :]
    encode(sources, 152, coarse, fine, modes, packed, out)


def plane_kernel(own, recv, coarse, fine, out, work, lines, packed):
    lane = lax.broadcasted_iota(jnp.int32, (16, 128), 1) % 16
    zero = jnp.where(own[0] == 0, -1.0 / (LS * LS), 0.0)
    total = fine[pl.ds(ZERO_ROW, 128), :] + fine[pl.ds(ZERO_ROW + own[0], 1), :][:, 0:1]
    inverse = jnp.where(total > 0.0, 1.0 / jnp.where(total > 0.0, total, 1.0), 0.0)
    shifts = []
    for t in range(3):
        packed[pl.ds(128 * t, 128), :] = recv[:, pl.ds(128 * t, 128)]
    moved = [
        swap_blocks([packed[pl.ds(128 * t + g, 16, stride=8), :] for g in range(8)])
        for t in range(3)
    ]
    for c in range(8):
        third = moved[2][c]
        rolled = pltpu.roll(third, 8, 1)
        first = moved[0][c] + pltpu.roll(moved[1][c], 1, 0) + jnp.where(lane == 0, rolled, 0.0)
        work[pl.ds(16 * c, 16), :] = first
        both = third + rolled
        for x in range(1, 8):
            work[pl.ds(128 * x + 16 * c, 16), :] = jnp.where(lane == x, both, 0.0)
        extra = jnp.sum(jnp.where(lane == 0, third, 0.0), axis=0, keepdims=True)
        shifts.append(jnp.sum(extra, axis=1, keepdims=True) * zero)
    lines[pl.ds(0, 128), :] = dot(three_lanes(work[pl.ds(0, 128), :]), coarse[Y_IN])
    lines[pl.ds(128, 896), :] = dot(three_lanes(work[pl.ds(128, 896), :]), coarse[LINES_IN])
    blocks = [
        jnp.concatenate([lines[pl.ds(128 * x + 16 * c, 16), :] for x in range(8)], axis=0)
        for c in range(8)
    ]
    spectrum = dot(coarse[X_IN], wide(blocks))
    spectrum = dot(coarse[X_OUT], wide([tile(spectrum, c) * inverse for c in range(8)]))
    spectrum = [tile(spectrum, c) for c in range(8)]
    at_lines = dot(three_lanes(jnp.concatenate(spectrum, axis=0)), coarse[LINES_OUT])
    first = jnp.concatenate([part[:16] for part in spectrum], axis=0)
    first = dot(three_lanes(first), coarse[Z_OUT])
    groups = [[], [], []]
    for c in range(8):
        own_line = first[16 * c : 16 * c + 16] + shifts[c]
        groups[0].append(own_line)
        groups[1].append(pltpu.roll(own_line, 15, 0))
        parts = [at_lines[128 * c + 16 * x : 128 * c + 16 * x + 16] for x in range(8)]
        third = jnp.where(lane == 0, pltpu.roll(parts[7], 1, 0), parts[0])
        for x in range(1, 8):
            third = jnp.where((lane == x) | (lane == 8 + x), parts[x], third)
        groups[2].append(third + shifts[c])
    for t in range(3):
        tiles = swap_blocks(groups[t])
        for g in range(8):
            packed[pl.ds(128 * t + g, 16, stride=8), :] = tiles[g]
        out[:, pl.ds(128 * t, 128)] = packed[pl.ds(128 * t, 128), :]


def decode(recv, modes, coarse, fine, packed, comps_in):
    for t in range(3):
        packed[pl.ds(128 * t, 128), :] = recv[:, pl.ds(128 * t, 128)].T
    mass = fine[pl.ds(ZERO_ROW, 1), :]
    values = [
        jnp.concatenate([packed[pl.ds(128 * t + 16 * c, 16), :] for t in range(3)], axis=0)
        for c in range(8)
    ]
    mode = dot(coarse[SOURCE], wide(values))
    stacks = []
    for c in range(8):
        own = modes[c] + fine[pl.ds(0, 128), :] * tile(mode, c)
        stacks.append(jnp.concatenate([own, values[c], values[c] * mass], axis=0))
    sites = dot(coarse[EXPAND], wide(stacks))
    sites = jnp.concatenate([tile(sites, c) for c in range(8)], axis=0)
    comps_in[...] = dot(three_lanes(sites), coarse[Z_OUT])


def update_body(last, refs):
    recv, modes, edge_x, edge_y, links, face_x, face_y, theta_in, coarse, fine = refs[:10]
    refs = refs[10:]
    if last:
        prior, prior_y, theta_first, div, gauge, theta = refs[:6]
        packed, comps_in, gs, edge_g, ay, prev, acc = refs[6:]
    else:
        out, modes_out, edge_x_out, edge_y_out, theta, gout, gout_y, theta_out = refs[:8]
        packed, comps_in, gs, edge_g, ay, prev, acc, sources = refs[8:]
    decode(recv, modes, coarse, fine, packed, comps_in)

    add_x = add_y = None
    if not last:
        add_x = algebra(lambda i, j: face_x[entry(i, j)], lambda i, j: face_x[9 + entry(i, j)])
        add_y = algebra(lambda i, j: face_y[entry(i, j)], lambda i, j: face_y[9 + entry(i, j)])
    whole_x, whole_y = [], []
    row = lax.broadcasted_iota(jnp.int32, (16, 128), 0)
    for c in range(8):
        line_x, line_y = edge_x[c], edge_y[c]
        if not last:
            top = row == 0
            line_x = line_x + add_x[c] + jnp.where(top, add_y[c][0:1], 0.0)
            line_y = line_y + add_y[c] + jnp.where(top[:8], add_x[c][0:1], 0.0)
        whole_x.append(line_x)
        whole_y.append(line_y)
        behind = pl.ds(176 * c + 144, 16)
        comps_in[behind, :] = comps_in[behind, :] - jnp.where(row == 0, 0.0, SCALE * line_x)
        below = pl.ds(176 * c + 168, 8)
        comps_in[below, :] = comps_in[below, :] - SCALE * line_y
    if not last:
        sq = squares(whole_x)
        theta_out[...] = (
            theta_in[...] + sq[:8] + sq[8:] + jnp.where(row[:8] == 0, 0.0, squares(whole_y))
        )

    def make(c, before):
        re6, im6 = exponent_rows(c)
        if before is not None:
            re6, im6 = times_rows(re6, im6, before[:9], before[9:])
        return full_matrix(re6, im6)

    def plane(index, first_row, inside):
        for half in range(2):
            rows = pl.ds(8 * half, 8)
            before = [prior[index, k, rows, :] for k in range(18)] if last else None
            g = make([comps_in[pl.ds(first_row(c) + 8 * half, 8), :] for c in range(8)], before)
            for k in range(18):
                gs[pl.ds(index * PLANE + 32 * k + 8 * half + 8, 8), :] = g[k]
                if not last:
                    gout[index, k, rows, :] = g[k]
            if last and inside:
                for p in range(2):
                    for i in range(2):
                        for j in range(3):
                            gauge[p, i, j, index - 1, rows, :] = g[9 * p + entry(i, j)]

    def inner(x, carry):
        plane(x + 1, lambda c: 176 * c + 16 * x, True)
        return carry

    lax.fori_loop(0, 8, inner, 0)
    plane(0, lambda c: 176 * c + 144, False)
    plane(9, lambda c: 176 * c + 128, False)
    for side in range(2):
        c = [comps_in[pl.ds(176 * k + 168 - 8 * side, 8), :] for k in range(8)]
        before = [prior_y[side, k] for k in range(18)] if last else None
        g = make(c, before)
        for k in range(18):
            if not last:
                gout_y[side, k] = g[k]
            if side == 0:
                edge_g[k] = g[k]
            else:
                gs[pl.ds(PLANE + 32 * k + 24, 8, stride=PLANE), :] = g[k]

    g = [edge_g[k] for k in range(18)]
    ahead = [gs[pl.ds(PLANE + 32 * k + 8, 8, stride=PLANE), :] for k in range(18)]
    edge = moved_algebra(g, lambda p, i, j: face_y[9 * p + entry(i, j)], ahead)
    for c in range(8):
        ay[pl.ds(24 * c + 7, 8, stride=192), :] = edge[c]
    for half in range(2):
        rows = pl.ds(8 * half, 8)
        start = 8 * half + 8
        g = [gs[pl.ds(32 * k + start, 8), :] for k in range(18)]
        ahead = [gs[pl.ds(PLANE + 32 * k + start, 8), :] for k in range(18)]
        edge = moved_algebra(g, lambda p, i, j: face_x[9 * p + entry(i, j), rows, :], ahead)
        for c in range(8):
            prev[c, rows, :] = edge[c]

    acc[...] = jnp.zeros_like(acc)

    def sites(x, carry):
        base = (x + 1) * PLANE
        for half in range(2):
            rows = pl.ds(8 * half, 8)
            start = 8 * half + 8
            total = [None] * 8

            def link_of(mu):
                return lambda p, i, j: links[18 * mu + 9 * p + entry(i, j), x, rows, :]

            g = [gs[pl.ds(base + 32 * k + start, 8), :] for k in range(18)]
            ahead = [gs[pl.ds(base + PLANE + 32 * k + start, 8), :] for k in range(18)]
            a = moved_algebra(g, link_of(0), ahead)
            for c in range(8):
                total[c] = prev[c, rows, :] - a[c]
                prev[c, rows, :] = a[c]
            ahead = [gs[pl.ds(base + 32 * k + start + 1, 8), :] for k in range(18)]
            a = moved_algebra(g, link_of(1), ahead)
            for c in range(8):
                ay[pl.ds(x * 192 + 24 * c + start, 8), :] = a[c]
            for c in range(8):
                total[c] = total[c] + (ay[pl.ds(x * 192 + 24 * c + start - 1, 8), :] - a[c])
            ahead = [pltpu.roll(v, 127, 1) for v in g]
            a = moved_algebra(g, link_of(2), ahead)
            for c in range(8):
                total[c] = total[c] + (pltpu.roll(a[c], 1, 1) - a[c])
                if last:
                    div[c, x, rows, :] = total[c]
                else:
                    sources[pl.ds(128 * c + 16 * x + 8 * half, 8), :] = total[c]
            acc[...] += squares(total)
        return carry

    lax.fori_loop(0, 8, sites, 0)
    if last:
        lane = lax.broadcasted_iota(jnp.int32, (1, 128), 1)
        sums = jnp.zeros((1, 128), F32)
        for k, part in enumerate((theta_first, theta_in, acc)):
            sums = sums + jnp.where(lane == k, jnp.sum(part[...]), 0.0)
        theta[...] = jnp.broadcast_to(sums, (128, 128))
    else:
        theta[...] = acc[...]
        for c in range(8):
            edge_x_out[c] = sources[pl.ds(128 * c, 16), :]
            edge_y_out[c] = sources[pl.ds(128 * c, 8, stride=16), :]
        encode(sources, 128, coarse, fine, modes_out, packed, out)


def update_kernel(*refs):
    update_body(False, refs)


def last_kernel(*refs):
    update_body(True, refs)


def struct(*shape):
    return jax.ShapeDtypeStruct(shape, F32)


def vmem(*shape):
    return pltpu.VMEM(shape, F32)


def whole():
    return pl.BlockSpec(memory_space=pltpu.VMEM)


def params(size):
    return pltpu.CompilerParams(vmem_limit_bytes=size * MEGA)


EDGES = [(8, 16, 128), (8, 8, 128)]


def first_call(links, tables):
    shapes = [struct(128, 384), struct(8, 128, 128)] + [struct(*e) for e in EDGES] + [struct(8, 128)]
    return pl.pallas_call(
        first_kernel,
        in_specs=[whole()] * 3,
        out_specs=[whole()] * len(shapes),
        out_shape=shapes,
        scratch_shapes=[vmem(8, 16, 128), vmem(8 * 152, 128), vmem(384, 128)],
        compiler_params=params(32),
        name="first_divergence",
    )(links, *tables)


def plane_call(own, recv, tables):
    return pl.pallas_call(
        plane_kernel,
        in_specs=[pl.BlockSpec(memory_space=pltpu.SMEM)] + [whole()] * 3,
        out_specs=whole(),
        out_shape=struct(128, 384),
        scratch_shapes=[vmem(1024, 128), vmem(1024, 128), vmem(384, 128)],
        compiler_params=params(32),
        name="plane_solve",
    )(own, recv, *tables)


def update_call(recv, state, links, face_x, face_y, tables, prior):
    last = prior is not None
    modes, edge_x, edge_y, theta = state
    operands = [recv, modes, edge_x, edge_y, links, face_x, face_y, theta] + list(tables)
    scratch = [
        vmem(384, 128),
        vmem(8 * 176, 128),
        vmem(10 * PLANE, 128),
        vmem(18, 8, 128),
        vmem(8 * 192, 128),
        vmem(8, 16, 128),
        vmem(8, 128),
    ]
    if last:
        shapes = [struct(8, 8, 16, 128), struct(2, 2, 3, 8, 16, 128), struct(128, 128)]
        operands += list(prior)
    else:
        shapes = [struct(128, 384), struct(8, 128, 128)] + [struct(*e) for e in EDGES]
        shapes += [struct(8, 128), struct(10, 18, 16, 128), struct(2, 18, 8, 128), struct(8, 128)]
        scratch += [vmem(8 * 128, 128)]
    return pl.pallas_call(
        last_kernel if last else update_kernel,
        in_specs=[whole()] * len(operands),
        out_specs=[whole()] * len(shapes),
        out_shape=shapes,
        scratch_shapes=scratch,
        compiler_params=params(32),
        name="last_update" if last else "update",
    )(*operands)


def shifted(value, axis, steps):
    count = lax.axis_size(axis)
    pairs = [(source, (source + steps) % count) for source in range(count)]
    return lax.ppermute(value, axis, pairs)


def exchange(value):
    return lax.all_to_all(value, ("gx", "gy"), split_axis=0, concat_axis=0, tiled=True)


def per_device(links):
    face_x = shifted(links[0, :, :, :, 7].reshape(18, 16, 128), "gx", 1)
    face_y = shifted(links[1, :, :, :, :, 15].reshape(18, 8, 128), "gy", 1)
    flat = links.reshape(54, 8, 16, 128)
    own = (lax.axis_index("gx") * 8 + lax.axis_index("gy")).astype(jnp.int32).reshape(1)
    tables = (jnp.asarray(COARSE), jnp.asarray(FINE))
    packed, *state = first_call(flat, tables)
    packed, face_x, face_y, own = lax.optimization_barrier((packed, face_x, face_y, own))
    prior = None
    for step in range(2):
        values = exchange(plane_call(own, exchange(packed), tables))
        results = update_call(values, state, flat, face_x, face_y, tables, prior)
        if step == 0:
            packed, modes, edge_x, edge_y, theta, gout, gout_y, theta_first = results
            state = (modes, edge_x, edge_y, theta)
            prior = (gout, gout_y, theta_first)
    div, gauge, sums = results
    sums = jnp.sum(exchange(sums), axis=0)[:3] / (3.0 * LS * LS * NZ)
    return (gauge, div, sums)


def solution(mesh):
    in_specs = (P(None, None, None, None, "gx", "gy", "ta"),)
    out_specs = (P(None, None, None, "gx", "gy", "ta"), P(None, "gx", "gy", "ta"), P("ta"))
    return jax.shard_map(
        per_device, mesh=mesh, in_specs=in_specs, out_specs=out_specs, check_vma=False
    )
```

```python
import math

import jax
import jax.numpy as jnp
import numpy as np
from jax import lax
from jax.experimental import pallas as pl
from jax.experimental.pallas import tpu as pltpu
from jax.sharding import PartitionSpec as P

LS = 128
NZ = 128
STEP_SIZE = 0.08
PEAK_MOMENTUM = 12.0
F32 = jnp.float32
BF16 = jnp.bfloat16
MEGA = 1024 * 1024


def real_basis(length):
    site = np.arange(length)[:, None]
    freq = np.arange(length)
    freq = np.where(freq <= length // 2, freq, freq - length // 2)
    phase = 2.0 * np.pi * ((site * freq[None, :]) % length) / length
    index = np.arange(length)[None, :]
    basis = np.where(index <= length // 2, np.cos(phase), np.sin(phase)) * np.sqrt(2.0 / length)
    basis[:, 0] = 1.0 / np.sqrt(length)
    basis[:, length // 2] = np.cos(np.pi * np.arange(length)) / np.sqrt(length)
    return basis, freq


def halves(table):
    high = table.astype(np.float32).astype(jnp.bfloat16)
    low = (table - high.astype(np.float64)).astype(np.float32).astype(jnp.bfloat16)
    return high, low


def right_table(table):
    high, low = halves(table)
    return np.concatenate([high, high, low], axis=0)


def left_table(table):
    high, low = halves(table)
    return np.concatenate([high, high, low], axis=1)


def sine_table():
    x, y = np.arange(8), np.arange(16)
    sx = np.sin(np.pi * np.outer(x, x) / 8.0) * np.sqrt(2.0 / 8.0)
    sy = np.sin(np.pi * np.outer(y, y) / 16.0) * np.sqrt(2.0 / 16.0)
    table = np.kron(sx, sy)
    keep = np.kron(x > 0, y > 0)
    table = table * np.outer(keep, keep)
    eigen = (4.0 * np.sin(np.pi * x / 16.0) ** 2)[:, None] + (4.0 * np.sin(np.pi * y / 32.0) ** 2)[None, :]
    return table, eigen.reshape(128), keep


BASIS, FREQ = real_basis(128)
SQUARES = 4.0 * np.sin(np.pi * FREQ / 128.0) ** 2
SINE, EIGEN, INNER = sine_table()


def node(x, y):
    return 16 * x + y


def reduce_table():
    out = np.zeros((48, 256))
    for y in range(16):
        out[y, node(0, y)] = 1.0
        if y > 0:
            out[y, 128:] = SINE[node(1, y)]
            out[16 + y, 128:] = SINE[node(7, y)]
    out[32, 128:] = SINE[INNER].sum(0)
    for x in range(1, 8):
        out[32 + x, node(x, 0)] = 1.0
        out[32 + x, 128:] = SINE[node(x, 1)]
        out[40 + x, 128:] = SINE[node(x, 15)]
    return out


def source_table():
    out = np.zeros((128, 48))
    for y in range(1, 16):
        out[:, y] = SINE[node(1, y)]
        out[:, 16 + y] = SINE[node(7, y)]
    for x in range(1, 8):
        out[:, 32 + x] = SINE[node(x, 1)]
        out[:, 40 + x] = SINE[node(x, 15)]
    return out


def expand_table():
    out = np.zeros((176, 224))
    val, mass = 128, 176

    def line_x(x):
        return 0 if x == 0 else (16 if x == 8 else 32 + x)

    def line_y(y):
        return 40 if y == 16 else y

    for x in range(1, 8):
        for y in range(1, 16):
            out[node(x, y), :128] = SINE[node(x, y)]
    for y in range(16):
        out[node(0, y), val + y] = 1.0
        out[128 + y, val + 16 + y] = 1.0
    for x in range(1, 8):
        out[node(x, 0), val + 32 + x] = 1.0
    for x in range(8):
        out[160 + x, val + 40 + x] = 1.0
    out[144, val + 32] = 1.0
    for y in range(1, 16):
        row = out[144 + y]
        row[val + y] += 4.0
        row[mass + y] += 1.0
        row[:128] -= SINE[node(1, y)]
        row[val + line_y(y - 1)] -= 1.0
        row[val + line_y(y + 1)] -= 1.0
    for x in range(1, 8):
        row = out[168 + x]
        row[val + line_x(x)] += 4.0
        row[mass + line_x(x)] += 1.0
        row[:128] -= SINE[node(x, 1)]
        row[val + line_x(x - 1)] -= 1.0
        row[val + line_x(x + 1)] -= 1.0
    row = out[168]
    row[val] += 4.0
    row[mass] += 1.0
    row[val + 33] -= 1.0
    row[val + 32] -= 1.0
    row[val + 1] -= 1.0
    return out


def lines_in():
    out = np.zeros((128, 128))
    for g in range(8):
        out[16 * g : 16 * g + 16] = BASIS[16 * g]
    return out


def lines_out():
    out = np.zeros((128, 128))
    for g in range(8):
        out[:, 16 * g : 16 * g + 8] = BASIS[16 * g][:, None]
        out[:, 16 * g + 8 : 16 * g + 16] = BASIS[(16 * g + 16) % 128][:, None]
    return out


SCALE = STEP_SIZE * PEAK_MOMENTUM
ORDER = np.array([8 * j + x for x in range(8) for j in range(16)])


def pack_tables():
    out = np.zeros((992, 768), jnp.bfloat16)
    rights = (BASIS * SCALE, BASIS.T, BASIS, lines_in(), lines_out())
    for k, table in enumerate(rights):
        out[:384, 128 * k : 128 * k + 128] = right_table(table)
    out[384:512, :384] = left_table(SINE)
    out[384:512, 384:] = left_table(BASIS[ORDER].T)
    out[512:640, :384] = left_table(BASIS[ORDER])
    out[512:640, 384:528] = left_table(source_table())
    out[640:688, :] = left_table(reduce_table())
    out[688:864, :672] = left_table(expand_table())
    for k, table in enumerate((INVERSE, PLANE_SUM)):
        rest = table.astype(np.float32).astype(np.float64)
        for part in range(3):
            piece = rest.astype(np.float32).astype(jnp.bfloat16)
            lanes = 384 * k + 128 * part
            out[864:992, lanes : lanes + 128] = piece
            rest = rest - piece.astype(np.float64)
    return out


INVERSE = INNER[:, None] / (np.where(INNER, EIGEN, 1.0)[:, None] + SQUARES[None, :])
PLANE_SUM = SQUARES[:, None] + SQUARES[None, :]
TABLE = pack_tables()
Z_IN, Z_OUT, Y_IN, LINES_IN, LINES_OUT = [(slice(0, 384), slice(128 * k, 128 * k + 128)) for k in range(5)]
MODES = (slice(384, 512), slice(0, 384))
X_IN = (slice(384, 512), slice(384, 768))
X_OUT = (slice(512, 640), slice(0, 384))
SOURCE = (slice(512, 640), slice(384, 528))
REDUCE = (slice(640, 688), slice(0, 768))
EXPAND = (slice(688, 864), slice(0, 672))


def float_table(table, which, rows=128):
    parts = [
        table[864 : 864 + rows, 384 * which + 128 * k : 384 * which + 128 * k + 128].astype(F32)
        for k in range(3)
    ]
    return (parts[0] + parts[1]) + parts[2]


def three_lanes(value):
    high = value.astype(BF16)
    low = (value - high.astype(F32)).astype(BF16)
    return jnp.concatenate([high, low, high], axis=1)


def three_rows(value):
    high = value.astype(BF16)
    low = (value - high.astype(F32)).astype(BF16)
    return jnp.concatenate([high, low, high], axis=0)


def swap_blocks(tiles):
    tiles = list(tiles)
    group = lax.broadcasted_iota(jnp.int32, tiles[0].shape, 1) // 16
    for bit in (1, 2, 4):
        upper = (group & bit) != 0
        for i in range(8):
            if i & bit:
                continue
            low, high = tiles[i], tiles[i | bit]
            tiles[i] = jnp.where(upper, pltpu.roll(high, 16 * bit, 1), low)
            tiles[i | bit] = jnp.where(upper, high, pltpu.roll(low, 128 - 16 * bit, 1))
    return tiles


def algebra(mreal, mimag):
    i00, i11, i22 = mimag(0, 0), mimag(1, 1), mimag(2, 2)
    middle = (i00 + i11 + i22) * (1.0 / 3.0)
    return [
        i00 - middle,
        i11 - middle,
        (mreal(0, 1) - mreal(1, 0)) * 0.5,
        (mimag(0, 1) + mimag(1, 0)) * 0.5,
        (mreal(0, 2) - mreal(2, 0)) * 0.5,
        (mimag(0, 2) + mimag(2, 0)) * 0.5,
        (mreal(1, 2) - mreal(2, 1)) * 0.5,
        (mimag(1, 2) + mimag(2, 1)) * 0.5,
    ]


def squares(c):
    third = c[0] + c[1]
    rest = c[2] * c[2] + c[3] * c[3] + c[4] * c[4] + c[5] * c[5] + c[6] * c[6] + c[7] * c[7]
    return c[0] * c[0] + c[1] * c[1] + third * third + 2.0 * rest


def entry(row, col):
    return row * 3 + col


def cross_row(first_re, first_im, second_re, second_im):
    out_re, out_im = [], []
    for k in range(3):
        a, b = (k + 1) % 3, (k + 2) % 3
        out_re.append(
            first_re[a] * second_re[b]
            - first_im[a] * second_im[b]
            - first_re[b] * second_re[a]
            + first_im[b] * second_im[a]
        )
        out_im.append(
            first_re[b] * second_im[a]
            + first_im[b] * second_re[a]
            - first_re[a] * second_im[b]
            - first_im[a] * second_re[b]
        )
    return out_re, out_im


def exponent_rows(c):
    c0, c1, c2, c3, c4, c5, c6, c7 = c
    n01 = c2 * c2 + c3 * c3
    n02 = c4 * c4 + c5 * c5
    n12 = c6 * c6 + c7 * c7
    s00 = 1.0 - 0.5 * (c0 * c0 + n01 + n02)
    s11 = 1.0 - 0.5 * (c1 * c1 + n01 + n12)
    d01 = c0 + c1
    p01r = -(d01 * c3) - (c4 * c6 + c5 * c7)
    p01i = d01 * c2 - (c5 * c6 - c4 * c7)
    p02r = c1 * c5 + (c2 * c6 - c3 * c7)
    p02i = -(c1 * c4) + (c2 * c7 + c3 * c6)
    p12r = -(c2 * c4 + c3 * c5) + c0 * c7
    p12i = -(c2 * c5 - c3 * c4) - c0 * c6
    r0 = [s00, c2 + 0.5 * p01r, c4 + 0.5 * p02r]
    i0 = [c0, c3 + 0.5 * p01i, c5 + 0.5 * p02i]
    r1 = [-c2 + 0.5 * p01r, s11, c6 + 0.5 * p12r]
    i1 = [c3 - 0.5 * p01i, c1, c7 + 0.5 * p12i]
    size = sum(r0[k] * r0[k] + i0[k] * i0[k] for k in range(3))
    scale = lax.rsqrt(size)
    r0 = [v * scale for v in r0]
    i0 = [v * scale for v in i0]
    pr = sum(r0[k] * r1[k] + i0[k] * i1[k] for k in range(3))
    pi = sum(r0[k] * i1[k] - i0[k] * r1[k] for k in range(3))
    r1, i1 = (
        [r1[k] - (pr * r0[k] - pi * i0[k]) for k in range(3)],
        [i1[k] - (pr * i0[k] + pi * r0[k]) for k in range(3)],
    )
    size = sum(r1[k] * r1[k] + i1[k] * i1[k] for k in range(3))
    scale = lax.rsqrt(size)
    r1 = [v * scale for v in r1]
    i1 = [v * scale for v in i1]
    return r0 + r1, i0 + i1


def full_matrix(re6, im6):
    re3, im3 = cross_row(re6[:3], im6[:3], re6[3:], im6[3:])
    return list(re6) + re3 + list(im6) + im3


def times_rows(gre, gim, hre, him):
    out_re, out_im = [], []
    for i in range(2):
        for j in range(3):
            acc_re = acc_im = None
            for k in range(3):
                ar, ai = gre[entry(i, k)], gim[entry(i, k)]
                br, bi = hre[entry(k, j)], him[entry(k, j)]
                pr, pi = ar * br - ai * bi, ar * bi + ai * br
                acc_re = pr if acc_re is None else acc_re + pr
                acc_im = pi if acc_im is None else acc_im + pi
            out_re.append(acc_re)
            out_im.append(acc_im)
    return out_re, out_im


def moved_algebra(g, link, ahead):
    gre, gim = g[:9], g[9:]
    are, aim = ahead[:9], ahead[9:]
    vre, vim = [None] * 9, [None] * 9
    for i in range(2):
        ur = [link(0, i, k) for k in range(3)]
        ui = [link(1, i, k) for k in range(3)]
        for j in range(3):
            br = [are[entry(j, k)] for k in range(3)]
            bi = [aim[entry(j, k)] for k in range(3)]
            vre[entry(i, j)] = (ur[0] * br[0] + ui[0] * bi[0]) + (
                (ur[1] * br[1] + ui[1] * bi[1]) + (ur[2] * br[2] + ui[2] * bi[2])
            )
            vim[entry(i, j)] = (ui[0] * br[0] - ur[0] * bi[0]) + (
                (ui[1] * br[1] - ur[1] * bi[1]) + (ui[2] * br[2] - ur[2] * bi[2])
            )

    vre[6:], vim[6:] = cross_row(vre[:3], vim[:3], vre[3:6], vim[3:6])

    def mreal(i, j):
        return sum(
            gre[entry(i, k)] * vre[entry(k, j)] - gim[entry(i, k)] * vim[entry(k, j)]
            for k in range(3)
        )

    def mimag(i, j):
        return sum(
            gre[entry(i, k)] * vim[entry(k, j)] + gim[entry(i, k)] * vre[entry(k, j)]
            for k in range(3)
        )

    return algebra(mreal, mimag)


PLANE = 18 * 32


def dot(left, right):
    return jnp.dot(left, right, preferred_element_type=F32)


def wide(pieces):
    return jnp.concatenate([three_rows(piece) for piece in pieces], axis=1)


def tile(value, c):
    return value[:, 128 * c : 128 * c + 128]


def encode(sources, stride, table, modes, packed, out):
    spectrum = dot(three_lanes(sources[...]), table[Z_IN])
    parts = [spectrum[stride * c : stride * c + stride] for c in range(8)]
    mode = dot(table[MODES], wide([part[:128] for part in parts]))
    inverse = float_table(table, 0)
    scaled = []
    for c in range(8):
        scaled.append(inverse * tile(mode, c))
        modes[c] = scaled[c]
    both = [jnp.concatenate([parts[c][:128], scaled[c]], axis=0) for c in range(8)]
    reduced = dot(table[REDUCE], wide(both))
    for c in range(8):
        values = tile(reduced, c)
        groups = [values[0:16], values[16:32], values[32:48]]
        if stride > 128:
            groups[1] = groups[1] + parts[c][128:144]
            groups[2] = jnp.concatenate([groups[2][:8], groups[2][8:] + parts[c][144:152]], axis=0)
        for t in range(3):
            packed[pl.ds(128 * t + 16 * c, 16), :] = groups[t]
    for t in range(3):
        out[:, pl.ds(128 * t, 128)] = packed[pl.ds(128 * t, 128), :].T


def first_kernel(*refs):
    links_hbm, table_hbm, out, modes, edge_x, edge_y, theta, table, face_x, face_y = refs[:10]
    links, prev, sources, packed, sems = refs[10:]

    def plane_copy(x):
        return pltpu.make_async_copy(links_hbm.at[:, x], links.at[x], sems.at[x])

    for x in range(8):
        plane_copy(x).start()
    table_copy = pltpu.make_async_copy(table_hbm, table, sems.at[8])
    table_copy.start()
    prev[...] = jnp.zeros_like(prev)
    theta[...] = jnp.zeros_like(theta)
    row = lax.broadcasted_iota(jnp.int32, (16, 128), 0)

    def planes(x, carry):
        plane_copy(x).wait()

        def of(mu):
            return algebra(
                lambda i, j: links[x, 18 * mu + entry(i, j)],
                lambda i, j: links[x, 18 * mu + 9 + entry(i, j)],
            )

        ax, ay, az = of(0), of(1), of(2)
        comps = []
        for c in range(8):
            back_y = jnp.where(row == 0, 0.0, pltpu.roll(ay[c], 1, 0))
            value = (prev[c] + back_y + pltpu.roll(az[c], 1, 1)) - ax[c] - ay[c] - az[c]
            prev[c] = ax[c]
            comps.append(value)
            sources[pl.ds(152 * c + 16 * x, 16), :] = value
            sources[pl.ds(152 * c + 144 + x, 1), :] = ay[c][15:16]
        for k in range(12):
            face_y[k, pl.ds(x, 1), :] = links[x, 18 + k % 6 + 9 * (k // 6), 15:16, :]
        inner = jnp.where((row > 0) & (x > 0), squares(comps), 0.0)
        theta[...] += inner[:8] + inner[8:]
        return carry

    lax.fori_loop(0, 8, planes, 0)
    for c in range(8):
        sources[pl.ds(152 * c + 128, 16), :] = prev[c]
        edge_x[c] = sources[pl.ds(152 * c, 16), :]
        edge_y[c] = sources[pl.ds(152 * c, 8, stride=16), :]
    for k in range(12):
        face_x[k] = links[7, k % 6 + 9 * (k // 6)]
    table_copy.wait()
    encode(sources, 152, table, modes, packed, out)


def plane_kernel(own, recv, table, out, work, lines, packed):
    lane = lax.broadcasted_iota(jnp.int32, (16, 128), 1) % 16
    zero = jnp.where(own[0] == 0, -1.0 / (LS * LS), 0.0)
    total = float_table(table, 1)
    work[pl.ds(0, 128), :] = total
    total = total + work[pl.ds(own[0], 1), :][:, 0:1]
    inverse = jnp.where(total > 0.0, 1.0 / jnp.where(total > 0.0, total, 1.0), 0.0)
    shifts = []
    for t in range(3):
        packed[pl.ds(128 * t, 128), :] = recv[:, pl.ds(128 * t, 128)]
    moved = [
        swap_blocks([packed[pl.ds(128 * t + g, 16, stride=8), :] for g in range(8)])
        for t in range(3)
    ]
    for c in range(8):
        third = moved[2][c]
        rolled = pltpu.roll(third, 8, 1)
        first = moved[0][c] + pltpu.roll(moved[1][c], 1, 0) + jnp.where(lane == 0, rolled, 0.0)
        work[pl.ds(16 * c, 16), :] = first
        both = third + rolled
        for x in range(1, 8):
            work[pl.ds(128 * x + 16 * c, 16), :] = jnp.where(lane == x, both, 0.0)
        extra = jnp.sum(jnp.where(lane == 0, third, 0.0), axis=0, keepdims=True)
        shifts.append(jnp.sum(extra, axis=1, keepdims=True) * zero)
    lines[pl.ds(0, 128), :] = dot(three_lanes(work[pl.ds(0, 128), :]), table[Y_IN])
    lines[pl.ds(128, 896), :] = dot(three_lanes(work[pl.ds(128, 896), :]), table[LINES_IN])
    blocks = [
        jnp.concatenate([lines[pl.ds(128 * x + 16 * c, 16), :] for x in range(8)], axis=0)
        for c in range(8)
    ]
    spectrum = dot(table[X_IN], wide(blocks))
    spectrum = dot(table[X_OUT], wide([tile(spectrum, c) * inverse for c in range(8)]))
    spectrum = [tile(spectrum, c) for c in range(8)]
    at_lines = dot(three_lanes(jnp.concatenate(spectrum, axis=0)), table[LINES_OUT])
    first = jnp.concatenate([part[:16] for part in spectrum], axis=0)
    first = dot(three_lanes(first), table[Z_OUT])
    groups = [[], [], []]
    for c in range(8):
        own_line = first[16 * c : 16 * c + 16] + shifts[c]
        groups[0].append(own_line)
        groups[1].append(pltpu.roll(own_line, 15, 0))
        parts = [at_lines[128 * c + 16 * x : 128 * c + 16 * x + 16] for x in range(8)]
        third = jnp.where(lane == 0, pltpu.roll(parts[7], 1, 0), parts[0])
        for x in range(1, 8):
            third = jnp.where((lane == x) | (lane == 8 + x), parts[x], third)
        groups[2].append(third + shifts[c])
    for t in range(3):
        tiles = swap_blocks(groups[t])
        for g in range(8):
            packed[pl.ds(128 * t + g, 16, stride=8), :] = tiles[g]
        out[:, pl.ds(128 * t, 128)] = packed[pl.ds(128 * t, 128), :]


def decode(recv, modes, table, packed, comps_in):
    for t in range(3):
        packed[pl.ds(128 * t, 128), :] = recv[:, pl.ds(128 * t, 128)].T
    mass = float_table(table, 1, 16)[0:1]
    inverse = float_table(table, 0)
    values = [
        jnp.concatenate([packed[pl.ds(128 * t + 16 * c, 16), :] for t in range(3)], axis=0)
        for c in range(8)
    ]
    mode = dot(table[SOURCE], wide(values))
    stacks = []
    for c in range(8):
        own = modes[c] + inverse * tile(mode, c)
        stacks.append(jnp.concatenate([own, values[c], values[c] * mass], axis=0))
    sites = dot(table[EXPAND], wide(stacks))
    sites = jnp.concatenate([tile(sites, c) for c in range(8)], axis=0)
    comps_in[...] = dot(three_lanes(sites), table[Z_OUT])


def update_body(last, refs):
    recv, modes, edge_x, edge_y, links_hbm, face_x, face_y, theta_in, table = refs[:9]
    refs = refs[9:]
    if last:
        prior, prior_y, theta_first, div, gauge, theta = refs[:6]
        links, sem, packed, comps_in, gs, edge_g, ay, prev, acc = refs[6:]
    else:
        out, modes_out, edge_x_out, edge_y_out, theta, gout, gout_y, theta_out = refs[:8]
        links, sem, packed, comps_in, gs, edge_g, ay, prev, acc, sources = refs[8:]
    copy = pltpu.make_async_copy(links_hbm, links, sem)
    copy.start()
    decode(recv, modes, table, packed, comps_in)

    add_x = add_y = None
    if not last:
        whole_face = full_matrix([face_x[k] for k in range(6)], [face_x[6 + k] for k in range(6)])
        add_x = algebra(lambda i, j: whole_face[entry(i, j)], lambda i, j: whole_face[9 + entry(i, j)])
        whole_face = full_matrix([face_y[k] for k in range(6)], [face_y[6 + k] for k in range(6)])
        add_y = algebra(lambda i, j: whole_face[entry(i, j)], lambda i, j: whole_face[9 + entry(i, j)])
    whole_x, whole_y = [], []
    row = lax.broadcasted_iota(jnp.int32, (16, 128), 0)
    for c in range(8):
        line_x, line_y = edge_x[c], edge_y[c]
        if not last:
            top = row == 0
            line_x = line_x + add_x[c] + jnp.where(top, add_y[c][0:1], 0.0)
            line_y = line_y + add_y[c] + jnp.where(top[:8], add_x[c][0:1], 0.0)
        whole_x.append(line_x)
        whole_y.append(line_y)
        behind = pl.ds(176 * c + 144, 16)
        comps_in[behind, :] = comps_in[behind, :] - jnp.where(row == 0, 0.0, SCALE * line_x)
        below = pl.ds(176 * c + 168, 8)
        comps_in[below, :] = comps_in[below, :] - SCALE * line_y
    if not last:
        sq = squares(whole_x)
        theta_out[...] = (
            theta_in[...] + sq[:8] + sq[8:] + jnp.where(row[:8] == 0, 0.0, squares(whole_y))
        )

    def make(c, before):
        re6, im6 = exponent_rows(c)
        if before is not None:
            re6, im6 = times_rows(re6, im6, before[:9], before[9:])
        return full_matrix(re6, im6)

    def plane(index, first_row, inside):
        for half in range(2):
            rows = pl.ds(8 * half, 8)
            before = [prior[index, k, rows, :] for k in range(18)] if last else None
            g = make([comps_in[pl.ds(first_row(c) + 8 * half, 8), :] for c in range(8)], before)
            for k in range(18):
                gs[pl.ds(index * PLANE + 32 * k + 8 * half + 8, 8), :] = g[k]
                if not last:
                    gout[index, k, rows, :] = g[k]
            if last and inside:
                for p in range(2):
                    for i in range(2):
                        for j in range(3):
                            gauge[p, i, j, index - 1, rows, :] = g[9 * p + entry(i, j)]

    def inner(x, carry):
        plane(x + 1, lambda c: 176 * c + 16 * x, True)
        return carry

    lax.fori_loop(0, 8, inner, 0)
    plane(0, lambda c: 176 * c + 144, False)
    plane(9, lambda c: 176 * c + 128, False)
    for side in range(2):
        c = [comps_in[pl.ds(176 * k + 168 - 8 * side, 8), :] for k in range(8)]
        before = [prior_y[side, k] for k in range(18)] if last else None
        g = make(c, before)
        for k in range(18):
            if not last:
                gout_y[side, k] = g[k]
            if side == 0:
                edge_g[k] = g[k]
            else:
                gs[pl.ds(PLANE + 32 * k + 24, 8, stride=PLANE), :] = g[k]

    g = [edge_g[k] for k in range(18)]
    ahead = [gs[pl.ds(PLANE + 32 * k + 8, 8, stride=PLANE), :] for k in range(18)]
    edge = moved_algebra(g, lambda p, i, j: face_y[6 * p + entry(i, j)], ahead)
    for c in range(8):
        ay[pl.ds(24 * c + 7, 8, stride=192), :] = edge[c]
    for half in range(2):
        rows = pl.ds(8 * half, 8)
        start = 8 * half + 8
        g = [gs[pl.ds(32 * k + start, 8), :] for k in range(18)]
        ahead = [gs[pl.ds(PLANE + 32 * k + start, 8), :] for k in range(18)]
        edge = moved_algebra(g, lambda p, i, j: face_x[6 * p + entry(i, j), rows, :], ahead)
        for c in range(8):
            prev[c, rows, :] = edge[c]

    copy.wait()
    acc[...] = jnp.zeros_like(acc)

    def sites(x, carry):
        base = (x + 1) * PLANE
        for half in range(2):
            rows = pl.ds(8 * half, 8)
            start = 8 * half + 8
            total = [None] * 8

            def link_of(mu):
                return lambda p, i, j: links[18 * mu + 9 * p + entry(i, j), x, rows, :]

            g = [gs[pl.ds(base + 32 * k + start, 8), :] for k in range(18)]
            ahead = [gs[pl.ds(base + PLANE + 32 * k + start, 8), :] for k in range(18)]
            a = moved_algebra(g, link_of(0), ahead)
            for c in range(8):
                total[c] = prev[c, rows, :] - a[c]
                prev[c, rows, :] = a[c]
            ahead = [gs[pl.ds(base + 32 * k + start + 1, 8), :] for k in range(18)]
            a = moved_algebra(g, link_of(1), ahead)
            for c in range(8):
                ay[pl.ds(x * 192 + 24 * c + start, 8), :] = a[c]
            for c in range(8):
                total[c] = total[c] + (ay[pl.ds(x * 192 + 24 * c + start - 1, 8), :] - a[c])
            ahead = [pltpu.roll(v, 127, 1) for v in g]
            a = moved_algebra(g, link_of(2), ahead)
            for c in range(8):
                total[c] = total[c] + (pltpu.roll(a[c], 1, 1) - a[c])
                if last:
                    div[c, x, rows, :] = total[c]
                else:
                    sources[pl.ds(128 * c + 16 * x + 8 * half, 8), :] = total[c]
            acc[...] += squares(total)
        return carry

    lax.fori_loop(0, 8, sites, 0)
    if last:
        lane = lax.broadcasted_iota(jnp.int32, (1, 128), 1)
        sums = jnp.zeros((1, 128), F32)
        for k, part in enumerate((theta_first, theta_in, acc)):
            sums = sums + jnp.where(lane == k, jnp.sum(part[...]), 0.0)
        theta[...] = jnp.broadcast_to(sums, (128, 128))
    else:
        theta[...] = acc[...]
        for c in range(8):
            edge_x_out[c] = sources[pl.ds(128 * c, 16), :]
            edge_y_out[c] = sources[pl.ds(128 * c, 8, stride=16), :]
        encode(sources, 128, table, modes_out, packed, out)


def update_kernel(*refs):
    update_body(False, refs)


def last_kernel(*refs):
    update_body(True, refs)


def struct(*shape):
    return jax.ShapeDtypeStruct(shape, F32)


def vmem(*shape):
    return pltpu.VMEM(shape, F32)


def whole():
    return pl.BlockSpec(memory_space=pltpu.VMEM)


def in_hbm(value):
    return pltpu.with_memory_space_constraint(value, pltpu.HBM)


def params(size):
    return pltpu.CompilerParams(vmem_limit_bytes=size * MEGA)


EDGES = [(8, 16, 128), (8, 8, 128)]


def first_call(links, table):
    shapes = [struct(128, 384), struct(8, 128, 128)] + [struct(*e) for e in EDGES] + [struct(8, 128)]
    shapes += [jax.ShapeDtypeStruct(table.shape, table.dtype), struct(12, 16, 128), struct(12, 8, 128)]
    return pl.pallas_call(
        first_kernel,
        in_specs=[pl.BlockSpec(memory_space=pl.ANY)] * 2,
        out_specs=[whole()] * len(shapes),
        out_shape=shapes,
        scratch_shapes=[
            vmem(8, 54, 16, 128),
            vmem(8, 16, 128),
            vmem(8 * 152, 128),
            vmem(384, 128),
            pltpu.SemaphoreType.DMA((9,)),
        ],
        compiler_params=params(32),
        name="first_divergence",
    )(in_hbm(links), in_hbm(table))


def plane_call(own, recv, table):
    return pl.pallas_call(
        plane_kernel,
        in_specs=[pl.BlockSpec(memory_space=pltpu.SMEM)] + [whole()] * 2,
        out_specs=whole(),
        out_shape=struct(128, 384),
        scratch_shapes=[vmem(1024, 128), vmem(1024, 128), vmem(384, 128)],
        compiler_params=params(32),
        name="plane_solve",
    )(own, recv, table)


def update_call(recv, state, links, face_x, face_y, table, prior):
    last = prior is not None
    modes, edge_x, edge_y, theta = state
    operands = [recv, modes, edge_x, edge_y, in_hbm(links), face_x, face_y, theta, table]
    scratch = [
        vmem(54, 8, 16, 128),
        pltpu.SemaphoreType.DMA,
        vmem(384, 128),
        vmem(8 * 176, 128),
        vmem(10 * PLANE, 128),
        vmem(18, 8, 128),
        vmem(8 * 192, 128),
        vmem(8, 16, 128),
        vmem(8, 128),
    ]
    if last:
        shapes = [struct(8, 8, 16, 128), struct(2, 2, 3, 8, 16, 128), struct(128, 128)]
        operands += list(prior)
    else:
        shapes = [struct(128, 384), struct(8, 128, 128)] + [struct(*e) for e in EDGES]
        shapes += [struct(8, 128), struct(10, 18, 16, 128), struct(2, 18, 8, 128), struct(8, 128)]
        scratch += [vmem(8 * 128, 128)]
    return pl.pallas_call(
        last_kernel if last else update_kernel,
        in_specs=[pl.BlockSpec(memory_space=pl.ANY) if k == 4 else whole() for k in range(len(operands))],
        out_specs=[whole()] * len(shapes),
        out_shape=shapes,
        scratch_shapes=scratch,
        compiler_params=params(32),
        name="last_update" if last else "update",
    )(*operands)


def shifted(value, axis, steps):
    count = lax.axis_size(axis)
    pairs = [(source, (source + steps) % count) for source in range(count)]
    return lax.ppermute(value, axis, pairs)


def exchange(value):
    return lax.all_to_all(value, ("gx", "gy"), split_axis=0, concat_axis=0, tiled=True)


def per_device(links):
    flat = links.reshape(54, 8, 16, 128)
    own = (lax.axis_index("gx") * 8 + lax.axis_index("gy")).astype(jnp.int32).reshape(1)
    table = jnp.asarray(TABLE)
    packed, modes, edge_x, edge_y, theta, table, face_x, face_y = first_call(flat, table)
    face_x = shifted(face_x, "gx", 1)
    face_y = shifted(face_y, "gy", 1)
    state = (modes, edge_x, edge_y, theta)
    packed, own = lax.optimization_barrier((packed, own))
    prior = None
    for step in range(2):
        values = exchange(plane_call(own, exchange(packed), table))
        results = update_call(values, state, flat, face_x, face_y, table, prior)
        if step == 0:
            packed, modes, edge_x, edge_y, theta, gout, gout_y, theta_first = results
            state = (modes, edge_x, edge_y, theta)
            prior = (gout, gout_y, theta_first)
    div, gauge, sums = results
    sums = jnp.sum(exchange(sums), axis=0)[:3] / (3.0 * LS * LS * NZ)
    return (gauge, div, sums)


def solution(mesh):
    in_specs = (P(None, None, None, None, "gx", "gy", "ta"),)
    out_specs = (P(None, None, None, "gx", "gy", "ta"), P(None, "gx", "gy", "ta"), P("ta"))
    return jax.shard_map(
        per_device, mesh=mesh, in_specs=in_specs, out_specs=out_specs, check_vma=False
    )
```

```python
import math

import jax
import jax.numpy as jnp
import numpy as np
from jax import lax
from jax.experimental import pallas as pl
from jax.experimental.pallas import tpu as pltpu
from jax.sharding import PartitionSpec as P

LS = 128
NZ = 128
STEP_SIZE = 0.08
PEAK_MOMENTUM = 12.0
F32 = jnp.float32
BF16 = jnp.bfloat16
MEGA = 1024 * 1024


def real_basis(length):
    site = np.arange(length)[:, None]
    freq = np.arange(length)
    freq = np.where(freq <= length // 2, freq, freq - length // 2)
    phase = 2.0 * np.pi * ((site * freq[None, :]) % length) / length
    index = np.arange(length)[None, :]
    basis = np.where(index <= length // 2, np.cos(phase), np.sin(phase)) * np.sqrt(2.0 / length)
    basis[:, 0] = 1.0 / np.sqrt(length)
    basis[:, length // 2] = np.cos(np.pi * np.arange(length)) / np.sqrt(length)
    return basis, freq


def halves(table):
    high = table.astype(np.float32).astype(jnp.bfloat16)
    low = (table - high.astype(np.float64)).astype(np.float32).astype(jnp.bfloat16)
    return high, low


def right_table(table):
    high, low = halves(table)
    return np.concatenate([high, high, low], axis=0)


def left_table(table):
    high, low = halves(table)
    return np.concatenate([high, high, low], axis=1)


def sine_table():
    x, y = np.arange(8), np.arange(16)
    sx = np.sin(np.pi * np.outer(x, x) / 8.0) * np.sqrt(2.0 / 8.0)
    sy = np.sin(np.pi * np.outer(y, y) / 16.0) * np.sqrt(2.0 / 16.0)
    table = np.kron(sx, sy)
    keep = np.kron(x > 0, y > 0)
    table = table * np.outer(keep, keep)
    eigen = (4.0 * np.sin(np.pi * x / 16.0) ** 2)[:, None] + (4.0 * np.sin(np.pi * y / 32.0) ** 2)[None, :]
    return table, eigen.reshape(128), keep


BASIS, FREQ = real_basis(128)
SQUARES = 4.0 * np.sin(np.pi * FREQ / 128.0) ** 2
SINE, EIGEN, INNER = sine_table()


def node(x, y):
    return 16 * x + y


def reduce_table():
    out = np.zeros((48, 128))
    for y in range(1, 16):
        out[y] = SINE[node(1, y)]
        out[16 + y] = SINE[node(7, y)]
    out[32] = SINE[INNER].sum(0)
    for x in range(1, 8):
        out[32 + x] = SINE[node(x, 1)]
        out[40 + x] = SINE[node(x, 15)]
    return out


def source_table():
    out = np.zeros((128, 48))
    for y in range(1, 16):
        out[:, y] = SINE[node(1, y)]
        out[:, 16 + y] = SINE[node(7, y)]
    for x in range(1, 8):
        out[:, 32 + x] = SINE[node(x, 1)]
        out[:, 40 + x] = SINE[node(x, 15)]
    return out


def expand_table():
    out = np.zeros((176, 176))
    val = 128

    def line_x(x):
        return 0 if x == 0 else (16 if x == 8 else 32 + x)

    def line_y(y):
        return 40 if y == 16 else y

    for x in range(1, 8):
        for y in range(1, 16):
            out[node(x, y), :128] = SINE[node(x, y)]
    for y in range(16):
        out[node(0, y), val + y] = 1.0
        out[128 + y, val + 16 + y] = 1.0
    for x in range(1, 8):
        out[node(x, 0), val + 32 + x] = 1.0
    for x in range(8):
        out[160 + x, val + 40 + x] = 1.0
    out[144, val + 32] = 1.0
    for y in range(1, 16):
        row = out[144 + y]
        row[val + y] += 4.0
        row[:128] -= SINE[node(1, y)]
        row[val + line_y(y - 1)] -= 1.0
        row[val + line_y(y + 1)] -= 1.0
    for x in range(1, 8):
        row = out[168 + x]
        row[val + line_x(x)] += 4.0
        row[:128] -= SINE[node(x, 1)]
        row[val + line_x(x - 1)] -= 1.0
        row[val + line_x(x + 1)] -= 1.0
    row = out[168]
    row[val] += 4.0
    row[val + 33] -= 1.0
    row[val + 32] -= 1.0
    row[val + 1] -= 1.0
    high, low = halves(out)
    assert not np.any(low[:, 128:].astype(np.float32))
    return np.concatenate([high, high, low[:, :128]], axis=1)


def lines_in():
    out = np.zeros((128, 128))
    for g in range(8):
        out[16 * g : 16 * g + 16] = BASIS[16 * g]
    return out


def lines_out():
    out = np.zeros((128, 128))
    for g in range(8):
        out[:, 16 * g : 16 * g + 8] = BASIS[16 * g][:, None]
        out[:, 16 * g + 8 : 16 * g + 16] = BASIS[(16 * g + 16) % 128][:, None]
    return out


SCALE = STEP_SIZE * PEAK_MOMENTUM
ORDER = np.array([8 * j + x for x in range(8) for j in range(16)])


def pack_tables():
    out = np.zeros((992, 768), jnp.bfloat16)
    rights = (BASIS * SCALE, BASIS.T, BASIS, lines_in(), lines_out())
    for k, table in enumerate(rights):
        out[:384, 128 * k : 128 * k + 128] = right_table(table)
    out[384:512, :384] = left_table(SINE)
    out[384:512, 384:] = left_table(BASIS[ORDER].T)
    out[512:640, :384] = left_table(BASIS[ORDER])
    out[512:640, 384:528] = left_table(source_table())
    out[640:688, :384] = left_table(reduce_table())
    out[688:864, :480] = expand_table()
    for k, table in enumerate((INVERSE, PLANE_SUM)):
        rest = table.astype(np.float32).astype(np.float64)
        for part in range(3):
            piece = rest.astype(np.float32).astype(jnp.bfloat16)
            lanes = 384 * k + 128 * part
            out[864:992, lanes : lanes + 128] = piece
            rest = rest - piece.astype(np.float64)
    return out


INVERSE = INNER[:, None] / (np.where(INNER, EIGEN, 1.0)[:, None] + SQUARES[None, :])
PLANE_SUM = SQUARES[:, None] + SQUARES[None, :]
TABLE = pack_tables()
Z_IN, Z_OUT, Y_IN, LINES_IN, LINES_OUT = [(slice(0, 384), slice(128 * k, 128 * k + 128)) for k in range(5)]
MODES = (slice(384, 512), slice(0, 384))
X_IN = (slice(384, 512), slice(384, 768))
X_OUT = (slice(512, 640), slice(0, 384))
SOURCE = (slice(512, 640), slice(384, 528))
REDUCE = (slice(640, 688), slice(0, 384))
EXPAND = (slice(688, 864), slice(0, 480))


def float_table(table, which, rows=128):
    parts = [
        table[864 : 864 + rows, 384 * which + 128 * k : 384 * which + 128 * k + 128].astype(F32)
        for k in range(3)
    ]
    return (parts[0] + parts[1]) + parts[2]


def three_lanes(value):
    high = value.astype(BF16)
    low = (value - high.astype(F32)).astype(BF16)
    return jnp.concatenate([high, low, high], axis=1)


def three_rows(value):
    high = value.astype(BF16)
    low = (value - high.astype(F32)).astype(BF16)
    return jnp.concatenate([high, low, high], axis=0)


def swap_blocks(tiles):
    tiles = list(tiles)
    group = lax.broadcasted_iota(jnp.int32, tiles[0].shape, 1) // 16
    for bit in (1, 2, 4):
        upper = (group & bit) != 0
        for i in range(8):
            if i & bit:
                continue
            low, high = tiles[i], tiles[i | bit]
            tiles[i] = jnp.where(upper, pltpu.roll(high, 16 * bit, 1), low)
            tiles[i | bit] = jnp.where(upper, high, pltpu.roll(low, 128 - 16 * bit, 1))
    return tiles


def algebra(mreal, mimag):
    i00, i11, i22 = mimag(0, 0), mimag(1, 1), mimag(2, 2)
    middle = (i00 + i11 + i22) * (1.0 / 3.0)
    return [
        i00 - middle,
        i11 - middle,
        (mreal(0, 1) - mreal(1, 0)) * 0.5,
        (mimag(0, 1) + mimag(1, 0)) * 0.5,
        (mreal(0, 2) - mreal(2, 0)) * 0.5,
        (mimag(0, 2) + mimag(2, 0)) * 0.5,
        (mreal(1, 2) - mreal(2, 1)) * 0.5,
        (mimag(1, 2) + mimag(2, 1)) * 0.5,
    ]


def squares(c):
    third = c[0] + c[1]
    rest = c[2] * c[2] + c[3] * c[3] + c[4] * c[4] + c[5] * c[5] + c[6] * c[6] + c[7] * c[7]
    return c[0] * c[0] + c[1] * c[1] + third * third + 2.0 * rest


def entry(row, col):
    return row * 3 + col


def cross_row(first_re, first_im, second_re, second_im):
    out_re, out_im = [], []
    for k in range(3):
        a, b = (k + 1) % 3, (k + 2) % 3
        out_re.append(
            first_re[a] * second_re[b]
            - first_im[a] * second_im[b]
            - first_re[b] * second_re[a]
            + first_im[b] * second_im[a]
        )
        out_im.append(
            first_re[b] * second_im[a]
            + first_im[b] * second_re[a]
            - first_re[a] * second_im[b]
            - first_im[a] * second_re[b]
        )
    return out_re, out_im


def exponent_rows(c):
    c0, c1, c2, c3, c4, c5, c6, c7 = c
    n01 = c2 * c2 + c3 * c3
    n02 = c4 * c4 + c5 * c5
    n12 = c6 * c6 + c7 * c7
    s00 = 1.0 - 0.5 * (c0 * c0 + n01 + n02)
    s11 = 1.0 - 0.5 * (c1 * c1 + n01 + n12)
    d01 = c0 + c1
    p01r = -(d01 * c3) - (c4 * c6 + c5 * c7)
    p01i = d01 * c2 - (c5 * c6 - c4 * c7)
    p02r = c1 * c5 + (c2 * c6 - c3 * c7)
    p02i = -(c1 * c4) + (c2 * c7 + c3 * c6)
    p12r = -(c2 * c4 + c3 * c5) + c0 * c7
    p12i = -(c2 * c5 - c3 * c4) - c0 * c6
    r0 = [s00, c2 + 0.5 * p01r, c4 + 0.5 * p02r]
    i0 = [c0, c3 + 0.5 * p01i, c5 + 0.5 * p02i]
    r1 = [-c2 + 0.5 * p01r, s11, c6 + 0.5 * p12r]
    i1 = [c3 - 0.5 * p01i, c1, c7 + 0.5 * p12i]
    size = sum(r0[k] * r0[k] + i0[k] * i0[k] for k in range(3))
    scale = lax.rsqrt(size)
    r0 = [v * scale for v in r0]
    i0 = [v * scale for v in i0]
    pr = sum(r0[k] * r1[k] + i0[k] * i1[k] for k in range(3))
    pi = sum(r0[k] * i1[k] - i0[k] * r1[k] for k in range(3))
    r1, i1 = (
        [r1[k] - (pr * r0[k] - pi * i0[k]) for k in range(3)],
        [i1[k] - (pr * i0[k] + pi * r0[k]) for k in range(3)],
    )
    size = sum(r1[k] * r1[k] + i1[k] * i1[k] for k in range(3))
    scale = lax.rsqrt(size)
    r1 = [v * scale for v in r1]
    i1 = [v * scale for v in i1]
    return r0 + r1, i0 + i1


def full_matrix(re6, im6):
    re3, im3 = cross_row(re6[:3], im6[:3], re6[3:], im6[3:])
    return list(re6) + re3 + list(im6) + im3


def times_rows(gre, gim, hre, him):
    out_re, out_im = [], []
    for i in range(2):
        for j in range(3):
            acc_re = acc_im = None
            for k in range(3):
                ar, ai = gre[entry(i, k)], gim[entry(i, k)]
                br, bi = hre[entry(k, j)], him[entry(k, j)]
                pr, pi = ar * br - ai * bi, ar * bi + ai * br
                acc_re = pr if acc_re is None else acc_re + pr
                acc_im = pi if acc_im is None else acc_im + pi
            out_re.append(acc_re)
            out_im.append(acc_im)
    return out_re, out_im


def moved_algebra(g, link, ahead):
    gre, gim = g[:9], g[9:]
    are, aim = ahead[:9], ahead[9:]
    vre, vim = [None] * 9, [None] * 9
    for i in range(2):
        ur = [link(0, i, k) for k in range(3)]
        ui = [link(1, i, k) for k in range(3)]
        for j in range(3):
            br = [are[entry(j, k)] for k in range(3)]
            bi = [aim[entry(j, k)] for k in range(3)]
            vre[entry(i, j)] = (ur[0] * br[0] + ui[0] * bi[0]) + (
                (ur[1] * br[1] + ui[1] * bi[1]) + (ur[2] * br[2] + ui[2] * bi[2])
            )
            vim[entry(i, j)] = (ui[0] * br[0] - ur[0] * bi[0]) + (
                (ui[1] * br[1] - ur[1] * bi[1]) + (ui[2] * br[2] - ur[2] * bi[2])
            )

    vre[6:], vim[6:] = cross_row(vre[:3], vim[:3], vre[3:6], vim[3:6])

    def mreal(i, j):
        return sum(
            gre[entry(i, k)] * vre[entry(k, j)] - gim[entry(i, k)] * vim[entry(k, j)]
            for k in range(3)
        )

    def mimag(i, j):
        return sum(
            gre[entry(i, k)] * vim[entry(k, j)] + gim[entry(i, k)] * vre[entry(k, j)]
            for k in range(3)
        )

    return algebra(mreal, mimag)


PLANE = 18 * 32


def dot(left, right):
    return jnp.dot(left, right, preferred_element_type=F32)


def wide(pieces):
    return jnp.concatenate([three_rows(piece) for piece in pieces], axis=1)


def tile(value, c):
    return value[:, 128 * c : 128 * c + 128]


def encode(spectrum, stride, table, modes, packed, out):
    mode = dot(table[MODES], wide([spectrum[pl.ds(stride * c, 128), :] for c in range(8)]))
    inverse = float_table(table, 0)
    scaled = []
    for c in range(8):
        scaled.append(inverse * tile(mode, c))
        modes[c] = scaled[c]
    reduced = dot(table[REDUCE], wide(scaled))
    corner = lax.broadcasted_iota(jnp.int32, (8, 128), 0) == 0
    for c in range(8):
        start = stride * c
        values = tile(reduced, c)
        line_x = values[0:16] + spectrum[pl.ds(start, 16), :]
        line_y = jnp.where(corner, 0.0, spectrum[pl.ds(start, 8, stride=16), :])
        next_x, next_y = values[16:32], values[40:48]
        if stride > 128:
            next_x = next_x + spectrum[pl.ds(start + 128, 16), :]
            next_y = next_y + spectrum[pl.ds(start + 144, 8), :]
        groups = [line_x, next_x, jnp.concatenate([values[32:40] + line_y, next_y], axis=0)]
        for t in range(3):
            packed[pl.ds(128 * t + 16 * c, 16), :] = groups[t]
    for t in range(3):
        out[pl.ds(t, 128, stride=3), :] = packed[pl.ds(128 * t, 128), :].T


def first_kernel(*refs):
    links_hbm, table_hbm, out, modes, edge_x, edge_y, theta, table, face_x, face_y = refs[:10]
    links, prev, sources, packed, sems = refs[10:]

    def plane_copy(x):
        return pltpu.make_async_copy(links_hbm.at[:, x], links.at[:, x], sems.at[x])

    for x in range(8):
        plane_copy(x).start()
    table_copy = pltpu.make_async_copy(table_hbm, table, sems.at[8])
    table_copy.start()
    prev[...] = jnp.zeros_like(prev)
    theta[...] = jnp.zeros_like(theta)
    row = lax.broadcasted_iota(jnp.int32, (16, 128), 0)

    def planes(x, carry):
        plane_copy(x).wait()

        def of(mu):
            return algebra(
                lambda i, j: links[18 * mu + entry(i, j), x],
                lambda i, j: links[18 * mu + 9 + entry(i, j), x],
            )

        ax, ay, az = of(0), of(1), of(2)
        comps = []
        for c in range(8):
            back_y = jnp.where(row == 0, 0.0, pltpu.roll(ay[c], 1, 0))
            value = (prev[c] + back_y + pltpu.roll(az[c], 1, 1)) - ax[c] - ay[c] - az[c]
            prev[c] = ax[c]
            comps.append(value)
            sources[pl.ds(152 * c + 16 * x, 16), :] = value
            sources[pl.ds(152 * c + 144 + x, 1), :] = ay[c][15:16]
        for k in range(12):
            face_y[k, pl.ds(x, 1), :] = links[18 + k % 6 + 9 * (k // 6), x, 15:16, :]
        inner = jnp.where((row > 0) & (x > 0), squares(comps), 0.0)
        theta[...] += inner[:8] + inner[8:]
        return carry

    lax.fori_loop(0, 8, planes, 0)
    for c in range(8):
        sources[pl.ds(152 * c + 128, 16), :] = prev[c]
        edge_x[c] = sources[pl.ds(152 * c, 16), :]
        edge_y[c] = sources[pl.ds(152 * c, 8, stride=16), :]
    for k in range(12):
        face_x[k] = links[k % 6 + 9 * (k // 6), 7]
    table_copy.wait()
    sources[...] = dot(three_lanes(sources[...]), table[Z_IN])
    encode(sources, 152, table, modes, packed, out)


def plane_kernel(own, recv, table, out, work, lines):
    lane = lax.broadcasted_iota(jnp.int32, (16, 128), 1) % 16
    zero = jnp.where(own[0] == 0, -1.0 / (LS * LS), 0.0)
    total = float_table(table, 1)
    work[pl.ds(0, 128), :] = total
    total = total + work[pl.ds(own[0], 1), :][:, 0:1]
    inverse = jnp.where(total > 0.0, 1.0 / jnp.where(total > 0.0, total, 1.0), 0.0)
    shifts = []
    moved = [
        swap_blocks([recv[pl.ds(3 * g + t, 16, stride=24), :] for g in range(8)])
        for t in range(3)
    ]
    for c in range(8):
        third = moved[2][c]
        rolled = pltpu.roll(third, 8, 1)
        first = moved[0][c] + pltpu.roll(moved[1][c], 1, 0) + jnp.where(lane == 0, rolled, 0.0)
        work[pl.ds(16 * c, 16), :] = first
        both = third + rolled
        for x in range(1, 8):
            work[pl.ds(128 * x + 16 * c, 16), :] = jnp.where(lane == x, both, 0.0)
        extra = jnp.sum(jnp.where(lane == 0, third, 0.0), axis=0, keepdims=True)
        shifts.append(jnp.sum(extra, axis=1, keepdims=True) * zero)
    lines[pl.ds(0, 128), :] = dot(three_lanes(work[pl.ds(0, 128), :]), table[Y_IN])
    lines[pl.ds(128, 896), :] = dot(three_lanes(work[pl.ds(128, 896), :]), table[LINES_IN])
    blocks = [
        jnp.concatenate([lines[pl.ds(128 * x + 16 * c, 16), :] for x in range(8)], axis=0)
        for c in range(8)
    ]
    spectrum = dot(table[X_IN], wide(blocks))
    spectrum = dot(table[X_OUT], wide([tile(spectrum, c) * inverse for c in range(8)]))
    spectrum = [tile(spectrum, c) for c in range(8)]
    at_lines = dot(three_lanes(jnp.concatenate(spectrum, axis=0)), table[LINES_OUT])
    first = jnp.concatenate([part[:16] for part in spectrum], axis=0)
    first = dot(three_lanes(first), table[Z_OUT])
    groups = [[], [], []]
    for c in range(8):
        own_line = first[16 * c : 16 * c + 16] + shifts[c]
        groups[0].append(own_line)
        groups[1].append(pltpu.roll(own_line, 15, 0))
        parts = [at_lines[128 * c + 16 * x : 128 * c + 16 * x + 16] for x in range(8)]
        third = jnp.where(lane == 0, pltpu.roll(parts[7], 1, 0), parts[0])
        for x in range(1, 8):
            third = jnp.where((lane == x) | (lane == 8 + x), parts[x], third)
        groups[2].append(third + shifts[c])
    for t in range(3):
        tiles = swap_blocks(groups[t])
        for g in range(8):
            out[pl.ds(3 * g + t, 16, stride=24), :] = tiles[g]


def decode(recv, modes, table, packed, comps_in):
    for t in range(3):
        packed[pl.ds(128 * t, 128), :] = recv[pl.ds(t, 128, stride=3), :].T
    mass = float_table(table, 1, 16)[0:1]
    inverse = float_table(table, 0)
    values = [
        jnp.concatenate([packed[pl.ds(128 * t + 16 * c, 16), :] for t in range(3)], axis=0)
        for c in range(8)
    ]
    mode = dot(table[SOURCE], wide(values))
    stacks = []
    for c in range(8):
        own = modes[c] + inverse * tile(mode, c)
        value = jnp.concatenate([own, values[c]], axis=0)
        high = value.astype(BF16)
        low = (value - high.astype(F32)).astype(BF16)
        stacks.append(jnp.concatenate([high, low, high[:128]], axis=0))
    sites = dot(table[EXPAND], jnp.concatenate(stacks, axis=1))
    row = lax.broadcasted_iota(jnp.int32, (16, 128), 0)
    parts = []
    for c in range(8):
        part, value = tile(sites, c), values[c]
        behind = part[144:160] + mass * jnp.where(row == 0, 0.0, value[0:16])
        below = part[168:176] + mass * jnp.where(row[:8] == 0, value[0:8], value[32:40])
        parts.append(jnp.concatenate([part[:144], behind, part[160:168], below], axis=0))
    comps_in[...] = dot(three_lanes(jnp.concatenate(parts, axis=0)), table[Z_OUT])


def make(c, before=None):
    re6, im6 = exponent_rows(c)
    if before is not None:
        re6, im6 = times_rows(re6, im6, before[:9], before[9:])
    return full_matrix(re6, im6)


def start_links(links_hbm, links, sems):
    def plane_copy(x):
        return pltpu.make_async_copy(links_hbm.at[:, x], links.at[:, x], sems.at[x])

    for x in range(8):
        plane_copy(x).start()
    return plane_copy


def moved_divergence(links, plane_copy, gs, ay, prev, emit):
    def sites(x, carry):
        plane_copy(x).wait()
        base = (x + 1) * PLANE
        for half in range(2):
            rows = pl.ds(8 * half, 8)
            start = 8 * half + 8
            total = [None] * 8

            def link_of(mu):
                return lambda p, i, j: links[18 * mu + 9 * p + entry(i, j), x, rows, :]

            g = [gs[pl.ds(base + 32 * k + start, 8), :] for k in range(18)]
            ahead = [gs[pl.ds(base + PLANE + 32 * k + start, 8), :] for k in range(18)]
            a = moved_algebra(g, link_of(0), ahead)
            for c in range(8):
                total[c] = prev[c, rows, :] - a[c]
                prev[c, rows, :] = a[c]
            ahead = [gs[pl.ds(base + 32 * k + start + 1, 8), :] for k in range(18)]
            a = moved_algebra(g, link_of(1), ahead)
            for c in range(8):
                ay[pl.ds(x * 192 + 24 * c + start, 8), :] = a[c]
            for c in range(8):
                total[c] = total[c] + (ay[pl.ds(x * 192 + 24 * c + start - 1, 8), :] - a[c])
            top = [v[7:8] for v in a]
            ahead = [pltpu.roll(v, 127, 1) for v in g]
            a = moved_algebra(g, link_of(2), ahead)
            for c in range(8):
                total[c] = total[c] + (pltpu.roll(a[c], 1, 1) - a[c])
            emit(x, half, total, top)
        return carry

    lax.fori_loop(0, 8, sites, 0)


def update_kernel(*refs):
    recv, modes, links_hbm, table = refs[:4]
    out, modes_out, edge_x, edge_y, theta, gout, gout_y, raw_x, raw_y = refs[4:13]
    links, sems, packed, comps_in, gs, ay, prev, sources = refs[13:]
    plane_copy = start_links(links_hbm, links, sems)
    decode(recv, modes, table, packed, comps_in)
    for c in range(8):
        raw_x[c] = comps_in[pl.ds(176 * c + 144, 16), :]
        raw_y[c] = comps_in[pl.ds(176 * c + 168, 8), :]

    def plane(index, first_row):
        for half in range(2):
            g = make([comps_in[pl.ds(first_row(c) + 8 * half, 8), :] for c in range(8)])
            for k in range(18):
                gs[pl.ds(index * PLANE + 32 * k + 8 * half + 8, 8), :] = g[k]
                gout[pl.ds((index - 1) * 288 + 16 * k + 8 * half, 8), :] = g[k]

    def inner(x, carry):
        plane(x + 1, lambda c: 176 * c + 16 * x)
        return carry

    lax.fori_loop(0, 8, inner, 0)
    plane(9, lambda c: 176 * c + 128)
    g = make([comps_in[pl.ds(176 * c + 160, 8), :] for c in range(8)])
    for k in range(18):
        gout_y[k] = g[k]
        gs[pl.ds(PLANE + 32 * k + 24, 8, stride=PLANE), :] = g[k]

    prev[...] = jnp.zeros_like(prev)
    theta[...] = jnp.zeros_like(theta)
    for c in range(8):
        ay[pl.ds(24 * c + 7, 8, stride=192), :] = jnp.zeros((8, 128), F32)
    row = lax.broadcasted_iota(jnp.int32, (8, 128), 0)

    def emit(x, half, total, top):
        for c in range(8):
            sources[pl.ds(152 * c + 16 * x + 8 * half, 8), :] = total[c]
            if half == 1:
                sources[pl.ds(152 * c + 144 + x, 1), :] = top[c]
        theta[...] += jnp.where((x > 0) & (row + half > 0), squares(total), 0.0)

    moved_divergence(links, plane_copy, gs, ay, prev, emit)
    for c in range(8):
        sources[pl.ds(152 * c + 128, 16), :] = prev[c]
        edge_x[c] = sources[pl.ds(152 * c, 16), :]
        edge_y[c] = sources[pl.ds(152 * c, 8, stride=16), :]
    sources[...] = dot(three_lanes(sources[...]), table[Z_IN])
    encode(sources, 152, table, modes_out, packed, out)


def whole_lines(line_x, line_y, add_x, add_y):
    top = lax.broadcasted_iota(jnp.int32, (16, 128), 0) == 0
    out_x, out_y = [], []
    for c in range(8):
        out_x.append(line_x[c] + add_x[c] + jnp.where(top, add_y[c][0:1], 0.0))
        out_y.append(line_y[c] + add_y[c] + jnp.where(top[:8], add_x[c][0:1], 0.0))
    sq = squares(out_x)
    return out_x, out_y, sq[:8] + sq[8:] + jnp.where(top[:8], 0.0, squares(out_y))


def last_kernel(*refs):
    recv, modes, links_hbm, table, line0_x, line0_y, line1_x, line1_y, raw_x, raw_y = refs[:10]
    face_x, face_y, theta0, theta1, prior, prior_y, div, gauge, theta = refs[10:19]
    links, sems, packed, comps_in, gs, behind, below, ay, prev, acc = refs[19:]
    plane_copy = start_links(links_hbm, links, sems)
    decode(recv, modes, table, packed, comps_in)
    row = lax.broadcasted_iota(jnp.int32, (16, 128), 0)

    face = full_matrix([face_x[k] for k in range(6)], [face_x[6 + k] for k in range(6)])
    add_x = algebra(lambda i, j: face[entry(i, j)], lambda i, j: face[9 + entry(i, j)])
    face = full_matrix([face_y[k] for k in range(6)], [face_y[6 + k] for k in range(6)])
    add_y = algebra(lambda i, j: face[entry(i, j)], lambda i, j: face[9 + entry(i, j)])
    whole_x, whole_y, extra0 = whole_lines(line0_x, line0_y, add_x, add_y)
    for half in range(2):
        rows = pl.ds(8 * half, 8)
        part = slice(8 * half, 8 * half + 8)
        taken = [jnp.where(row == 0, 0.0, SCALE * whole_x[c])[part] for c in range(8)]
        g = make([raw_x[c, rows, :] - taken[c] for c in range(8)])
        for k in range(18):
            behind[k, rows, :] = g[k]
        ahead = [prior[pl.ds(16 * k + 8 * half, 8), :] for k in range(18)]
        edge = moved_algebra(g, lambda p, i, j: face_x[6 * p + entry(i, j), rows, :], ahead)
        for c in range(8):
            prev[c, rows, :] = edge[c]
    g = make([raw_y[c] - SCALE * whole_y[c] for c in range(8)])
    for k in range(18):
        below[k] = g[k]
    ahead = [prior[pl.ds(16 * k, 8, stride=288), :] for k in range(18)]
    edge = moved_algebra(g, lambda p, i, j: face_y[6 * p + entry(i, j)], ahead)
    whole_x, whole_y, extra1 = whole_lines(line1_x, line1_y, prev, edge)

    for c in range(8):
        rows = pl.ds(176 * c + 144, 16)
        comps_in[rows, :] = comps_in[rows, :] - jnp.where(row == 0, 0.0, SCALE * whole_x[c])
        rows = pl.ds(176 * c + 168, 8)
        comps_in[rows, :] = comps_in[rows, :] - SCALE * whole_y[c]

    def plane(index, first_row, before):
        for half in range(2):
            rows = pl.ds(8 * half, 8)
            g = make([comps_in[pl.ds(first_row(c) + 8 * half, 8), :] for c in range(8)], before(half))
            for k in range(18):
                gs[pl.ds(index * PLANE + 32 * k + 8 * half + 8, 8), :] = g[k]
            if not isinstance(index, int):
                for p in range(2):
                    for i in range(2):
                        for j in range(3):
                            gauge[p, i, j, index - 1, rows, :] = g[9 * p + entry(i, j)]

    def before_at(index):
        return lambda half: [
            prior[pl.ds((index - 1) * 288 + 16 * k + 8 * half, 8), :] for k in range(18)
        ]

    def inner(x, carry):
        plane(x + 1, lambda c: 176 * c + 16 * x, before_at(x + 1))
        return carry

    lax.fori_loop(0, 8, inner, 0)
    plane(
        0,
        lambda c: 176 * c + 144,
        lambda half: [behind[k, pl.ds(8 * half, 8), :] for k in range(18)],
    )
    plane(9, lambda c: 176 * c + 128, before_at(9))
    g = make(
        [comps_in[pl.ds(176 * c + 160, 8), :] for c in range(8)], [prior_y[k] for k in range(18)]
    )
    for k in range(18):
        gs[pl.ds(PLANE + 32 * k + 24, 8, stride=PLANE), :] = g[k]

    g = make([comps_in[pl.ds(176 * c + 168, 8), :] for c in range(8)], [below[k] for k in range(18)])
    ahead = [gs[pl.ds(PLANE + 32 * k + 8, 8, stride=PLANE), :] for k in range(18)]
    edge = moved_algebra(g, lambda p, i, j: face_y[6 * p + entry(i, j)], ahead)
    for c in range(8):
        ay[pl.ds(24 * c + 7, 8, stride=192), :] = edge[c]
    for half in range(2):
        rows = pl.ds(8 * half, 8)
        start = 8 * half + 8
        g = [gs[pl.ds(32 * k + start, 8), :] for k in range(18)]
        ahead = [gs[pl.ds(PLANE + 32 * k + start, 8), :] for k in range(18)]
        edge = moved_algebra(g, lambda p, i, j: face_x[6 * p + entry(i, j), rows, :], ahead)
        for c in range(8):
            prev[c, rows, :] = edge[c]

    acc[...] = jnp.zeros_like(acc)

    def emit(x, half, total, top):
        for c in range(8):
            div[c, x, pl.ds(8 * half, 8), :] = total[c]
        acc[...] += squares(total)

    moved_divergence(links, plane_copy, gs, ay, prev, emit)
    lane = lax.broadcasted_iota(jnp.int32, (1, 128), 1)
    sums = jnp.zeros((1, 128), F32)
    for k, part in enumerate((theta0[...] + extra0, theta1[...] + extra1, acc[...])):
        sums = sums + jnp.where(lane == k, jnp.sum(part), 0.0)
    theta[...] = jnp.broadcast_to(sums * (1.0 / (3.0 * LS * LS * NZ)), (128, 128))


def struct(*shape):
    return jax.ShapeDtypeStruct(shape, F32)


def vmem(*shape):
    return pltpu.VMEM(shape, F32)


def whole():
    return pl.BlockSpec(memory_space=pltpu.VMEM)


def in_hbm(value):
    return pltpu.with_memory_space_constraint(value, pltpu.HBM)


def params(size):
    return pltpu.CompilerParams(vmem_limit_bytes=size * MEGA)


EDGES = [(8, 16, 128), (8, 8, 128)]


def first_call(links, table):
    shapes = [struct(384, 128), struct(8, 128, 128)] + [struct(*e) for e in EDGES] + [struct(8, 128)]
    shapes += [jax.ShapeDtypeStruct(table.shape, table.dtype), struct(12, 16, 128), struct(12, 8, 128)]
    return pl.pallas_call(
        first_kernel,
        in_specs=[pl.BlockSpec(memory_space=pl.ANY)] * 2,
        out_specs=[whole()] * len(shapes),
        out_shape=shapes,
        scratch_shapes=[
            vmem(54, 8, 16, 128),
            vmem(8, 16, 128),
            vmem(8 * 152, 128),
            vmem(384, 128),
            pltpu.SemaphoreType.DMA((9,)),
        ],
        compiler_params=params(32),
        name="first_divergence",
    )(in_hbm(links), in_hbm(table))


def plane_call(own, recv, table):
    return pl.pallas_call(
        plane_kernel,
        in_specs=[pl.BlockSpec(memory_space=pltpu.SMEM)] + [whole()] * 2,
        out_specs=whole(),
        out_shape=struct(384, 128),
        scratch_shapes=[vmem(1024, 128), vmem(1024, 128)],
        compiler_params=params(32),
        name="plane_solve",
    )(own, recv, table)


def update_call(kernel, operands, shapes, extra, name):
    scratch = [
        vmem(54, 8, 16, 128),
        pltpu.SemaphoreType.DMA((8,)),
        vmem(384, 128),
        vmem(8 * 176, 128),
        vmem(10 * PLANE, 128),
    ]
    return pl.pallas_call(
        kernel,
        in_specs=[pl.BlockSpec(memory_space=pl.ANY) if k == 2 else whole() for k in range(len(operands))],
        out_specs=[whole()] * len(shapes),
        out_shape=shapes,
        scratch_shapes=scratch + extra,
        compiler_params=params(32),
        name=name,
    )(*operands)


def shifted(value, axis, steps):
    count = lax.axis_size(axis)
    pairs = [(source, (source + steps) % count) for source in range(count)]
    return lax.ppermute(value, axis, pairs)


def exchange(value):
    rows = value.reshape(128, 1, value.size // 128)
    rows = lax.all_to_all(rows, ("gx", "gy"), split_axis=0, concat_axis=0, tiled=True)
    return rows.reshape(value.shape)


def per_device(links):
    flat = links.reshape(54, 8, 16, 128)
    own = (lax.axis_index("gx") * 8 + lax.axis_index("gy")).astype(jnp.int32).reshape(1)
    table = jnp.asarray(TABLE)
    packed, modes, edge_x, edge_y, theta, table, face_x, face_y = first_call(flat, table)
    face_x = shifted(face_x, "gx", 1)
    face_y = shifted(face_y, "gy", 1)
    packed, own = lax.optimization_barrier((packed, own))
    values = exchange(plane_call(own, exchange(packed), table))
    edges = [struct(*e) for e in EDGES]
    shapes = [struct(384, 128), struct(8, 128, 128)] + edges + [struct(8, 128)]
    shapes += [struct(9 * 288, 128), struct(18, 8, 128)] + edges
    packed, modes, edge1_x, edge1_y, theta1, prior, prior_y, raw_x, raw_y = update_call(
        update_kernel,
        [values, modes, in_hbm(flat), table],
        shapes,
        [vmem(8 * 192, 128), vmem(8, 16, 128), vmem(8 * 152, 128)],
        "update",
    )
    packed, face_x, face_y = lax.optimization_barrier((packed, face_x, face_y))
    values = exchange(plane_call(own, exchange(packed), table))
    operands = [values, modes, in_hbm(flat), table, edge_x, edge_y, edge1_x, edge1_y, raw_x, raw_y]
    operands += [face_x, face_y, theta, theta1, prior, prior_y]
    div, gauge, sums = update_call(
        last_kernel,
        operands,
        [struct(8, 8, 16, 128), struct(2, 2, 3, 8, 16, 128), struct(128, 128)],
        [vmem(18, 16, 128), vmem(18, 8, 128), vmem(8 * 192, 128), vmem(8, 16, 128), vmem(8, 128)],
        "last_update",
    )
    return (gauge, div, jnp.sum(exchange(sums)[:, :3], axis=0))


def solution(mesh):
    in_specs = (P(None, None, None, None, "gx", "gy", "ta"),)
    out_specs = (P(None, None, None, "gx", "gy", "ta"), P(None, "gx", "gy", "ta"), P("ta"))
    return jax.shard_map(
        per_device, mesh=mesh, in_specs=in_specs, out_specs=out_specs, check_vma=False
    )
```

```python
import math

import jax
import jax.numpy as jnp
import numpy as np
from jax import lax
from jax.experimental import pallas as pl
from jax.experimental.pallas import tpu as pltpu
from jax.sharding import PartitionSpec as P

LS = 128
NZ = 128
STEP_SIZE = 0.08
PEAK_MOMENTUM = 12.0
F32 = jnp.float32
BF16 = jnp.bfloat16
MEGA = 1024 * 1024


def real_basis(length):
    site = np.arange(length)[:, None]
    freq = np.arange(length)
    freq = np.where(freq <= length // 2, freq, freq - length // 2)
    phase = 2.0 * np.pi * ((site * freq[None, :]) % length) / length
    index = np.arange(length)[None, :]
    basis = np.where(index <= length // 2, np.cos(phase), np.sin(phase)) * np.sqrt(2.0 / length)
    basis[:, 0] = 1.0 / np.sqrt(length)
    basis[:, length // 2] = np.cos(np.pi * np.arange(length)) / np.sqrt(length)
    return basis, freq


def thirds(table):
    rest, out = table.astype(np.float32).astype(np.float64), []
    for _ in range(3):
        piece = rest.astype(np.float32).astype(jnp.bfloat16)
        out.append(piece)
        rest = rest - piece.astype(np.float64)
    return out


def right_table(table):
    return np.concatenate(thirds(table), axis=0)


def left_table(table):
    return np.concatenate(thirds(table), axis=1)


def sine_table():
    x, y = np.arange(8), np.arange(16)
    sx = np.sin(np.pi * np.outer(x, x) / 8.0) * np.sqrt(2.0 / 8.0)
    sy = np.sin(np.pi * np.outer(y, y) / 16.0) * np.sqrt(2.0 / 16.0)
    table = np.kron(sx, sy)
    keep = np.kron(x > 0, y > 0)
    table = table * np.outer(keep, keep)
    eigen = (4.0 * np.sin(np.pi * x / 16.0) ** 2)[:, None] + (4.0 * np.sin(np.pi * y / 32.0) ** 2)[None, :]
    return table, eigen.reshape(128), keep


BASIS, FREQ = real_basis(128)
SQUARES = 4.0 * np.sin(np.pi * FREQ / 128.0) ** 2
SINE, EIGEN, INNER = sine_table()


def node(x, y):
    return 16 * x + y


def reduce_table():
    out = np.zeros((48, 128))
    for y in range(1, 16):
        out[y] = SINE[node(1, y)]
        out[16 + y] = SINE[node(7, y)]
    out[32] = SINE[INNER].sum(0)
    for x in range(1, 8):
        out[32 + x] = SINE[node(x, 1)]
        out[40 + x] = SINE[node(x, 15)]
    return out


def source_table():
    out = np.zeros((128, 48))
    for y in range(1, 16):
        out[:, y] = SINE[node(1, y)]
        out[:, 16 + y] = SINE[node(7, y)]
    for x in range(1, 8):
        out[:, 32 + x] = SINE[node(x, 1)]
        out[:, 40 + x] = SINE[node(x, 15)]
    return out


def expand_table():
    out = np.zeros((176, 176))
    val = 128

    def line_x(x):
        return 0 if x == 0 else (16 if x == 8 else 32 + x)

    def line_y(y):
        return 40 if y == 16 else y

    for x in range(1, 8):
        for y in range(1, 16):
            out[node(x, y), :128] = SINE[node(x, y)]
    for y in range(16):
        out[node(0, y), val + y] = 1.0
        out[128 + y, val + 16 + y] = 1.0
    for x in range(1, 8):
        out[node(x, 0), val + 32 + x] = 1.0
    for x in range(8):
        out[160 + x, val + 40 + x] = 1.0
    out[144, val + 32] = 1.0
    for y in range(1, 16):
        row = out[144 + y]
        row[val + y] += 4.0
        row[:128] -= SINE[node(1, y)]
        row[val + line_y(y - 1)] -= 1.0
        row[val + line_y(y + 1)] -= 1.0
    for x in range(1, 8):
        row = out[168 + x]
        row[val + line_x(x)] += 4.0
        row[:128] -= SINE[node(x, 1)]
        row[val + line_x(x - 1)] -= 1.0
        row[val + line_x(x + 1)] -= 1.0
    row = out[168]
    row[val] += 4.0
    row[val + 33] -= 1.0
    row[val + 32] -= 1.0
    row[val + 1] -= 1.0
    values = thirds(out[:, 128:])[0]
    return np.concatenate([left_table(out[:, :128]), values, values, values], axis=1)


def lines_in():
    out = np.zeros((128, 128))
    for g in range(8):
        out[16 * g : 16 * g + 16] = BASIS[16 * g]
    return out


def lines_out():
    out = np.zeros((128, 128))
    for g in range(8):
        out[:, 16 * g : 16 * g + 8] = BASIS[16 * g][:, None]
        out[:, 16 * g + 8 : 16 * g + 16] = BASIS[(16 * g + 16) % 128][:, None]
    return out


SCALE = STEP_SIZE * PEAK_MOMENTUM
ORDER = np.array([8 * j + x for x in range(8) for j in range(16)])


def pack_tables():
    out = np.zeros((992, 768), jnp.bfloat16)
    rights = (BASIS * SCALE, BASIS.T, BASIS, lines_in(), lines_out())
    for k, table in enumerate(rights):
        out[:384, 128 * k : 128 * k + 128] = right_table(table)
    out[384:512, :384] = left_table(SINE)
    out[384:512, 384:] = left_table(BASIS[ORDER].T)
    out[512:640, :384] = left_table(BASIS[ORDER])
    high, middle, low = thirds(source_table())
    out[512:640, 384:672] = np.concatenate([high, high, high, middle, middle, low], axis=1)
    out[640:688, :384] = left_table(reduce_table())
    out[688:864, :528] = expand_table()
    for k, table in enumerate((INVERSE, PLANE_SUM)):
        out[864:992, 384 * k : 384 * k + 384] = left_table(table)
    return out


INVERSE = INNER[:, None] / (np.where(INNER, EIGEN, 1.0)[:, None] + SQUARES[None, :])
PLANE_SUM = SQUARES[:, None] + SQUARES[None, :]
TABLE = pack_tables()
Z_IN, Z_OUT, Y_IN, LINES_IN, LINES_OUT = [(slice(0, 384), slice(128 * k, 128 * k + 128)) for k in range(5)]
MODES = (slice(384, 512), slice(0, 384))
X_IN = (slice(384, 512), slice(384, 768))
X_OUT = (slice(512, 640), slice(0, 384))
SOURCE = (slice(512, 640), slice(384, 672))
REDUCE = (slice(640, 688), slice(0, 384))
EXPAND = (slice(688, 864), slice(0, 384))
EXPAND_LINES = (slice(688, 864), slice(384, 528))


def float_table(table, which, rows=128):
    parts = [
        table[864 : 864 + rows, 384 * which + 128 * k : 384 * which + 128 * k + 128].astype(F32)
        for k in range(3)
    ]
    return (parts[0] + parts[1]) + parts[2]


def parts_of(value):
    high = value.astype(BF16)
    rest = value - high.astype(F32)
    middle = rest.astype(BF16)
    return high, middle, (rest - middle.astype(F32)).astype(BF16)


def products(value, axis, fine):
    high, middle, low = parts_of(value)
    parts = [high, middle, low, high, middle, high] if fine else [high, middle, high]
    return jnp.concatenate(parts, axis=axis)


def chosen(fine):
    return (0, 0, 0, 1, 1, 2) if fine else (0, 0, 1)


def right_dot(value, table, place, fine):
    rows, lanes = place
    parts = [table[rows.start + 128 * k : rows.start + 128 * k + 128, lanes] for k in chosen(fine)]
    return dot(products(value, 1, fine), jnp.concatenate(parts, axis=0))


def left_dot(table, place, pieces, fine):
    rows, lanes = place
    parts = [table[rows, lanes.start + 128 * k : lanes.start + 128 * k + 128] for k in chosen(fine)]
    pieces = [products(piece, 0, fine) for piece in pieces]
    return dot(jnp.concatenate(parts, axis=1), jnp.concatenate(pieces, axis=1))


def swap_blocks(tiles):
    tiles = list(tiles)
    group = lax.broadcasted_iota(jnp.int32, tiles[0].shape, 1) // 16
    for bit in (1, 2, 4):
        upper = (group & bit) != 0
        for i in range(8):
            if i & bit:
                continue
            low, high = tiles[i], tiles[i | bit]
            tiles[i] = jnp.where(upper, pltpu.roll(high, 16 * bit, 1), low)
            tiles[i | bit] = jnp.where(upper, high, pltpu.roll(low, 128 - 16 * bit, 1))
    return tiles


def algebra(mreal, mimag):
    i00, i11, i22 = mimag(0, 0), mimag(1, 1), mimag(2, 2)
    middle = (i00 + i11 + i22) * (1.0 / 3.0)
    return [
        i00 - middle,
        i11 - middle,
        (mreal(0, 1) - mreal(1, 0)) * 0.5,
        (mimag(0, 1) + mimag(1, 0)) * 0.5,
        (mreal(0, 2) - mreal(2, 0)) * 0.5,
        (mimag(0, 2) + mimag(2, 0)) * 0.5,
        (mreal(1, 2) - mreal(2, 1)) * 0.5,
        (mimag(1, 2) + mimag(2, 1)) * 0.5,
    ]


def squares(c):
    third = c[0] + c[1]
    rest = c[2] * c[2] + c[3] * c[3] + c[4] * c[4] + c[5] * c[5] + c[6] * c[6] + c[7] * c[7]
    return c[0] * c[0] + c[1] * c[1] + third * third + 2.0 * rest


def entry(row, col):
    return row * 3 + col


def cross_row(first_re, first_im, second_re, second_im):
    out_re, out_im = [], []
    for k in range(3):
        a, b = (k + 1) % 3, (k + 2) % 3
        out_re.append(
            first_re[a] * second_re[b]
            - first_im[a] * second_im[b]
            - first_re[b] * second_re[a]
            + first_im[b] * second_im[a]
        )
        out_im.append(
            first_re[b] * second_im[a]
            + first_im[b] * second_re[a]
            - first_re[a] * second_im[b]
            - first_im[a] * second_re[b]
        )
    return out_re, out_im


def exponent_rows(c):
    c0, c1, c2, c3, c4, c5, c6, c7 = c
    n01 = c2 * c2 + c3 * c3
    n02 = c4 * c4 + c5 * c5
    n12 = c6 * c6 + c7 * c7
    s00 = 1.0 - 0.5 * (c0 * c0 + n01 + n02)
    s11 = 1.0 - 0.5 * (c1 * c1 + n01 + n12)
    d01 = c0 + c1
    p01r = -(d01 * c3) - (c4 * c6 + c5 * c7)
    p01i = d01 * c2 - (c5 * c6 - c4 * c7)
    p02r = c1 * c5 + (c2 * c6 - c3 * c7)
    p02i = -(c1 * c4) + (c2 * c7 + c3 * c6)
    p12r = -(c2 * c4 + c3 * c5) + c0 * c7
    p12i = -(c2 * c5 - c3 * c4) - c0 * c6
    r0 = [s00, c2 + 0.5 * p01r, c4 + 0.5 * p02r]
    i0 = [c0, c3 + 0.5 * p01i, c5 + 0.5 * p02i]
    r1 = [-c2 + 0.5 * p01r, s11, c6 + 0.5 * p12r]
    i1 = [c3 - 0.5 * p01i, c1, c7 + 0.5 * p12i]
    size = sum(r0[k] * r0[k] + i0[k] * i0[k] for k in range(3))
    scale = lax.rsqrt(size)
    r0 = [v * scale for v in r0]
    i0 = [v * scale for v in i0]
    pr = sum(r0[k] * r1[k] + i0[k] * i1[k] for k in range(3))
    pi = sum(r0[k] * i1[k] - i0[k] * r1[k] for k in range(3))
    r1, i1 = (
        [r1[k] - (pr * r0[k] - pi * i0[k]) for k in range(3)],
        [i1[k] - (pr * i0[k] + pi * r0[k]) for k in range(3)],
    )
    size = sum(r1[k] * r1[k] + i1[k] * i1[k] for k in range(3))
    scale = lax.rsqrt(size)
    r1 = [v * scale for v in r1]
    i1 = [v * scale for v in i1]
    return r0 + r1, i0 + i1


def full_matrix(re6, im6):
    re3, im3 = cross_row(re6[:3], im6[:3], re6[3:], im6[3:])
    return list(re6) + re3 + list(im6) + im3


def times_rows(gre, gim, hre, him):
    out_re, out_im = [], []
    for i in range(2):
        for j in range(3):
            acc_re = acc_im = None
            for k in range(3):
                ar, ai = gre[entry(i, k)], gim[entry(i, k)]
                br, bi = hre[entry(k, j)], him[entry(k, j)]
                pr, pi = ar * br - ai * bi, ar * bi + ai * br
                acc_re = pr if acc_re is None else acc_re + pr
                acc_im = pi if acc_im is None else acc_im + pi
            out_re.append(acc_re)
            out_im.append(acc_im)
    return out_re, out_im


def moved_algebra(g, link, ahead):
    gre, gim = g[:9], g[9:]
    are, aim = ahead[:9], ahead[9:]
    vre, vim = [None] * 9, [None] * 9
    for i in range(2):
        ur = [link(0, i, k) for k in range(3)]
        ui = [link(1, i, k) for k in range(3)]
        for j in range(3):
            br = [are[entry(j, k)] for k in range(3)]
            bi = [aim[entry(j, k)] for k in range(3)]
            vre[entry(i, j)] = (ur[0] * br[0] + ui[0] * bi[0]) + (
                (ur[1] * br[1] + ui[1] * bi[1]) + (ur[2] * br[2] + ui[2] * bi[2])
            )
            vim[entry(i, j)] = (ui[0] * br[0] - ur[0] * bi[0]) + (
                (ui[1] * br[1] - ur[1] * bi[1]) + (ui[2] * br[2] - ur[2] * bi[2])
            )

    vre[6:], vim[6:] = cross_row(vre[:3], vim[:3], vre[3:6], vim[3:6])

    def mreal(i, j):
        return sum(
            gre[entry(i, k)] * vre[entry(k, j)] - gim[entry(i, k)] * vim[entry(k, j)]
            for k in range(3)
        )

    def mimag(i, j):
        return sum(
            gre[entry(i, k)] * vim[entry(k, j)] + gim[entry(i, k)] * vre[entry(k, j)]
            for k in range(3)
        )

    return algebra(mreal, mimag)


PLANE = 18 * 32


def dot(left, right):
    return jnp.dot(left, right, preferred_element_type=F32)


def tile(value, c):
    return value[:, 128 * c : 128 * c + 128]


def encode(spectrum, stride, table, modes, packed, out):
    mode = left_dot(table, MODES, [spectrum[pl.ds(stride * c, 128), :] for c in range(8)], False)
    inverse = float_table(table, 0)
    scaled = []
    for c in range(8):
        scaled.append(inverse * tile(mode, c))
        modes[c] = scaled[c]
    reduced = left_dot(table, REDUCE, scaled, False)
    corner = lax.broadcasted_iota(jnp.int32, (8, 128), 0) == 0
    for c in range(8):
        start = stride * c
        values = tile(reduced, c)
        line_x = values[0:16] + spectrum[pl.ds(start, 16), :]
        line_y = jnp.where(corner, 0.0, spectrum[pl.ds(start, 8, stride=16), :])
        next_x, next_y = values[16:32], values[40:48]
        if stride > 128:
            next_x = next_x + spectrum[pl.ds(start + 128, 16), :]
            next_y = next_y + spectrum[pl.ds(start + 144, 8), :]
        groups = [line_x, next_x, jnp.concatenate([values[32:40] + line_y, next_y], axis=0)]
        for t in range(3):
            packed[pl.ds(128 * t + 16 * c, 16), :] = groups[t]
    for t in range(3):
        out[pl.ds(t, 128, stride=3), :] = packed[pl.ds(128 * t, 128), :].T


def first_kernel(*refs):
    links_hbm, table_hbm, out, modes, edge_x, edge_y, theta, table, face_x, face_y = refs[:10]
    links, prev, sources, packed, sems = refs[10:]

    def plane_copy(x):
        return pltpu.make_async_copy(links_hbm.at[:, x], links.at[:, x], sems.at[x])

    for x in range(8):
        plane_copy(x).start()
    table_copy = pltpu.make_async_copy(table_hbm, table, sems.at[8])
    table_copy.start()
    prev[...] = jnp.zeros_like(prev)
    theta[...] = jnp.zeros_like(theta)
    row = lax.broadcasted_iota(jnp.int32, (16, 128), 0)

    def planes(x, carry):
        plane_copy(x).wait()

        def of(mu):
            return algebra(
                lambda i, j: links[18 * mu + entry(i, j), x],
                lambda i, j: links[18 * mu + 9 + entry(i, j), x],
            )

        ax, ay, az = of(0), of(1), of(2)
        comps = []
        for c in range(8):
            back_y = jnp.where(row == 0, 0.0, pltpu.roll(ay[c], 1, 0))
            value = (prev[c] + back_y + pltpu.roll(az[c], 1, 1)) - ax[c] - ay[c] - az[c]
            prev[c] = ax[c]
            comps.append(value)
            sources[pl.ds(152 * c + 16 * x, 16), :] = value
            sources[pl.ds(152 * c + 144 + x, 1), :] = ay[c][15:16]
        for k in range(12):
            face_y[k, pl.ds(x, 1), :] = links[18 + k % 6 + 9 * (k // 6), x, 15:16, :]
        inner = jnp.where((row > 0) & (x > 0), squares(comps), 0.0)
        theta[...] += inner[:8] + inner[8:]
        return carry

    lax.fori_loop(0, 8, planes, 0)
    for c in range(8):
        sources[pl.ds(152 * c + 128, 16), :] = prev[c]
        edge_x[c] = sources[pl.ds(152 * c, 16), :]
        edge_y[c] = sources[pl.ds(152 * c, 8, stride=16), :]
    for k in range(12):
        face_x[k] = links[k % 6 + 9 * (k // 6), 7]
    table_copy.wait()
    sources[...] = right_dot(sources[...], table, Z_IN, False)
    encode(sources, 152, table, modes, packed, out)


def plane_kernel(own, recv, table, out, work, lines):
    lane = lax.broadcasted_iota(jnp.int32, (16, 128), 1) % 16
    zero = jnp.where(own[0] == 0, -1.0 / (LS * LS), 0.0)
    total = float_table(table, 1)
    work[pl.ds(0, 128), :] = total
    total = total + work[pl.ds(own[0], 1), :][:, 0:1]
    inverse = jnp.where(total > 0.0, 1.0 / jnp.where(total > 0.0, total, 1.0), 0.0)
    shifts = []
    moved = [
        swap_blocks([recv[pl.ds(3 * g + t, 16, stride=24), :] for g in range(8)])
        for t in range(3)
    ]
    for c in range(8):
        third = moved[2][c]
        rolled = pltpu.roll(third, 8, 1)
        first = moved[0][c] + pltpu.roll(moved[1][c], 1, 0) + jnp.where(lane == 0, rolled, 0.0)
        work[pl.ds(16 * c, 16), :] = first
        both = third + rolled
        for x in range(1, 8):
            work[pl.ds(128 * x + 16 * c, 16), :] = jnp.where(lane == x, both, 0.0)
        extra = jnp.sum(jnp.where(lane == 0, third, 0.0), axis=0, keepdims=True)
        shifts.append(jnp.sum(extra, axis=1, keepdims=True) * zero)
    lines[pl.ds(0, 128), :] = right_dot(work[pl.ds(0, 128), :], table, Y_IN, False)
    lines[pl.ds(128, 896), :] = right_dot(work[pl.ds(128, 896), :], table, LINES_IN, False)
    blocks = [
        jnp.concatenate([lines[pl.ds(128 * x + 16 * c, 16), :] for x in range(8)], axis=0)
        for c in range(8)
    ]
    spectrum = left_dot(table, X_IN, blocks, False)
    spectrum = left_dot(table, X_OUT, [tile(spectrum, c) * inverse for c in range(8)], True)
    spectrum = [tile(spectrum, c) for c in range(8)]
    at_lines = right_dot(jnp.concatenate(spectrum, axis=0), table, LINES_OUT, True)
    first = jnp.concatenate([part[:16] for part in spectrum], axis=0)
    first = right_dot(first, table, Z_OUT, True)
    groups = [[], [], []]
    for c in range(8):
        own_line = first[16 * c : 16 * c + 16] + shifts[c]
        groups[0].append(own_line)
        groups[1].append(pltpu.roll(own_line, 15, 0))
        parts = [at_lines[128 * c + 16 * x : 128 * c + 16 * x + 16] for x in range(8)]
        third = jnp.where(lane == 0, pltpu.roll(parts[7], 1, 0), parts[0])
        for x in range(1, 8):
            third = jnp.where((lane == x) | (lane == 8 + x), parts[x], third)
        groups[2].append(third + shifts[c])
    for t in range(3):
        tiles = swap_blocks(groups[t])
        for g in range(8):
            out[pl.ds(3 * g + t, 16, stride=24), :] = tiles[g]


def decode(recv, modes, table, packed, comps_in):
    for t in range(3):
        packed[pl.ds(128 * t, 128), :] = recv[pl.ds(t, 128, stride=3), :].T
    mass = float_table(table, 1, 16)[0:1]
    inverse = float_table(table, 0)
    values = [
        jnp.concatenate([packed[pl.ds(128 * t + 16 * c, 16), :] for t in range(3)], axis=0)
        for c in range(8)
    ]
    mode = dot(table[SOURCE], jnp.concatenate([products(value, 0, True) for value in values], axis=1))
    stacks = []
    for c in range(8):
        own = modes[c] + inverse * tile(mode, c)
        stacks.append(own)
    sites = left_dot(table, EXPAND, stacks, True)
    exact = [jnp.concatenate(parts_of(value), axis=0) for value in values]
    sites = sites + dot(table[EXPAND_LINES], jnp.concatenate(exact, axis=1))
    row = lax.broadcasted_iota(jnp.int32, (16, 128), 0)
    parts = []
    for c in range(8):
        part, value = tile(sites, c), values[c]
        behind = part[144:160] + mass * jnp.where(row == 0, 0.0, value[0:16])
        below = part[168:176] + mass * jnp.where(row[:8] == 0, value[0:8], value[32:40])
        parts.append(jnp.concatenate([part[:144], behind, part[160:168], below], axis=0))
    comps_in[...] = right_dot(jnp.concatenate(parts, axis=0), table, Z_OUT, True)


def make(c, before=None):
    re6, im6 = exponent_rows(c)
    if before is not None:
        re6, im6 = times_rows(re6, im6, before[:9], before[9:])
    return full_matrix(re6, im6)


def start_links(links_hbm, links, sems):
    def plane_copy(x):
        return pltpu.make_async_copy(links_hbm.at[:, x], links.at[:, x], sems.at[x])

    for x in range(8):
        plane_copy(x).start()
    return plane_copy


def moved_divergence(links, plane_copy, gs, ay, prev, emit):
    def sites(x, carry):
        plane_copy(x).wait()
        base = (x + 1) * PLANE
        for half in range(2):
            rows = pl.ds(8 * half, 8)
            start = 8 * half + 8
            total = [None] * 8

            def link_of(mu):
                return lambda p, i, j: links[18 * mu + 9 * p + entry(i, j), x, rows, :]

            g = [gs[pl.ds(base + 32 * k + start, 8), :] for k in range(18)]
            ahead = [gs[pl.ds(base + PLANE + 32 * k + start, 8), :] for k in range(18)]
            a = moved_algebra(g, link_of(0), ahead)
            for c in range(8):
                total[c] = prev[c, rows, :] - a[c]
                prev[c, rows, :] = a[c]
            ahead = [gs[pl.ds(base + 32 * k + start + 1, 8), :] for k in range(18)]
            a = moved_algebra(g, link_of(1), ahead)
            for c in range(8):
                ay[pl.ds(x * 192 + 24 * c + start, 8), :] = a[c]
            for c in range(8):
                total[c] = total[c] + (ay[pl.ds(x * 192 + 24 * c + start - 1, 8), :] - a[c])
            top = [v[7:8] for v in a]
            ahead = [pltpu.roll(v, 127, 1) for v in g]
            a = moved_algebra(g, link_of(2), ahead)
            for c in range(8):
                total[c] = total[c] + (pltpu.roll(a[c], 1, 1) - a[c])
            emit(x, half, total, top)
        return carry

    lax.fori_loop(0, 8, sites, 0)


def update_kernel(*refs):
    recv, modes, links_hbm, table = refs[:4]
    out, modes_out, edge_x, edge_y, theta, gout, gout_y, raw_x, raw_y = refs[4:13]
    links, sems, packed, comps_in, gs, ay, prev, sources = refs[13:]
    plane_copy = start_links(links_hbm, links, sems)
    decode(recv, modes, table, packed, comps_in)
    for c in range(8):
        raw_x[c] = comps_in[pl.ds(176 * c + 144, 16), :]
        raw_y[c] = comps_in[pl.ds(176 * c + 168, 8), :]

    def plane(index, first_row):
        for half in range(2):
            g = make([comps_in[pl.ds(first_row(c) + 8 * half, 8), :] for c in range(8)])
            for k in range(18):
                gs[pl.ds(index * PLANE + 32 * k + 8 * half + 8, 8), :] = g[k]
                gout[pl.ds((index - 1) * 288 + 16 * k + 8 * half, 8), :] = g[k]

    def inner(x, carry):
        plane(x + 1, lambda c: 176 * c + 16 * x)
        return carry

    lax.fori_loop(0, 8, inner, 0)
    plane(9, lambda c: 176 * c + 128)
    g = make([comps_in[pl.ds(176 * c + 160, 8), :] for c in range(8)])
    for k in range(18):
        gout_y[k] = g[k]
        gs[pl.ds(PLANE + 32 * k + 24, 8, stride=PLANE), :] = g[k]

    prev[...] = jnp.zeros_like(prev)
    theta[...] = jnp.zeros_like(theta)
    for c in range(8):
        ay[pl.ds(24 * c + 7, 8, stride=192), :] = jnp.zeros((8, 128), F32)
    row = lax.broadcasted_iota(jnp.int32, (8, 128), 0)

    def emit(x, half, total, top):
        for c in range(8):
            sources[pl.ds(152 * c + 16 * x + 8 * half, 8), :] = total[c]
            if half == 1:
                sources[pl.ds(152 * c + 144 + x, 1), :] = top[c]
        theta[...] += jnp.where((x > 0) & (row + half > 0), squares(total), 0.0)

    moved_divergence(links, plane_copy, gs, ay, prev, emit)
    for c in range(8):
        sources[pl.ds(152 * c + 128, 16), :] = prev[c]
        edge_x[c] = sources[pl.ds(152 * c, 16), :]
        edge_y[c] = sources[pl.ds(152 * c, 8, stride=16), :]
    sources[...] = right_dot(sources[...], table, Z_IN, False)
    encode(sources, 152, table, modes_out, packed, out)


def whole_lines(line_x, line_y, add_x, add_y):
    top = lax.broadcasted_iota(jnp.int32, (16, 128), 0) == 0
    out_x, out_y = [], []
    for c in range(8):
        out_x.append(line_x[c] + add_x[c] + jnp.where(top, add_y[c][0:1], 0.0))
        out_y.append(line_y[c] + add_y[c] + jnp.where(top[:8], add_x[c][0:1], 0.0))
    sq = squares(out_x)
    return out_x, out_y, sq[:8] + sq[8:] + jnp.where(top[:8], 0.0, squares(out_y))


def last_kernel(*refs):
    recv, modes, links_hbm, table, line0_x, line0_y, line1_x, line1_y, raw_x, raw_y = refs[:10]
    face_x, face_y, theta0, theta1, prior, prior_y, div_hbm, gauge_hbm, theta = refs[10:19]
    links, sems, packed, comps_in, gs, behind, below, ay, prev, acc, div, gauge, out_sems = refs[19:]
    plane_copy = start_links(links_hbm, links, sems)
    decode(recv, modes, table, packed, comps_in)
    row = lax.broadcasted_iota(jnp.int32, (16, 128), 0)

    face = full_matrix([face_x[k] for k in range(6)], [face_x[6 + k] for k in range(6)])
    add_x = algebra(lambda i, j: face[entry(i, j)], lambda i, j: face[9 + entry(i, j)])
    face = full_matrix([face_y[k] for k in range(6)], [face_y[6 + k] for k in range(6)])
    add_y = algebra(lambda i, j: face[entry(i, j)], lambda i, j: face[9 + entry(i, j)])
    whole_x, whole_y, extra0 = whole_lines(line0_x, line0_y, add_x, add_y)
    for half in range(2):
        rows = pl.ds(8 * half, 8)
        part = slice(8 * half, 8 * half + 8)
        taken = [jnp.where(row == 0, 0.0, SCALE * whole_x[c])[part] for c in range(8)]
        g = make([raw_x[c, rows, :] - taken[c] for c in range(8)])
        for k in range(18):
            behind[k, rows, :] = g[k]
        ahead = [prior[pl.ds(16 * k + 8 * half, 8), :] for k in range(18)]
        edge = moved_algebra(g, lambda p, i, j: face_x[6 * p + entry(i, j), rows, :], ahead)
        for c in range(8):
            prev[c, rows, :] = edge[c]
    g = make([raw_y[c] - SCALE * whole_y[c] for c in range(8)])
    for k in range(18):
        below[k] = g[k]
    ahead = [prior[pl.ds(16 * k, 8, stride=288), :] for k in range(18)]
    edge = moved_algebra(g, lambda p, i, j: face_y[6 * p + entry(i, j)], ahead)
    whole_x, whole_y, extra1 = whole_lines(line1_x, line1_y, prev, edge)

    for c in range(8):
        rows = pl.ds(176 * c + 144, 16)
        comps_in[rows, :] = comps_in[rows, :] - jnp.where(row == 0, 0.0, SCALE * whole_x[c])
        rows = pl.ds(176 * c + 168, 8)
        comps_in[rows, :] = comps_in[rows, :] - SCALE * whole_y[c]

    def plane(index, first_row, before):
        for half in range(2):
            rows = pl.ds(8 * half, 8)
            g = make([comps_in[pl.ds(first_row(c) + 8 * half, 8), :] for c in range(8)], before(half))
            for k in range(18):
                gs[pl.ds(index * PLANE + 32 * k + 8 * half + 8, 8), :] = g[k]
            if not isinstance(index, int):
                for p in range(2):
                    for i in range(2):
                        for j in range(3):
                            gauge[p, i, j, index - 1, rows, :] = g[9 * p + entry(i, j)]

    def before_at(index):
        return lambda half: [
            prior[pl.ds((index - 1) * 288 + 16 * k + 8 * half, 8), :] for k in range(18)
        ]

    def inner(x, carry):
        plane(x + 1, lambda c: 176 * c + 16 * x, before_at(x + 1))
        return carry

    lax.fori_loop(0, 8, inner, 0)
    gauge_copy = pltpu.make_async_copy(gauge, gauge_hbm, out_sems.at[8])
    gauge_copy.start()

    def div_copy(x):
        return pltpu.make_async_copy(div.at[:, x], div_hbm.at[:, x], out_sems.at[x])

    plane(
        0,
        lambda c: 176 * c + 144,
        lambda half: [behind[k, pl.ds(8 * half, 8), :] for k in range(18)],
    )
    plane(9, lambda c: 176 * c + 128, before_at(9))
    g = make(
        [comps_in[pl.ds(176 * c + 160, 8), :] for c in range(8)], [prior_y[k] for k in range(18)]
    )
    for k in range(18):
        gs[pl.ds(PLANE + 32 * k + 24, 8, stride=PLANE), :] = g[k]

    g = make([comps_in[pl.ds(176 * c + 168, 8), :] for c in range(8)], [below[k] for k in range(18)])
    ahead = [gs[pl.ds(PLANE + 32 * k + 8, 8, stride=PLANE), :] for k in range(18)]
    edge = moved_algebra(g, lambda p, i, j: face_y[6 * p + entry(i, j)], ahead)
    for c in range(8):
        ay[pl.ds(24 * c + 7, 8, stride=192), :] = edge[c]
    for half in range(2):
        rows = pl.ds(8 * half, 8)
        start = 8 * half + 8
        g = [gs[pl.ds(32 * k + start, 8), :] for k in range(18)]
        ahead = [gs[pl.ds(PLANE + 32 * k + start, 8), :] for k in range(18)]
        edge = moved_algebra(g, lambda p, i, j: face_x[6 * p + entry(i, j), rows, :], ahead)
        for c in range(8):
            prev[c, rows, :] = edge[c]

    acc[...] = jnp.zeros_like(acc)

    def emit(x, half, total, top):
        for c in range(8):
            div[c, x, pl.ds(8 * half, 8), :] = total[c]
        acc[...] += squares(total)
        if half == 1:
            div_copy(x).start()

    moved_divergence(links, plane_copy, gs, ay, prev, emit)
    lane = lax.broadcasted_iota(jnp.int32, (1, 128), 1)
    sums = jnp.zeros((1, 128), F32)
    for k, part in enumerate((theta0[...] + extra0, theta1[...] + extra1, acc[...])):
        sums = sums + jnp.where(lane == k, jnp.sum(part), 0.0)
    theta[...] = jnp.broadcast_to(sums * (1.0 / (3.0 * LS * LS * NZ)), (128, 128))
    gauge_copy.wait()
    for x in range(8):
        div_copy(x).wait()


def struct(*shape):
    return jax.ShapeDtypeStruct(shape, F32)


def vmem(*shape):
    return pltpu.VMEM(shape, F32)


def whole():
    return pl.BlockSpec(memory_space=pltpu.VMEM)


def in_hbm(value):
    return pltpu.with_memory_space_constraint(value, pltpu.HBM)


def params(size):
    return pltpu.CompilerParams(vmem_limit_bytes=size * MEGA)


EDGES = [(8, 16, 128), (8, 8, 128)]


def first_call(links, table):
    shapes = [struct(384, 128), struct(8, 128, 128)] + [struct(*e) for e in EDGES] + [struct(8, 128)]
    shapes += [jax.ShapeDtypeStruct(table.shape, table.dtype), struct(12, 16, 128), struct(12, 8, 128)]
    return pl.pallas_call(
        first_kernel,
        in_specs=[pl.BlockSpec(memory_space=pl.ANY)] * 2,
        out_specs=[whole()] * len(shapes),
        out_shape=shapes,
        scratch_shapes=[
            vmem(54, 8, 16, 128),
            vmem(8, 16, 128),
            vmem(8 * 152, 128),
            vmem(384, 128),
            pltpu.SemaphoreType.DMA((9,)),
        ],
        compiler_params=params(32),
        name="first_divergence",
    )(in_hbm(links), in_hbm(table))


def plane_call(own, recv, table):
    return pl.pallas_call(
        plane_kernel,
        in_specs=[pl.BlockSpec(memory_space=pltpu.SMEM)] + [whole()] * 2,
        out_specs=whole(),
        out_shape=struct(384, 128),
        scratch_shapes=[vmem(1024, 128), vmem(1024, 128)],
        compiler_params=params(32),
        name="plane_solve",
    )(own, recv, table)


def update_call(kernel, operands, shapes, extra, name, copied=0):
    scratch = [
        vmem(54, 8, 16, 128),
        pltpu.SemaphoreType.DMA((8,)),
        vmem(384, 128),
        vmem(8 * 176, 128),
        vmem(10 * PLANE, 128),
    ]
    return pl.pallas_call(
        kernel,
        in_specs=[pl.BlockSpec(memory_space=pl.ANY) if k == 2 else whole() for k in range(len(operands))],
        out_specs=[pl.BlockSpec(memory_space=pl.ANY)] * copied + [whole()] * (len(shapes) - copied),
        out_shape=shapes,
        scratch_shapes=scratch + extra,
        compiler_params=params(32),
        name=name,
    )(*operands)


def shifted(value, axis, steps):
    count = lax.axis_size(axis)
    pairs = [(source, (source + steps) % count) for source in range(count)]
    return lax.ppermute(value, axis, pairs)


def exchange(value):
    rows = value.reshape(128, 1, value.size // 128)
    rows = lax.all_to_all(rows, ("gx", "gy"), split_axis=0, concat_axis=0, tiled=True)
    return rows.reshape(value.shape)


def per_device(links):
    flat = links.reshape(54, 8, 16, 128)
    own = (lax.axis_index("gx") * 8 + lax.axis_index("gy")).astype(jnp.int32).reshape(1)
    table = jnp.asarray(TABLE)
    packed, modes, edge_x, edge_y, theta, table, face_x, face_y = first_call(flat, table)
    face_x = shifted(face_x, "gx", 1)
    face_y = shifted(face_y, "gy", 1)
    packed, own = lax.optimization_barrier((packed, own))
    values = exchange(plane_call(own, exchange(packed), table))
    edges = [struct(*e) for e in EDGES]
    shapes = [struct(384, 128), struct(8, 128, 128)] + edges + [struct(8, 128)]
    shapes += [struct(9 * 288, 128), struct(18, 8, 128)] + edges
    packed, modes, edge1_x, edge1_y, theta1, prior, prior_y, raw_x, raw_y = update_call(
        update_kernel,
        [values, modes, in_hbm(flat), table],
        shapes,
        [vmem(8 * 192, 128), vmem(8, 16, 128), vmem(8 * 152, 128)],
        "update",
    )
    packed, face_x, face_y = lax.optimization_barrier((packed, face_x, face_y))
    values = exchange(plane_call(own, exchange(packed), table))
    operands = [values, modes, in_hbm(flat), table, edge_x, edge_y, edge1_x, edge1_y, raw_x, raw_y]
    operands += [face_x, face_y, theta, theta1, prior, prior_y]
    div, gauge, sums = update_call(
        last_kernel,
        operands,
        [struct(8, 8, 16, 128), struct(2, 2, 3, 8, 16, 128), struct(128, 128)],
        [vmem(18, 16, 128), vmem(18, 8, 128), vmem(8 * 192, 128), vmem(8, 16, 128), vmem(8, 128)]
        + [vmem(8, 8, 16, 128), vmem(2, 2, 3, 8, 16, 128), pltpu.SemaphoreType.DMA((9,))],
        "last_update",
        2,
    )
    return (gauge, div, jnp.sum(exchange(sums)[:, :3], axis=0))


def solution(mesh):
    in_specs = (P(None, None, None, None, "gx", "gy", "ta"),)
    out_specs = (P(None, None, None, "gx", "gy", "ta"), P(None, "gx", "gy", "ta"), P("ta"))
    return jax.shard_map(
        per_device, mesh=mesh, in_specs=in_specs, out_specs=out_specs, check_vma=False
    )
```

```python
import math

import jax
import jax.numpy as jnp
import numpy as np
from jax import lax
from jax.experimental import pallas as pl
from jax.experimental.pallas import tpu as pltpu
from jax.sharding import PartitionSpec as P

LS = 128
NZ = 128
STEP_SIZE = 0.08
PEAK_MOMENTUM = 12.0
F32 = jnp.float32
BF16 = jnp.bfloat16
MEGA = 1024 * 1024


def real_basis(length):
    site = np.arange(length)[:, None]
    freq = np.arange(length)
    freq = np.where(freq <= length // 2, freq, freq - length // 2)
    phase = 2.0 * np.pi * ((site * freq[None, :]) % length) / length
    index = np.arange(length)[None, :]
    basis = np.where(index <= length // 2, np.cos(phase), np.sin(phase)) * np.sqrt(2.0 / length)
    basis[:, 0] = 1.0 / np.sqrt(length)
    basis[:, length // 2] = np.cos(np.pi * np.arange(length)) / np.sqrt(length)
    return basis, freq


def thirds(table):
    rest, out = table.astype(np.float32).astype(np.float64), []
    for _ in range(3):
        piece = rest.astype(np.float32).astype(jnp.bfloat16)
        out.append(piece)
        rest = rest - piece.astype(np.float64)
    return out


def right_table(table):
    return np.concatenate(thirds(table), axis=0)


def left_table(table):
    return np.concatenate(thirds(table), axis=1)


def sine_table():
    x, y = np.arange(8), np.arange(16)
    sx = np.sin(np.pi * np.outer(x, x) / 8.0) * np.sqrt(2.0 / 8.0)
    sy = np.sin(np.pi * np.outer(y, y) / 16.0) * np.sqrt(2.0 / 16.0)
    table = np.kron(sx, sy)
    keep = np.kron(x > 0, y > 0)
    table = table * np.outer(keep, keep)
    eigen = (4.0 * np.sin(np.pi * x / 16.0) ** 2)[:, None] + (4.0 * np.sin(np.pi * y / 32.0) ** 2)[None, :]
    return table, eigen.reshape(128), keep


BASIS, FREQ = real_basis(128)
SQUARES = 4.0 * np.sin(np.pi * FREQ / 128.0) ** 2
SINE, EIGEN, INNER = sine_table()


def node(x, y):
    return 16 * x + y


def reduce_table():
    out = np.zeros((48, 128))
    for y in range(1, 16):
        out[y] = SINE[node(1, y)]
        out[16 + y] = SINE[node(7, y)]
    out[32] = SINE[INNER].sum(0)
    for x in range(1, 8):
        out[32 + x] = SINE[node(x, 1)]
        out[40 + x] = SINE[node(x, 15)]
    return out


def source_table():
    out = np.zeros((128, 48))
    for y in range(1, 16):
        out[:, y] = SINE[node(1, y)]
        out[:, 16 + y] = SINE[node(7, y)]
    for x in range(1, 8):
        out[:, 32 + x] = SINE[node(x, 1)]
        out[:, 40 + x] = SINE[node(x, 15)]
    return out


def expand_table():
    out = np.zeros((176, 176))
    val = 128

    def line_x(x):
        return 0 if x == 0 else (16 if x == 8 else 32 + x)

    def line_y(y):
        return 40 if y == 16 else y

    for x in range(1, 8):
        for y in range(1, 16):
            out[node(x, y), :128] = SINE[node(x, y)]
    for y in range(16):
        out[node(0, y), val + y] = 1.0
        out[128 + y, val + 16 + y] = 1.0
    for x in range(1, 8):
        out[node(x, 0), val + 32 + x] = 1.0
    for x in range(8):
        out[160 + x, val + 40 + x] = 1.0
    out[144, val + 32] = 1.0
    for y in range(1, 16):
        row = out[144 + y]
        row[val + y] += 4.0
        row[:128] -= SINE[node(1, y)]
        row[val + line_y(y - 1)] -= 1.0
        row[val + line_y(y + 1)] -= 1.0
    for x in range(1, 8):
        row = out[168 + x]
        row[val + line_x(x)] += 4.0
        row[:128] -= SINE[node(x, 1)]
        row[val + line_x(x - 1)] -= 1.0
        row[val + line_x(x + 1)] -= 1.0
    row = out[168]
    row[val] += 4.0
    row[val + 33] -= 1.0
    row[val + 32] -= 1.0
    row[val + 1] -= 1.0
    values = thirds(out[:, 128:])[0]
    return np.concatenate([left_table(out[:, :128]), values, values, values], axis=1)


def lines_in():
    out = np.zeros((128, 128))
    for g in range(8):
        out[16 * g : 16 * g + 16] = BASIS[16 * g]
    return out


def lines_out():
    out = np.zeros((128, 128))
    for g in range(8):
        out[:, 16 * g : 16 * g + 8] = BASIS[16 * g][:, None]
        out[:, 16 * g + 8 : 16 * g + 16] = BASIS[(16 * g + 16) % 128][:, None]
    return out


SCALE = STEP_SIZE * PEAK_MOMENTUM
ORDER = np.array([8 * j + x for x in range(8) for j in range(16)])


def pack_tables():
    out = np.zeros((992, 768), jnp.bfloat16)
    rights = (BASIS * SCALE, BASIS.T, BASIS, lines_in(), lines_out())
    for k, table in enumerate(rights):
        out[:384, 128 * k : 128 * k + 128] = right_table(table)
    out[384:512, :384] = left_table(SINE)
    out[384:512, 384:] = left_table(BASIS[ORDER].T)
    out[512:640, :384] = left_table(BASIS[ORDER])
    high, middle, low = thirds(source_table())
    out[512:640, 384:672] = np.concatenate([high, high, high, middle, middle, low], axis=1)
    out[640:688, :384] = left_table(reduce_table())
    out[688:864, :528] = expand_table()
    for k, table in enumerate((INVERSE, PLANE_SUM)):
        out[864:992, 384 * k : 384 * k + 384] = left_table(table)
    return out


INVERSE = INNER[:, None] / (np.where(INNER, EIGEN, 1.0)[:, None] + SQUARES[None, :])
PLANE_SUM = SQUARES[:, None] + SQUARES[None, :]
TABLE = pack_tables()
Z_IN, Z_OUT, Y_IN, LINES_IN, LINES_OUT = [(slice(0, 384), slice(128 * k, 128 * k + 128)) for k in range(5)]
MODES = (slice(384, 512), slice(0, 384))
X_IN = (slice(384, 512), slice(384, 768))
X_OUT = (slice(512, 640), slice(0, 384))
SOURCE = (slice(512, 640), slice(384, 672))
REDUCE = (slice(640, 688), slice(0, 384))
EXPAND = (slice(688, 864), slice(0, 384))
EXPAND_LINES = (slice(688, 864), slice(384, 528))


def float_table(table, which, rows=128):
    parts = [
        table[864 : 864 + rows, 384 * which + 128 * k : 384 * which + 128 * k + 128].astype(F32)
        for k in range(3)
    ]
    return (parts[0] + parts[1]) + parts[2]


def parts_of(value):
    high = value.astype(BF16)
    rest = value - high.astype(F32)
    middle = rest.astype(BF16)
    return high, middle, (rest - middle.astype(F32)).astype(BF16)


def products(value, axis, fine):
    high, middle, low = parts_of(value)
    parts = [high, middle, low, high, middle, high] if fine else [high, middle, high]
    return jnp.concatenate(parts, axis=axis)


def chosen(fine):
    return (0, 0, 0, 1, 1, 2) if fine else (0, 0, 1)


def right_dot(value, table, place, fine):
    rows, lanes = place
    parts = [table[rows.start + 128 * k : rows.start + 128 * k + 128, lanes] for k in chosen(fine)]
    return dot(products(value, 1, fine), jnp.concatenate(parts, axis=0))


def left_dot(table, place, pieces, fine):
    rows, lanes = place
    parts = [table[rows, lanes.start + 128 * k : lanes.start + 128 * k + 128] for k in chosen(fine)]
    pieces = [products(piece, 0, fine) for piece in pieces]
    return dot(jnp.concatenate(parts, axis=1), jnp.concatenate(pieces, axis=1))


def swap_blocks(tiles):
    tiles = list(tiles)
    group = lax.broadcasted_iota(jnp.int32, tiles[0].shape, 1) // 16
    for bit in (1, 2, 4):
        upper = (group & bit) != 0
        for i in range(8):
            if i & bit:
                continue
            low, high = tiles[i], tiles[i | bit]
            tiles[i] = jnp.where(upper, pltpu.roll(high, 16 * bit, 1), low)
            tiles[i | bit] = jnp.where(upper, high, pltpu.roll(low, 128 - 16 * bit, 1))
    return tiles


def algebra(mreal, mimag):
    i00, i11, i22 = mimag(0, 0), mimag(1, 1), mimag(2, 2)
    middle = (i00 + i11 + i22) * (1.0 / 3.0)
    return [
        i00 - middle,
        i11 - middle,
        (mreal(0, 1) - mreal(1, 0)) * 0.5,
        (mimag(0, 1) + mimag(1, 0)) * 0.5,
        (mreal(0, 2) - mreal(2, 0)) * 0.5,
        (mimag(0, 2) + mimag(2, 0)) * 0.5,
        (mreal(1, 2) - mreal(2, 1)) * 0.5,
        (mimag(1, 2) + mimag(2, 1)) * 0.5,
    ]


def squares(c):
    third = c[0] + c[1]
    rest = c[2] * c[2] + c[3] * c[3] + c[4] * c[4] + c[5] * c[5] + c[6] * c[6] + c[7] * c[7]
    return c[0] * c[0] + c[1] * c[1] + third * third + 2.0 * rest


def entry(row, col):
    return row * 3 + col


def cross_row(first_re, first_im, second_re, second_im):
    out_re, out_im = [], []
    for k in range(3):
        a, b = (k + 1) % 3, (k + 2) % 3
        out_re.append(
            first_re[a] * second_re[b]
            - first_im[a] * second_im[b]
            - first_re[b] * second_re[a]
            + first_im[b] * second_im[a]
        )
        out_im.append(
            first_re[b] * second_im[a]
            + first_im[b] * second_re[a]
            - first_re[a] * second_im[b]
            - first_im[a] * second_re[b]
        )
    return out_re, out_im


def exponent_rows(c):
    c0, c1, c2, c3, c4, c5, c6, c7 = c
    n01 = c2 * c2 + c3 * c3
    n02 = c4 * c4 + c5 * c5
    n12 = c6 * c6 + c7 * c7
    s00 = 1.0 - 0.5 * (c0 * c0 + n01 + n02)
    s11 = 1.0 - 0.5 * (c1 * c1 + n01 + n12)
    d01 = c0 + c1
    p01r = -(d01 * c3) - (c4 * c6 + c5 * c7)
    p01i = d01 * c2 - (c5 * c6 - c4 * c7)
    p02r = c1 * c5 + (c2 * c6 - c3 * c7)
    p02i = -(c1 * c4) + (c2 * c7 + c3 * c6)
    p12r = -(c2 * c4 + c3 * c5) + c0 * c7
    p12i = -(c2 * c5 - c3 * c4) - c0 * c6
    r0 = [s00, c2 + 0.5 * p01r, c4 + 0.5 * p02r]
    i0 = [c0, c3 + 0.5 * p01i, c5 + 0.5 * p02i]
    r1 = [-c2 + 0.5 * p01r, s11, c6 + 0.5 * p12r]
    i1 = [c3 - 0.5 * p01i, c1, c7 + 0.5 * p12i]
    size = sum(r0[k] * r0[k] + i0[k] * i0[k] for k in range(3))
    scale = lax.rsqrt(size)
    r0 = [v * scale for v in r0]
    i0 = [v * scale for v in i0]
    pr = sum(r0[k] * r1[k] + i0[k] * i1[k] for k in range(3))
    pi = sum(r0[k] * i1[k] - i0[k] * r1[k] for k in range(3))
    r1, i1 = (
        [r1[k] - (pr * r0[k] - pi * i0[k]) for k in range(3)],
        [i1[k] - (pr * i0[k] + pi * r0[k]) for k in range(3)],
    )
    size = sum(r1[k] * r1[k] + i1[k] * i1[k] for k in range(3))
    scale = lax.rsqrt(size)
    r1 = [v * scale for v in r1]
    i1 = [v * scale for v in i1]
    return r0 + r1, i0 + i1


def full_matrix(re6, im6):
    re3, im3 = cross_row(re6[:3], im6[:3], re6[3:], im6[3:])
    return list(re6) + re3 + list(im6) + im3


def times_rows(gre, gim, hre, him):
    out_re, out_im = [], []
    for i in range(2):
        for j in range(3):
            acc_re = acc_im = None
            for k in range(3):
                ar, ai = gre[entry(i, k)], gim[entry(i, k)]
                br, bi = hre[entry(k, j)], him[entry(k, j)]
                pr, pi = ar * br - ai * bi, ar * bi + ai * br
                acc_re = pr if acc_re is None else acc_re + pr
                acc_im = pi if acc_im is None else acc_im + pi
            out_re.append(acc_re)
            out_im.append(acc_im)
    return out_re, out_im


def moved_algebra(g, link, ahead):
    gre, gim = g[:9], g[9:]
    are, aim = ahead[:9], ahead[9:]
    vre, vim = [None] * 9, [None] * 9
    for i in range(2):
        ur = [link(0, i, k) for k in range(3)]
        ui = [link(1, i, k) for k in range(3)]
        for j in range(3):
            br = [are[entry(j, k)] for k in range(3)]
            bi = [aim[entry(j, k)] for k in range(3)]
            vre[entry(i, j)] = (ur[0] * br[0] + ui[0] * bi[0]) + (
                (ur[1] * br[1] + ui[1] * bi[1]) + (ur[2] * br[2] + ui[2] * bi[2])
            )
            vim[entry(i, j)] = (ui[0] * br[0] - ur[0] * bi[0]) + (
                (ui[1] * br[1] - ur[1] * bi[1]) + (ui[2] * br[2] - ur[2] * bi[2])
            )

    vre[6:], vim[6:] = cross_row(vre[:3], vim[:3], vre[3:6], vim[3:6])

    def mreal(i, j):
        return sum(
            gre[entry(i, k)] * vre[entry(k, j)] - gim[entry(i, k)] * vim[entry(k, j)]
            for k in range(3)
        )

    def mimag(i, j):
        return sum(
            gre[entry(i, k)] * vim[entry(k, j)] + gim[entry(i, k)] * vre[entry(k, j)]
            for k in range(3)
        )

    return algebra(mreal, mimag)


PLANE = 18 * 32


def dot(left, right):
    return jnp.dot(left, right, preferred_element_type=F32)


def tile(value, c):
    return value[:, 128 * c : 128 * c + 128]


def encode(spectrum, stride, table, modes, packed, out):
    mode = left_dot(table, MODES, [spectrum[pl.ds(stride * c, 128), :] for c in range(8)], False)
    inverse = float_table(table, 0)
    scaled = []
    for c in range(8):
        scaled.append(inverse * tile(mode, c))
        modes[c] = scaled[c]
    reduced = left_dot(table, REDUCE, scaled, False)
    corner = lax.broadcasted_iota(jnp.int32, (8, 128), 0) == 0
    for c in range(8):
        start = stride * c
        values = tile(reduced, c)
        line_x = values[0:16] + spectrum[pl.ds(start, 16), :]
        line_y = jnp.where(corner, 0.0, spectrum[pl.ds(start, 8, stride=16), :])
        next_x, next_y = values[16:32], values[40:48]
        if stride > 128:
            next_x = next_x + spectrum[pl.ds(start + 128, 16), :]
            next_y = next_y + spectrum[pl.ds(start + 144, 8), :]
        groups = [line_x, next_x, jnp.concatenate([values[32:40] + line_y, next_y], axis=0)]
        for t in range(3):
            packed[pl.ds(128 * t + 16 * c, 16), :] = groups[t]
    for t in range(3):
        out[pl.ds(t, 128, stride=3), :] = packed[pl.ds(128 * t, 128), :].T


def first_kernel(*refs):
    links_hbm, table_hbm, out, modes, edge_x, edge_y, theta, table, face_x, face_y = refs[:10]
    links, prev, sources, packed, sems = refs[10:]

    def plane_copy(x):
        return pltpu.make_async_copy(links_hbm.at[:, x], links.at[:, x], sems.at[x])

    for x in range(8):
        plane_copy(x).start()
    table_copy = pltpu.make_async_copy(table_hbm, table, sems.at[8])
    table_copy.start()
    prev[...] = jnp.zeros_like(prev)
    theta[...] = jnp.zeros_like(theta)
    row = lax.broadcasted_iota(jnp.int32, (16, 128), 0)

    def planes(x, carry):
        plane_copy(x).wait()

        def of(mu):
            return algebra(
                lambda i, j: links[18 * mu + entry(i, j), x],
                lambda i, j: links[18 * mu + 9 + entry(i, j), x],
            )

        ax, ay, az = of(0), of(1), of(2)
        comps = []
        for c in range(8):
            back_y = jnp.where(row == 0, 0.0, pltpu.roll(ay[c], 1, 0))
            value = (prev[c] + back_y + pltpu.roll(az[c], 1, 1)) - ax[c] - ay[c] - az[c]
            prev[c] = ax[c]
            comps.append(value)
            sources[pl.ds(152 * c + 16 * x, 16), :] = value
            sources[pl.ds(152 * c + 144 + x, 1), :] = ay[c][15:16]
        for k in range(12):
            face_y[k, pl.ds(x, 1), :] = links[18 + k % 6 + 9 * (k // 6), x, 15:16, :]
        inner = jnp.where((row > 0) & (x > 0), squares(comps), 0.0)
        theta[...] += inner[:8] + inner[8:]
        return carry

    lax.fori_loop(0, 8, planes, 0)
    for c in range(8):
        sources[pl.ds(152 * c + 128, 16), :] = prev[c]
        edge_x[c] = sources[pl.ds(152 * c, 16), :]
        edge_y[c] = sources[pl.ds(152 * c, 8, stride=16), :]
    for k in range(12):
        face_x[k] = links[k % 6 + 9 * (k // 6), 7]
    table_copy.wait()
    sources[...] = right_dot(sources[...], table, Z_IN, False)
    encode(sources, 152, table, modes, packed, out)


def plane_kernel(own, recv, table, out, work, lines):
    lane = lax.broadcasted_iota(jnp.int32, (16, 128), 1) % 16
    zero = jnp.where(own[0] == 0, -1.0 / (LS * LS), 0.0)
    total = float_table(table, 1)
    work[pl.ds(0, 128), :] = total
    total = total + work[pl.ds(own[0], 1), :][:, 0:1]
    inverse = jnp.where(total > 0.0, 1.0 / jnp.where(total > 0.0, total, 1.0), 0.0)
    shifts = []
    moved = [
        swap_blocks([recv[pl.ds(3 * g + t, 16, stride=24), :] for g in range(8)])
        for t in range(3)
    ]
    for c in range(8):
        third = moved[2][c]
        rolled = pltpu.roll(third, 8, 1)
        first = moved[0][c] + pltpu.roll(moved[1][c], 1, 0) + jnp.where(lane == 0, rolled, 0.0)
        work[pl.ds(16 * c, 16), :] = first
        both = third + rolled
        for x in range(1, 8):
            work[pl.ds(128 * x + 16 * c, 16), :] = jnp.where(lane == x, both, 0.0)
        extra = jnp.sum(jnp.where(lane == 0, third, 0.0), axis=0, keepdims=True)
        shifts.append(jnp.sum(extra, axis=1, keepdims=True) * zero)
    lines[pl.ds(0, 128), :] = right_dot(work[pl.ds(0, 128), :], table, Y_IN, False)
    lines[pl.ds(128, 896), :] = right_dot(work[pl.ds(128, 896), :], table, LINES_IN, False)
    blocks = [
        jnp.concatenate([lines[pl.ds(128 * x + 16 * c, 16), :] for x in range(8)], axis=0)
        for c in range(8)
    ]
    spectrum = left_dot(table, X_IN, blocks, False)
    spectrum = left_dot(table, X_OUT, [tile(spectrum, c) * inverse for c in range(8)], True)
    spectrum = [tile(spectrum, c) for c in range(8)]
    at_lines = right_dot(jnp.concatenate(spectrum, axis=0), table, LINES_OUT, True)
    first = jnp.concatenate([part[:16] for part in spectrum], axis=0)
    first = right_dot(first, table, Z_OUT, True)
    groups = [[], [], []]
    for c in range(8):
        own_line = first[16 * c : 16 * c + 16] + shifts[c]
        groups[0].append(own_line)
        groups[1].append(pltpu.roll(own_line, 15, 0))
        parts = [at_lines[128 * c + 16 * x : 128 * c + 16 * x + 16] for x in range(8)]
        third = jnp.where(lane == 0, pltpu.roll(parts[7], 1, 0), parts[0])
        for x in range(1, 8):
            third = jnp.where((lane == x) | (lane == 8 + x), parts[x], third)
        groups[2].append(third + shifts[c])
    for t in range(3):
        tiles = swap_blocks(groups[t])
        for g in range(8):
            out[pl.ds(3 * g + t, 16, stride=24), :] = tiles[g]


def decode(recv, modes, table, packed, comps_in):
    for t in range(3):
        packed[pl.ds(128 * t, 128), :] = recv[pl.ds(t, 128, stride=3), :].T
    mass = float_table(table, 1, 16)[0:1]
    inverse = float_table(table, 0)
    values = [
        jnp.concatenate([packed[pl.ds(128 * t + 16 * c, 16), :] for t in range(3)], axis=0)
        for c in range(8)
    ]
    mode = dot(table[SOURCE], jnp.concatenate([products(value, 0, True) for value in values], axis=1))
    stacks = []
    for c in range(8):
        own = modes[c] + inverse * tile(mode, c)
        stacks.append(own)
    sites = left_dot(table, EXPAND, stacks, True)
    exact = [jnp.concatenate(parts_of(value), axis=0) for value in values]
    sites = sites + dot(table[EXPAND_LINES], jnp.concatenate(exact, axis=1))
    row = lax.broadcasted_iota(jnp.int32, (16, 128), 0)
    parts = []
    for c in range(8):
        part, value = tile(sites, c), values[c]
        behind = part[144:160] + mass * jnp.where(row == 0, 0.0, value[0:16])
        below = part[168:176] + mass * jnp.where(row[:8] == 0, value[0:8], value[32:40])
        parts.append(jnp.concatenate([part[:144], behind, part[160:168], below], axis=0))
    for k in range(0, 8, 2):
        group = jnp.concatenate(parts[k : k + 2], axis=0)
        comps_in[pl.ds(176 * k, 352), :] = right_dot(group, table, Z_OUT, True)


def make(c, before=None):
    re6, im6 = exponent_rows(c)
    if before is not None:
        re6, im6 = times_rows(re6, im6, before[:9], before[9:])
    return full_matrix(re6, im6)


def start_links(links_hbm, links, sems):
    def plane_copy(x):
        return pltpu.make_async_copy(links_hbm.at[:, x], links.at[:, x], sems.at[x])

    for x in range(8):
        plane_copy(x).start()
    return plane_copy


def moved_divergence(links, plane_copy, gs, ay, prev, emit):
    def sites(x, carry):
        plane_copy(x).wait()
        base = (x + 1) * PLANE
        for half in range(2):
            rows = pl.ds(8 * half, 8)
            start = 8 * half + 8
            total = [None] * 8

            def link_of(mu):
                return lambda p, i, j: links[18 * mu + 9 * p + entry(i, j), x, rows, :]

            g = [gs[pl.ds(base + 32 * k + start, 8), :] for k in range(18)]
            ahead = [gs[pl.ds(base + PLANE + 32 * k + start, 8), :] for k in range(18)]
            a = moved_algebra(g, link_of(0), ahead)
            for c in range(8):
                total[c] = prev[c, rows, :] - a[c]
                prev[c, rows, :] = a[c]
            ahead = [gs[pl.ds(base + 32 * k + start + 1, 8), :] for k in range(18)]
            a = moved_algebra(g, link_of(1), ahead)
            for c in range(8):
                ay[pl.ds(x * 192 + 24 * c + start, 8), :] = a[c]
            for c in range(8):
                total[c] = total[c] + (ay[pl.ds(x * 192 + 24 * c + start - 1, 8), :] - a[c])
            top = [v[7:8] for v in a]
            ahead = [pltpu.roll(v, 127, 1) for v in g]
            a = moved_algebra(g, link_of(2), ahead)
            for c in range(8):
                total[c] = total[c] + (pltpu.roll(a[c], 1, 1) - a[c])
            emit(x, half, total, top)
        return carry

    lax.fori_loop(0, 8, sites, 0)


def update_kernel(*refs):
    recv, modes, links_hbm, table = refs[:4]
    out, modes_out, edge_x, edge_y, theta, gout, gout_y, raw_x, raw_y = refs[4:13]
    links, sems, packed, comps_in, gs, ay, prev, sources = refs[13:]
    plane_copy = start_links(links_hbm, links, sems)
    decode(recv, modes, table, packed, comps_in)
    for c in range(8):
        raw_x[c] = comps_in[pl.ds(176 * c + 144, 16), :]
        raw_y[c] = comps_in[pl.ds(176 * c + 168, 8), :]

    def plane(index, first_row):
        for half in range(2):
            g = make([comps_in[pl.ds(first_row(c) + 8 * half, 8), :] for c in range(8)])
            for k in range(18):
                gs[pl.ds(index * PLANE + 32 * k + 8 * half + 8, 8), :] = g[k]
                gout[pl.ds((index - 1) * 288 + 16 * k + 8 * half, 8), :] = g[k]

    def inner(x, carry):
        plane(x + 1, lambda c: 176 * c + 16 * x)
        return carry

    lax.fori_loop(0, 8, inner, 0)
    plane(9, lambda c: 176 * c + 128)
    g = make([comps_in[pl.ds(176 * c + 160, 8), :] for c in range(8)])
    for k in range(18):
        gout_y[k] = g[k]
        gs[pl.ds(PLANE + 32 * k + 24, 8, stride=PLANE), :] = g[k]

    prev[...] = jnp.zeros_like(prev)
    theta[...] = jnp.zeros_like(theta)
    for c in range(8):
        ay[pl.ds(24 * c + 7, 8, stride=192), :] = jnp.zeros((8, 128), F32)
    row = lax.broadcasted_iota(jnp.int32, (8, 128), 0)

    def emit(x, half, total, top):
        for c in range(8):
            sources[pl.ds(152 * c + 16 * x + 8 * half, 8), :] = total[c]
            if half == 1:
                sources[pl.ds(152 * c + 144 + x, 1), :] = top[c]
        theta[...] += jnp.where((x > 0) & (row + half > 0), squares(total), 0.0)

    moved_divergence(links, plane_copy, gs, ay, prev, emit)
    for c in range(8):
        sources[pl.ds(152 * c + 128, 16), :] = prev[c]
        edge_x[c] = sources[pl.ds(152 * c, 16), :]
        edge_y[c] = sources[pl.ds(152 * c, 8, stride=16), :]
    sources[...] = right_dot(sources[...], table, Z_IN, False)
    encode(sources, 152, table, modes_out, packed, out)


def whole_lines(line_x, line_y, add_x, add_y):
    top = lax.broadcasted_iota(jnp.int32, (16, 128), 0) == 0
    out_x, out_y = [], []
    for c in range(8):
        out_x.append(line_x[c] + add_x[c] + jnp.where(top, add_y[c][0:1], 0.0))
        out_y.append(line_y[c] + add_y[c] + jnp.where(top[:8], add_x[c][0:1], 0.0))
    sq = squares(out_x)
    return out_x, out_y, sq[:8] + sq[8:] + jnp.where(top[:8], 0.0, squares(out_y))


def last_kernel(*refs):
    recv, modes, links_hbm, table, line0_x, line0_y, line1_x, line1_y, raw_x, raw_y = refs[:10]
    face_x, face_y, theta0, theta1, prior, prior_y, div_hbm, gauge_hbm, theta = refs[10:19]
    links, sems, packed, comps_in, gs, behind, below, ay, prev, acc, div, gauge, out_sems = refs[19:]
    plane_copy = start_links(links_hbm, links, sems)
    decode(recv, modes, table, packed, comps_in)
    row = lax.broadcasted_iota(jnp.int32, (16, 128), 0)

    face = full_matrix([face_x[k] for k in range(6)], [face_x[6 + k] for k in range(6)])
    add_x = algebra(lambda i, j: face[entry(i, j)], lambda i, j: face[9 + entry(i, j)])
    face = full_matrix([face_y[k] for k in range(6)], [face_y[6 + k] for k in range(6)])
    add_y = algebra(lambda i, j: face[entry(i, j)], lambda i, j: face[9 + entry(i, j)])
    whole_x, whole_y, extra0 = whole_lines(line0_x, line0_y, add_x, add_y)
    for half in range(2):
        rows = pl.ds(8 * half, 8)
        part = slice(8 * half, 8 * half + 8)
        taken = [jnp.where(row == 0, 0.0, SCALE * whole_x[c])[part] for c in range(8)]
        g = make([raw_x[c, rows, :] - taken[c] for c in range(8)])
        for k in range(18):
            behind[k, rows, :] = g[k]
        ahead = [prior[pl.ds(16 * k + 8 * half, 8), :] for k in range(18)]
        edge = moved_algebra(g, lambda p, i, j: face_x[6 * p + entry(i, j), rows, :], ahead)
        for c in range(8):
            prev[c, rows, :] = edge[c]
    g = make([raw_y[c] - SCALE * whole_y[c] for c in range(8)])
    for k in range(18):
        below[k] = g[k]
    ahead = [prior[pl.ds(16 * k, 8, stride=288), :] for k in range(18)]
    edge = moved_algebra(g, lambda p, i, j: face_y[6 * p + entry(i, j)], ahead)
    whole_x, whole_y, extra1 = whole_lines(line1_x, line1_y, prev, edge)

    for c in range(8):
        rows = pl.ds(176 * c + 144, 16)
        comps_in[rows, :] = comps_in[rows, :] - jnp.where(row == 0, 0.0, SCALE * whole_x[c])
        rows = pl.ds(176 * c + 168, 8)
        comps_in[rows, :] = comps_in[rows, :] - SCALE * whole_y[c]

    def plane(index, first_row, before):
        for half in range(2):
            rows = pl.ds(8 * half, 8)
            g = make([comps_in[pl.ds(first_row(c) + 8 * half, 8), :] for c in range(8)], before(half))
            for k in range(18):
                gs[pl.ds(index * PLANE + 32 * k + 8 * half + 8, 8), :] = g[k]
            if not isinstance(index, int):
                for p in range(2):
                    for i in range(2):
                        for j in range(3):
                            gauge[p, i, j, index - 1, rows, :] = g[9 * p + entry(i, j)]

    def before_at(index):
        return lambda half: [
            prior[pl.ds((index - 1) * 288 + 16 * k + 8 * half, 8), :] for k in range(18)
        ]

    def inner(x, carry):
        plane(x + 1, lambda c: 176 * c + 16 * x, before_at(x + 1))
        return carry

    lax.fori_loop(0, 8, inner, 0)
    gauge_copy = pltpu.make_async_copy(gauge, gauge_hbm, out_sems.at[8])
    gauge_copy.start()

    def div_copy(x):
        return pltpu.make_async_copy(div.at[:, x], div_hbm.at[:, x], out_sems.at[x])

    plane(
        0,
        lambda c: 176 * c + 144,
        lambda half: [behind[k, pl.ds(8 * half, 8), :] for k in range(18)],
    )
    plane(9, lambda c: 176 * c + 128, before_at(9))
    g = make(
        [comps_in[pl.ds(176 * c + 160, 8), :] for c in range(8)], [prior_y[k] for k in range(18)]
    )
    for k in range(18):
        gs[pl.ds(PLANE + 32 * k + 24, 8, stride=PLANE), :] = g[k]

    g = make([comps_in[pl.ds(176 * c + 168, 8), :] for c in range(8)], [below[k] for k in range(18)])
    ahead = [gs[pl.ds(PLANE + 32 * k + 8, 8, stride=PLANE), :] for k in range(18)]
    edge = moved_algebra(g, lambda p, i, j: face_y[6 * p + entry(i, j)], ahead)
    for c in range(8):
        ay[pl.ds(24 * c + 7, 8, stride=192), :] = edge[c]
    for half in range(2):
        rows = pl.ds(8 * half, 8)
        start = 8 * half + 8
        g = [gs[pl.ds(32 * k + start, 8), :] for k in range(18)]
        ahead = [gs[pl.ds(PLANE + 32 * k + start, 8), :] for k in range(18)]
        edge = moved_algebra(g, lambda p, i, j: face_x[6 * p + entry(i, j), rows, :], ahead)
        for c in range(8):
            prev[c, rows, :] = edge[c]

    acc[...] = jnp.zeros_like(acc)

    def emit(x, half, total, top):
        for c in range(8):
            div[c, x, pl.ds(8 * half, 8), :] = total[c]
        acc[...] += squares(total)
        if half == 1:
            div_copy(x).start()

    moved_divergence(links, plane_copy, gs, ay, prev, emit)
    lane = lax.broadcasted_iota(jnp.int32, (1, 128), 1)
    sums = jnp.zeros((1, 128), F32)
    for k, part in enumerate((theta0[...] + extra0, theta1[...] + extra1, acc[...])):
        sums = sums + jnp.where(lane == k, jnp.sum(part), 0.0)
    theta[...] = jnp.broadcast_to(sums * (1.0 / (3.0 * LS * LS * NZ)), (128, 128))
    gauge_copy.wait()
    for x in range(8):
        div_copy(x).wait()


def struct(*shape):
    return jax.ShapeDtypeStruct(shape, F32)


def vmem(*shape):
    return pltpu.VMEM(shape, F32)


def whole():
    return pl.BlockSpec(memory_space=pltpu.VMEM)


def in_hbm(value):
    return pltpu.with_memory_space_constraint(value, pltpu.HBM)


def params(size):
    return pltpu.CompilerParams(vmem_limit_bytes=size * MEGA)


EDGES = [(8, 16, 128), (8, 8, 128)]


def first_call(links, table):
    shapes = [struct(384, 128), struct(8, 128, 128)] + [struct(*e) for e in EDGES] + [struct(8, 128)]
    shapes += [jax.ShapeDtypeStruct(table.shape, table.dtype), struct(12, 16, 128), struct(12, 8, 128)]
    return pl.pallas_call(
        first_kernel,
        in_specs=[pl.BlockSpec(memory_space=pl.ANY)] * 2,
        out_specs=[whole()] * len(shapes),
        out_shape=shapes,
        scratch_shapes=[
            vmem(54, 8, 16, 128),
            vmem(8, 16, 128),
            vmem(8 * 152, 128),
            vmem(384, 128),
            pltpu.SemaphoreType.DMA((9,)),
        ],
        compiler_params=params(32),
        name="first_divergence",
    )(in_hbm(links), in_hbm(table))


def plane_call(own, recv, table):
    return pl.pallas_call(
        plane_kernel,
        in_specs=[pl.BlockSpec(memory_space=pltpu.SMEM)] + [whole()] * 2,
        out_specs=whole(),
        out_shape=struct(384, 128),
        scratch_shapes=[vmem(1024, 128), vmem(1024, 128)],
        compiler_params=params(32),
        name="plane_solve",
    )(own, recv, table)


def update_call(kernel, operands, shapes, extra, name, copied=0):
    scratch = [
        vmem(54, 8, 16, 128),
        pltpu.SemaphoreType.DMA((8,)),
        vmem(384, 128),
        vmem(8 * 176, 128),
        vmem(10 * PLANE, 128),
    ]
    return pl.pallas_call(
        kernel,
        in_specs=[pl.BlockSpec(memory_space=pl.ANY) if k == 2 else whole() for k in range(len(operands))],
        out_specs=[pl.BlockSpec(memory_space=pl.ANY)] * copied + [whole()] * (len(shapes) - copied),
        out_shape=shapes,
        scratch_shapes=scratch + extra,
        compiler_params=params(32),
        name=name,
    )(*operands)


def shifted(value, axis, steps):
    count = lax.axis_size(axis)
    pairs = [(source, (source + steps) % count) for source in range(count)]
    return lax.ppermute(value, axis, pairs)


def exchange(value):
    rows = value.reshape(128, 1, value.size // 128)
    rows = lax.all_to_all(rows, ("gx", "gy"), split_axis=0, concat_axis=0, tiled=True)
    return rows.reshape(value.shape)


def per_device(links):
    flat = links.reshape(54, 8, 16, 128)
    own = (lax.axis_index("gx") * 8 + lax.axis_index("gy")).astype(jnp.int32).reshape(1)
    table = jnp.asarray(TABLE)
    packed, modes, edge_x, edge_y, theta, table, face_x, face_y = first_call(flat, table)
    face_x = shifted(face_x, "gx", 1)
    face_y = shifted(face_y, "gy", 1)
    packed, own = lax.optimization_barrier((packed, own))
    values = exchange(plane_call(own, exchange(packed), table))
    edges = [struct(*e) for e in EDGES]
    shapes = [struct(384, 128), struct(8, 128, 128)] + edges + [struct(8, 128)]
    shapes += [struct(9 * 288, 128), struct(18, 8, 128)] + edges
    packed, modes, edge1_x, edge1_y, theta1, prior, prior_y, raw_x, raw_y = update_call(
        update_kernel,
        [values, modes, in_hbm(flat), table],
        shapes,
        [vmem(8 * 192, 128), vmem(8, 16, 128), vmem(8 * 152, 128)],
        "update",
    )
    packed, face_x, face_y = lax.optimization_barrier((packed, face_x, face_y))
    values = exchange(plane_call(own, exchange(packed), table))
    operands = [values, modes, in_hbm(flat), table, edge_x, edge_y, edge1_x, edge1_y, raw_x, raw_y]
    operands += [face_x, face_y, theta, theta1, prior, prior_y]
    div, gauge, sums = update_call(
        last_kernel,
        operands,
        [struct(8, 8, 16, 128), struct(2, 2, 3, 8, 16, 128), struct(128, 128)],
        [vmem(18, 16, 128), vmem(18, 8, 128), vmem(8 * 192, 128), vmem(8, 16, 128), vmem(8, 128)]
        + [vmem(8, 8, 16, 128), vmem(2, 2, 3, 8, 16, 128), pltpu.SemaphoreType.DMA((9,))],
        "last_update",
        2,
    )
    return (gauge, div, jnp.sum(exchange(sums)[:, :3], axis=0))


def solution(mesh):
    in_specs = (P(None, None, None, None, "gx", "gy", "ta"),)
    out_specs = (P(None, None, None, "gx", "gy", "ta"), P(None, "gx", "gy", "ta"), P("ta"))
    return jax.shard_map(
        per_device, mesh=mesh, in_specs=in_specs, out_specs=out_specs, check_vma=False
    )
```

```python
import math

import jax
import jax.numpy as jnp
import numpy as np
from jax import lax
from jax.experimental import pallas as pl
from jax.experimental.pallas import tpu as pltpu
from jax.sharding import PartitionSpec as P

LS = 128
NZ = 128
STEP_SIZE = 0.08
PEAK_MOMENTUM = 12.0
F32 = jnp.float32
BF16 = jnp.bfloat16
MEGA = 1024 * 1024


def real_basis(length):
    site = np.arange(length)[:, None]
    freq = np.arange(length)
    freq = np.where(freq <= length // 2, freq, freq - length // 2)
    phase = 2.0 * np.pi * ((site * freq[None, :]) % length) / length
    index = np.arange(length)[None, :]
    basis = np.where(index <= length // 2, np.cos(phase), np.sin(phase)) * np.sqrt(2.0 / length)
    basis[:, 0] = 1.0 / np.sqrt(length)
    basis[:, length // 2] = np.cos(np.pi * np.arange(length)) / np.sqrt(length)
    return basis, freq


def thirds(table):
    rest, out = table.astype(np.float32).astype(np.float64), []
    for _ in range(3):
        piece = rest.astype(np.float32).astype(jnp.bfloat16)
        out.append(piece)
        rest = rest - piece.astype(np.float64)
    return out


def right_table(table):
    return np.concatenate(thirds(table), axis=0)


def left_table(table):
    return np.concatenate(thirds(table), axis=1)


def sine_table():
    x, y = np.arange(8), np.arange(16)
    sx = np.sin(np.pi * np.outer(x, x) / 8.0) * np.sqrt(2.0 / 8.0)
    sy = np.sin(np.pi * np.outer(y, y) / 16.0) * np.sqrt(2.0 / 16.0)
    table = np.kron(sx, sy)
    keep = np.kron(x > 0, y > 0)
    table = table * np.outer(keep, keep)
    eigen = (4.0 * np.sin(np.pi * x / 16.0) ** 2)[:, None] + (4.0 * np.sin(np.pi * y / 32.0) ** 2)[None, :]
    return table, eigen.reshape(128), keep


BASIS, FREQ = real_basis(128)
SQUARES = 4.0 * np.sin(np.pi * FREQ / 128.0) ** 2
SINE, EIGEN, INNER = sine_table()


def node(x, y):
    return 16 * x + y


def reduce_table():
    out = np.zeros((48, 128))
    for y in range(1, 16):
        out[y] = SINE[node(1, y)]
        out[16 + y] = SINE[node(7, y)]
    out[32] = SINE[INNER].sum(0)
    for x in range(1, 8):
        out[32 + x] = SINE[node(x, 1)]
        out[40 + x] = SINE[node(x, 15)]
    return out


def source_table():
    out = np.zeros((128, 48))
    for y in range(1, 16):
        out[:, y] = SINE[node(1, y)]
        out[:, 16 + y] = SINE[node(7, y)]
    for x in range(1, 8):
        out[:, 32 + x] = SINE[node(x, 1)]
        out[:, 40 + x] = SINE[node(x, 15)]
    return out


def expand_table():
    out = np.zeros((176, 176))
    val = 128

    def line_x(x):
        return 0 if x == 0 else (16 if x == 8 else 32 + x)

    def line_y(y):
        return 40 if y == 16 else y

    for x in range(1, 8):
        for y in range(1, 16):
            out[node(x, y), :128] = SINE[node(x, y)]
    for y in range(16):
        out[node(0, y), val + y] = 1.0
        out[128 + y, val + 16 + y] = 1.0
    for x in range(1, 8):
        out[node(x, 0), val + 32 + x] = 1.0
    for x in range(8):
        out[160 + x, val + 40 + x] = 1.0
    out[144, val + 32] = 1.0
    for y in range(1, 16):
        row = out[144 + y]
        row[val + y] += 4.0
        row[:128] -= SINE[node(1, y)]
        row[val + line_y(y - 1)] -= 1.0
        row[val + line_y(y + 1)] -= 1.0
    for x in range(1, 8):
        row = out[168 + x]
        row[val + line_x(x)] += 4.0
        row[:128] -= SINE[node(x, 1)]
        row[val + line_x(x - 1)] -= 1.0
        row[val + line_x(x + 1)] -= 1.0
    row = out[168]
    row[val] += 4.0
    row[val + 33] -= 1.0
    row[val + 32] -= 1.0
    row[val + 1] -= 1.0
    values = thirds(out[:, 128:])[0]
    return np.concatenate([left_table(out[:, :128]), values, values, values], axis=1)


def lines_in():
    out = np.zeros((128, 128))
    for g in range(8):
        out[16 * g : 16 * g + 16] = BASIS[16 * g]
    return out


def lines_out():
    out = np.zeros((128, 128))
    for g in range(8):
        out[:, 16 * g : 16 * g + 8] = BASIS[16 * g][:, None]
        out[:, 16 * g + 8 : 16 * g + 16] = BASIS[(16 * g + 16) % 128][:, None]
    return out


SCALE = STEP_SIZE * PEAK_MOMENTUM
ORDER = np.array([8 * j + x for x in range(8) for j in range(16)])


def pack_tables():
    out = np.zeros((992, 768), jnp.bfloat16)
    rights = (BASIS * SCALE, BASIS.T, BASIS, lines_in(), lines_out())
    for k, table in enumerate(rights):
        out[:384, 128 * k : 128 * k + 128] = right_table(table)
    out[384:512, :384] = left_table(SINE)
    out[384:512, 384:] = left_table(BASIS[ORDER].T)
    out[512:640, :384] = left_table(BASIS[ORDER])
    high, middle, low = thirds(source_table())
    out[512:640, 384:672] = np.concatenate([high, high, high, middle, middle, low], axis=1)
    out[640:688, :384] = left_table(reduce_table())
    out[688:864, :528] = expand_table()
    for k, table in enumerate((INVERSE, PLANE_SUM)):
        out[864:992, 384 * k : 384 * k + 384] = left_table(table)
    return out


INVERSE = INNER[:, None] / (np.where(INNER, EIGEN, 1.0)[:, None] + SQUARES[None, :])
PLANE_SUM = SQUARES[:, None] + SQUARES[None, :]
TABLE = pack_tables()
Z_IN, Z_OUT, Y_IN, LINES_IN, LINES_OUT = [(slice(0, 384), slice(128 * k, 128 * k + 128)) for k in range(5)]
MODES = (slice(384, 512), slice(0, 384))
X_IN = (slice(384, 512), slice(384, 768))
X_OUT = (slice(512, 640), slice(0, 384))
SOURCE = (slice(512, 640), slice(384, 672))
REDUCE = (slice(640, 688), slice(0, 384))
EXPAND = (slice(688, 864), slice(0, 384))
EXPAND_LINES = (slice(688, 864), slice(384, 528))


def float_table(table, which, rows=128):
    parts = [
        table[864 : 864 + rows, 384 * which + 128 * k : 384 * which + 128 * k + 128].astype(F32)
        for k in range(3)
    ]
    return (parts[0] + parts[1]) + parts[2]


def parts_of(value):
    high = value.astype(BF16)
    rest = value - high.astype(F32)
    middle = rest.astype(BF16)
    return high, middle, (rest - middle.astype(F32)).astype(BF16)


def products(value, axis, fine):
    high, middle, low = parts_of(value)
    parts = [high, middle, low, high, middle, high] if fine else [high, middle, high]
    return jnp.concatenate(parts, axis=axis)


def chosen(fine):
    return (0, 0, 0, 1, 1, 2) if fine else (0, 0, 1)


def right_dot(value, table, place, fine):
    rows, lanes = place
    parts = [table[rows.start + 128 * k : rows.start + 128 * k + 128, lanes] for k in chosen(fine)]
    return dot(products(value, 1, fine), jnp.concatenate(parts, axis=0))


def left_dot(table, place, pieces, fine):
    rows, lanes = place
    parts = [table[rows, lanes.start + 128 * k : lanes.start + 128 * k + 128] for k in chosen(fine)]
    pieces = [products(piece, 0, fine) for piece in pieces]
    return dot(jnp.concatenate(parts, axis=1), jnp.concatenate(pieces, axis=1))


def swap_blocks(tiles):
    tiles = list(tiles)
    group = lax.broadcasted_iota(jnp.int32, tiles[0].shape, 1) // 16
    for bit in (1, 2, 4):
        upper = (group & bit) != 0
        for i in range(8):
            if i & bit:
                continue
            low, high = tiles[i], tiles[i | bit]
            tiles[i] = jnp.where(upper, pltpu.roll(high, 16 * bit, 1), low)
            tiles[i | bit] = jnp.where(upper, high, pltpu.roll(low, 128 - 16 * bit, 1))
    return tiles


def algebra(mreal, mimag):
    i00, i11, i22 = mimag(0, 0), mimag(1, 1), mimag(2, 2)
    middle = (i00 + i11 + i22) * (1.0 / 3.0)
    return [
        i00 - middle,
        i11 - middle,
        (mreal(0, 1) - mreal(1, 0)) * 0.5,
        (mimag(0, 1) + mimag(1, 0)) * 0.5,
        (mreal(0, 2) - mreal(2, 0)) * 0.5,
        (mimag(0, 2) + mimag(2, 0)) * 0.5,
        (mreal(1, 2) - mreal(2, 1)) * 0.5,
        (mimag(1, 2) + mimag(2, 1)) * 0.5,
    ]


def squares(c):
    third = c[0] + c[1]
    rest = c[2] * c[2] + c[3] * c[3] + c[4] * c[4] + c[5] * c[5] + c[6] * c[6] + c[7] * c[7]
    return c[0] * c[0] + c[1] * c[1] + third * third + 2.0 * rest


def entry(row, col):
    return row * 3 + col


def cross_row(first_re, first_im, second_re, second_im):
    out_re, out_im = [], []
    for k in range(3):
        a, b = (k + 1) % 3, (k + 2) % 3
        out_re.append(
            first_re[a] * second_re[b]
            - first_im[a] * second_im[b]
            - first_re[b] * second_re[a]
            + first_im[b] * second_im[a]
        )
        out_im.append(
            first_re[b] * second_im[a]
            + first_im[b] * second_re[a]
            - first_re[a] * second_im[b]
            - first_im[a] * second_re[b]
        )
    return out_re, out_im


def exponent_rows(c):
    c0, c1, c2, c3, c4, c5, c6, c7 = c
    n01 = c2 * c2 + c3 * c3
    n02 = c4 * c4 + c5 * c5
    n12 = c6 * c6 + c7 * c7
    s00 = 1.0 - 0.5 * (c0 * c0 + n01 + n02)
    s11 = 1.0 - 0.5 * (c1 * c1 + n01 + n12)
    d01 = c0 + c1
    p01r = -(d01 * c3) - (c4 * c6 + c5 * c7)
    p01i = d01 * c2 - (c5 * c6 - c4 * c7)
    p02r = c1 * c5 + (c2 * c6 - c3 * c7)
    p02i = -(c1 * c4) + (c2 * c7 + c3 * c6)
    p12r = -(c2 * c4 + c3 * c5) + c0 * c7
    p12i = -(c2 * c5 - c3 * c4) - c0 * c6
    r0 = [s00, c2 + 0.5 * p01r, c4 + 0.5 * p02r]
    i0 = [c0, c3 + 0.5 * p01i, c5 + 0.5 * p02i]
    r1 = [-c2 + 0.5 * p01r, s11, c6 + 0.5 * p12r]
    i1 = [c3 - 0.5 * p01i, c1, c7 + 0.5 * p12i]
    size = sum(r0[k] * r0[k] + i0[k] * i0[k] for k in range(3))
    scale = lax.rsqrt(size)
    r0 = [v * scale for v in r0]
    i0 = [v * scale for v in i0]
    pr = sum(r0[k] * r1[k] + i0[k] * i1[k] for k in range(3))
    pi = sum(r0[k] * i1[k] - i0[k] * r1[k] for k in range(3))
    r1, i1 = (
        [r1[k] - (pr * r0[k] - pi * i0[k]) for k in range(3)],
        [i1[k] - (pr * i0[k] + pi * r0[k]) for k in range(3)],
    )
    size = sum(r1[k] * r1[k] + i1[k] * i1[k] for k in range(3))
    scale = lax.rsqrt(size)
    r1 = [v * scale for v in r1]
    i1 = [v * scale for v in i1]
    return r0 + r1, i0 + i1


def full_matrix(re6, im6):
    re3, im3 = cross_row(re6[:3], im6[:3], re6[3:], im6[3:])
    return list(re6) + re3 + list(im6) + im3


def times_rows(gre, gim, hre, him):
    out_re, out_im = [], []
    for i in range(2):
        for j in range(3):
            acc_re = acc_im = None
            for k in range(3):
                ar, ai = gre[entry(i, k)], gim[entry(i, k)]
                br, bi = hre[entry(k, j)], him[entry(k, j)]
                pr, pi = ar * br - ai * bi, ar * bi + ai * br
                acc_re = pr if acc_re is None else acc_re + pr
                acc_im = pi if acc_im is None else acc_im + pi
            out_re.append(acc_re)
            out_im.append(acc_im)
    return out_re, out_im


def moved_algebra(g, link, ahead):
    gre, gim = g[:9], g[9:]
    are, aim = ahead[:9], ahead[9:]
    vre, vim = [None] * 9, [None] * 9
    for i in range(2):
        ur = [link(0, i, k) for k in range(3)]
        ui = [link(1, i, k) for k in range(3)]
        for j in range(3):
            br = [are[entry(j, k)] for k in range(3)]
            bi = [aim[entry(j, k)] for k in range(3)]
            vre[entry(i, j)] = (ur[0] * br[0] + ui[0] * bi[0]) + (
                (ur[1] * br[1] + ui[1] * bi[1]) + (ur[2] * br[2] + ui[2] * bi[2])
            )
            vim[entry(i, j)] = (ui[0] * br[0] - ur[0] * bi[0]) + (
                (ui[1] * br[1] - ur[1] * bi[1]) + (ui[2] * br[2] - ur[2] * bi[2])
            )

    vre[6:], vim[6:] = cross_row(vre[:3], vim[:3], vre[3:6], vim[3:6])

    def mreal(i, j):
        return sum(
            gre[entry(i, k)] * vre[entry(k, j)] - gim[entry(i, k)] * vim[entry(k, j)]
            for k in range(3)
        )

    def mimag(i, j):
        return sum(
            gre[entry(i, k)] * vim[entry(k, j)] + gim[entry(i, k)] * vre[entry(k, j)]
            for k in range(3)
        )

    return algebra(mreal, mimag)


PLANE = 18 * 32


def dot(left, right):
    return jnp.dot(left, right, preferred_element_type=F32)


def tile(value, c):
    return value[:, 128 * c : 128 * c + 128]


def encode(spectrum, stride, table, modes, packed, out):
    mode = left_dot(table, MODES, [spectrum[pl.ds(stride * c, 128), :] for c in range(8)], False)
    inverse = float_table(table, 0)
    scaled = []
    for c in range(8):
        scaled.append(inverse * tile(mode, c))
        modes[c] = scaled[c]
    reduced = left_dot(table, REDUCE, scaled, False)
    corner = lax.broadcasted_iota(jnp.int32, (8, 128), 0) == 0
    for c in range(8):
        start = stride * c
        values = tile(reduced, c)
        line_x = values[0:16] + spectrum[pl.ds(start, 16), :]
        line_y = jnp.where(corner, 0.0, spectrum[pl.ds(start, 8, stride=16), :])
        next_x, next_y = values[16:32], values[40:48]
        if stride > 128:
            next_x = next_x + spectrum[pl.ds(start + 128, 16), :]
            next_y = next_y + spectrum[pl.ds(start + 144, 8), :]
        groups = [line_x, next_x, jnp.concatenate([values[32:40] + line_y, next_y], axis=0)]
        for t in range(3):
            packed[pl.ds(128 * t + 16 * c, 16), :] = groups[t]
    for t in range(3):
        out[pl.ds(t, 128, stride=3), :] = packed[pl.ds(128 * t, 128), :].T


def first_kernel(*refs):
    links_hbm, table_hbm, out, modes, edge_x, edge_y, theta, table, face_x, face_y = refs[:10]
    links, prev, sources, packed, sems = refs[10:]

    def plane_copy(x):
        return pltpu.make_async_copy(links_hbm.at[:, x], links.at[:, x], sems.at[x])

    for x in range(8):
        plane_copy(x).start()
    table_copy = pltpu.make_async_copy(table_hbm, table, sems.at[8])
    table_copy.start()
    prev[...] = jnp.zeros_like(prev)
    theta[...] = jnp.zeros_like(theta)
    row = lax.broadcasted_iota(jnp.int32, (16, 128), 0)

    def planes(x, carry):
        plane_copy(x).wait()

        def of(mu):
            return algebra(
                lambda i, j: links[18 * mu + entry(i, j), x],
                lambda i, j: links[18 * mu + 9 + entry(i, j), x],
            )

        ax, ay, az = of(0), of(1), of(2)
        comps = []
        for c in range(8):
            back_y = jnp.where(row == 0, 0.0, pltpu.roll(ay[c], 1, 0))
            value = (prev[c] + back_y + pltpu.roll(az[c], 1, 1)) - ax[c] - ay[c] - az[c]
            prev[c] = ax[c]
            comps.append(value)
            sources[pl.ds(152 * c + 16 * x, 16), :] = value
            sources[pl.ds(152 * c + 144 + x, 1), :] = ay[c][15:16]
        for k in range(12):
            face_y[k, pl.ds(x, 1), :] = links[18 + k % 6 + 9 * (k // 6), x, 15:16, :]
        inner = jnp.where((row > 0) & (x > 0), squares(comps), 0.0)
        theta[...] += inner[:8] + inner[8:]
        return carry

    lax.fori_loop(0, 8, planes, 0)
    for c in range(8):
        sources[pl.ds(152 * c + 128, 16), :] = prev[c]
        edge_x[c] = sources[pl.ds(152 * c, 16), :]
        edge_y[c] = sources[pl.ds(152 * c, 8, stride=16), :]
    for k in range(12):
        face_x[k] = links[k % 6 + 9 * (k // 6), 7]
    table_copy.wait()
    sources[...] = right_dot(sources[...], table, Z_IN, False)
    encode(sources, 152, table, modes, packed, out)


def plane_kernel(own, recv, table, out, work, lines):
    lane = lax.broadcasted_iota(jnp.int32, (16, 128), 1) % 16
    zero = jnp.where(own[0] == 0, -1.0 / (LS * LS), 0.0)
    total = float_table(table, 1)
    work[pl.ds(0, 128), :] = total
    total = total + work[pl.ds(own[0], 1), :][:, 0:1]
    inverse = jnp.where(total > 0.0, 1.0 / jnp.where(total > 0.0, total, 1.0), 0.0)
    shifts = []
    moved = [
        swap_blocks([recv[pl.ds(3 * g + t, 16, stride=24), :] for g in range(8)])
        for t in range(3)
    ]
    for c in range(8):
        third = moved[2][c]
        rolled = pltpu.roll(third, 8, 1)
        first = moved[0][c] + pltpu.roll(moved[1][c], 1, 0) + jnp.where(lane == 0, rolled, 0.0)
        work[pl.ds(16 * c, 16), :] = first
        both = third + rolled
        for x in range(1, 8):
            work[pl.ds(128 * x + 16 * c, 16), :] = jnp.where(lane == x, both, 0.0)
        extra = jnp.sum(jnp.where(lane == 0, third, 0.0), axis=0, keepdims=True)
        shifts.append(jnp.sum(extra, axis=1, keepdims=True) * zero)
    lines[pl.ds(0, 128), :] = right_dot(work[pl.ds(0, 128), :], table, Y_IN, False)
    lines[pl.ds(128, 896), :] = right_dot(work[pl.ds(128, 896), :], table, LINES_IN, False)
    blocks = [
        jnp.concatenate([lines[pl.ds(128 * x + 16 * c, 16), :] for x in range(8)], axis=0)
        for c in range(8)
    ]
    spectrum = left_dot(table, X_IN, blocks, False)
    spectrum = left_dot(table, X_OUT, [tile(spectrum, c) * inverse for c in range(8)], True)
    spectrum = [tile(spectrum, c) for c in range(8)]
    at_lines = right_dot(jnp.concatenate(spectrum, axis=0), table, LINES_OUT, True)
    first = jnp.concatenate([part[:16] for part in spectrum], axis=0)
    first = right_dot(first, table, Z_OUT, True)
    groups = [[], [], []]
    for c in range(8):
        own_line = first[16 * c : 16 * c + 16] + shifts[c]
        groups[0].append(own_line)
        groups[1].append(pltpu.roll(own_line, 15, 0))
        parts = [at_lines[128 * c + 16 * x : 128 * c + 16 * x + 16] for x in range(8)]
        third = jnp.where(lane == 0, pltpu.roll(parts[7], 1, 0), parts[0])
        for x in range(1, 8):
            third = jnp.where((lane == x) | (lane == 8 + x), parts[x], third)
        groups[2].append(third + shifts[c])
    for t in range(3):
        tiles = swap_blocks(groups[t])
        for g in range(8):
            out[pl.ds(3 * g + t, 16, stride=24), :] = tiles[g]


def decode(recv, modes, table, packed, comps_in):
    for t in range(3):
        packed[pl.ds(128 * t, 128), :] = recv[pl.ds(t, 128, stride=3), :].T
    mass = float_table(table, 1, 16)[0:1]
    inverse = float_table(table, 0)
    values = [
        jnp.concatenate([packed[pl.ds(128 * t + 16 * c, 16), :] for t in range(3)], axis=0)
        for c in range(8)
    ]
    mode = dot(table[SOURCE], jnp.concatenate([products(value, 0, True) for value in values], axis=1))
    stacks = []
    for c in range(8):
        own = modes[c] + inverse * tile(mode, c)
        stacks.append(own)
    sites = left_dot(table, EXPAND, stacks, True)
    exact = [jnp.concatenate(parts_of(value), axis=0) for value in values]
    sites = sites + dot(table[EXPAND_LINES], jnp.concatenate(exact, axis=1))
    row = lax.broadcasted_iota(jnp.int32, (16, 128), 0)
    parts = []
    for c in range(8):
        part, value = tile(sites, c), values[c]
        behind = part[144:160] + mass * jnp.where(row == 0, 0.0, value[0:16])
        below = part[168:176] + mass * jnp.where(row[:8] == 0, value[0:8], value[32:40])
        parts.append(jnp.concatenate([part[:144], behind, part[160:168], below], axis=0))
    for k in range(0, 8, 2):
        group = jnp.concatenate(parts[k : k + 2], axis=0)
        comps_in[pl.ds(176 * k, 352), :] = right_dot(group, table, Z_OUT, True)


def make(c, before=None):
    re6, im6 = exponent_rows(c)
    if before is not None:
        re6, im6 = times_rows(re6, im6, before[:9], before[9:])
    return full_matrix(re6, im6)


def start_links(links_hbm, links, sems):
    def plane_copy(x):
        return pltpu.make_async_copy(links_hbm.at[:, x], links.at[:, x], sems.at[x])

    for x in range(8):
        plane_copy(x).start()
    return plane_copy


def moved_divergence(links, plane_copy, gs, ay, prev, emit):
    def sites(x, carry):
        plane_copy(x).wait()
        base = (x + 1) * PLANE
        for half in range(2):
            rows = pl.ds(8 * half, 8)
            start = 8 * half + 8
            total = [None] * 8

            def link_of(mu):
                return lambda p, i, j: links[18 * mu + 9 * p + entry(i, j), x, rows, :]

            g = [gs[pl.ds(base + 32 * k + start, 8), :] for k in range(18)]
            ahead = [gs[pl.ds(base + PLANE + 32 * k + start, 8), :] for k in range(18)]
            a = moved_algebra(g, link_of(0), ahead)
            for c in range(8):
                total[c] = prev[c, rows, :] - a[c]
                prev[c, rows, :] = a[c]
            ahead = [gs[pl.ds(base + 32 * k + start + 1, 8), :] for k in range(18)]
            a = moved_algebra(g, link_of(1), ahead)
            for c in range(8):
                ay[pl.ds(x * 192 + 24 * c + start, 8), :] = a[c]
            for c in range(8):
                total[c] = total[c] + (ay[pl.ds(x * 192 + 24 * c + start - 1, 8), :] - a[c])
            top = [v[7:8] for v in a]
            ahead = [pltpu.roll(v, 127, 1) for v in g]
            a = moved_algebra(g, link_of(2), ahead)
            for c in range(8):
                total[c] = total[c] + (pltpu.roll(a[c], 1, 1) - a[c])
            emit(x, half, total, top)
        return carry

    lax.fori_loop(0, 8, sites, 0)


def update_kernel(*refs):
    recv, modes, links_hbm, table = refs[:4]
    out, modes_out, edge_x, edge_y, theta, gout, gout_y, raw_x, raw_y = refs[4:13]
    links, sems, packed, comps_in, gs, ay, prev, sources = refs[13:]
    plane_copy = start_links(links_hbm, links, sems)
    decode(recv, modes, table, packed, comps_in)
    for c in range(8):
        raw_x[c] = comps_in[pl.ds(176 * c + 144, 16), :]
        raw_y[c] = comps_in[pl.ds(176 * c + 168, 8), :]

    def plane(index, first_row):
        for half in range(2):
            g = make([comps_in[pl.ds(first_row(c) + 8 * half, 8), :] for c in range(8)])
            for k in range(18):
                gs[pl.ds(index * PLANE + 32 * k + 8 * half + 8, 8), :] = g[k]
                gout[pl.ds((index - 1) * 288 + 16 * k + 8 * half, 8), :] = g[k]

    def inner(x, carry):
        plane(x + 1, lambda c: 176 * c + 16 * x)
        return carry

    lax.fori_loop(0, 8, inner, 0, unroll=2)
    plane(9, lambda c: 176 * c + 128)
    g = make([comps_in[pl.ds(176 * c + 160, 8), :] for c in range(8)])
    for k in range(18):
        gout_y[k] = g[k]
        gs[pl.ds(PLANE + 32 * k + 24, 8, stride=PLANE), :] = g[k]

    prev[...] = jnp.zeros_like(prev)
    theta[...] = jnp.zeros_like(theta)
    for c in range(8):
        ay[pl.ds(24 * c + 7, 8, stride=192), :] = jnp.zeros((8, 128), F32)
    row = lax.broadcasted_iota(jnp.int32, (8, 128), 0)

    def emit(x, half, total, top):
        for c in range(8):
            sources[pl.ds(152 * c + 16 * x + 8 * half, 8), :] = total[c]
            if half == 1:
                sources[pl.ds(152 * c + 144 + x, 1), :] = top[c]
        theta[...] += jnp.where((x > 0) & (row + half > 0), squares(total), 0.0)

    moved_divergence(links, plane_copy, gs, ay, prev, emit)
    for c in range(8):
        sources[pl.ds(152 * c + 128, 16), :] = prev[c]
        edge_x[c] = sources[pl.ds(152 * c, 16), :]
        edge_y[c] = sources[pl.ds(152 * c, 8, stride=16), :]
    sources[...] = right_dot(sources[...], table, Z_IN, False)
    encode(sources, 152, table, modes_out, packed, out)


def whole_lines(line_x, line_y, add_x, add_y):
    top = lax.broadcasted_iota(jnp.int32, (16, 128), 0) == 0
    out_x, out_y = [], []
    for c in range(8):
        out_x.append(line_x[c] + add_x[c] + jnp.where(top, add_y[c][0:1], 0.0))
        out_y.append(line_y[c] + add_y[c] + jnp.where(top[:8], add_x[c][0:1], 0.0))
    sq = squares(out_x)
    return out_x, out_y, sq[:8] + sq[8:] + jnp.where(top[:8], 0.0, squares(out_y))


def last_kernel(*refs):
    recv, modes, links_hbm, table, line0_x, line0_y, line1_x, line1_y, raw_x, raw_y = refs[:10]
    face_x, face_y, theta0, theta1, prior, prior_y, div_hbm, gauge_hbm, theta = refs[10:19]
    links, sems, packed, comps_in, gs, behind, below, ay, prev, acc, div, gauge, out_sems = refs[19:]
    plane_copy = start_links(links_hbm, links, sems)
    decode(recv, modes, table, packed, comps_in)
    row = lax.broadcasted_iota(jnp.int32, (16, 128), 0)

    face = full_matrix([face_x[k] for k in range(6)], [face_x[6 + k] for k in range(6)])
    add_x = algebra(lambda i, j: face[entry(i, j)], lambda i, j: face[9 + entry(i, j)])
    face = full_matrix([face_y[k] for k in range(6)], [face_y[6 + k] for k in range(6)])
    add_y = algebra(lambda i, j: face[entry(i, j)], lambda i, j: face[9 + entry(i, j)])
    whole_x, whole_y, extra0 = whole_lines(line0_x, line0_y, add_x, add_y)
    for half in range(2):
        rows = pl.ds(8 * half, 8)
        part = slice(8 * half, 8 * half + 8)
        taken = [jnp.where(row == 0, 0.0, SCALE * whole_x[c])[part] for c in range(8)]
        g = make([raw_x[c, rows, :] - taken[c] for c in range(8)])
        for k in range(18):
            behind[k, rows, :] = g[k]
        ahead = [prior[pl.ds(16 * k + 8 * half, 8), :] for k in range(18)]
        edge = moved_algebra(g, lambda p, i, j: face_x[6 * p + entry(i, j), rows, :], ahead)
        for c in range(8):
            prev[c, rows, :] = edge[c]
    g = make([raw_y[c] - SCALE * whole_y[c] for c in range(8)])
    for k in range(18):
        below[k] = g[k]
    ahead = [prior[pl.ds(16 * k, 8, stride=288), :] for k in range(18)]
    edge = moved_algebra(g, lambda p, i, j: face_y[6 * p + entry(i, j)], ahead)
    whole_x, whole_y, extra1 = whole_lines(line1_x, line1_y, prev, edge)

    for c in range(8):
        rows = pl.ds(176 * c + 144, 16)
        comps_in[rows, :] = comps_in[rows, :] - jnp.where(row == 0, 0.0, SCALE * whole_x[c])
        rows = pl.ds(176 * c + 168, 8)
        comps_in[rows, :] = comps_in[rows, :] - SCALE * whole_y[c]

    def plane(index, first_row, before):
        for half in range(2):
            rows = pl.ds(8 * half, 8)
            g = make([comps_in[pl.ds(first_row(c) + 8 * half, 8), :] for c in range(8)], before(half))
            for k in range(18):
                gs[pl.ds(index * PLANE + 32 * k + 8 * half + 8, 8), :] = g[k]
            if not isinstance(index, int):
                for p in range(2):
                    for i in range(2):
                        for j in range(3):
                            gauge[p, i, j, index - 1, rows, :] = g[9 * p + entry(i, j)]

    def before_at(index):
        return lambda half: [
            prior[pl.ds((index - 1) * 288 + 16 * k + 8 * half, 8), :] for k in range(18)
        ]

    def inner(x, carry):
        plane(x + 1, lambda c: 176 * c + 16 * x, before_at(x + 1))
        return carry

    lax.fori_loop(0, 8, inner, 0, unroll=2)
    gauge_copy = pltpu.make_async_copy(gauge, gauge_hbm, out_sems.at[8])
    gauge_copy.start()

    def div_copy(x):
        return pltpu.make_async_copy(div.at[:, x], div_hbm.at[:, x], out_sems.at[x])

    plane(
        0,
        lambda c: 176 * c + 144,
        lambda half: [behind[k, pl.ds(8 * half, 8), :] for k in range(18)],
    )
    plane(9, lambda c: 176 * c + 128, before_at(9))
    g = make(
        [comps_in[pl.ds(176 * c + 160, 8), :] for c in range(8)], [prior_y[k] for k in range(18)]
    )
    for k in range(18):
        gs[pl.ds(PLANE + 32 * k + 24, 8, stride=PLANE), :] = g[k]

    g = make([comps_in[pl.ds(176 * c + 168, 8), :] for c in range(8)], [below[k] for k in range(18)])
    ahead = [gs[pl.ds(PLANE + 32 * k + 8, 8, stride=PLANE), :] for k in range(18)]
    edge = moved_algebra(g, lambda p, i, j: face_y[6 * p + entry(i, j)], ahead)
    for c in range(8):
        ay[pl.ds(24 * c + 7, 8, stride=192), :] = edge[c]
    for half in range(2):
        rows = pl.ds(8 * half, 8)
        start = 8 * half + 8
        g = [gs[pl.ds(32 * k + start, 8), :] for k in range(18)]
        ahead = [gs[pl.ds(PLANE + 32 * k + start, 8), :] for k in range(18)]
        edge = moved_algebra(g, lambda p, i, j: face_x[6 * p + entry(i, j), rows, :], ahead)
        for c in range(8):
            prev[c, rows, :] = edge[c]

    acc[...] = jnp.zeros_like(acc)

    def emit(x, half, total, top):
        for c in range(8):
            div[c, x, pl.ds(8 * half, 8), :] = total[c]
        acc[...] += squares(total)
        if half == 1:
            div_copy(x).start()

    moved_divergence(links, plane_copy, gs, ay, prev, emit)
    lane = lax.broadcasted_iota(jnp.int32, (1, 128), 1)
    sums = jnp.zeros((1, 128), F32)
    for k, part in enumerate((theta0[...] + extra0, theta1[...] + extra1, acc[...])):
        sums = sums + jnp.where(lane == k, jnp.sum(part), 0.0)
    theta[...] = jnp.broadcast_to(sums * (1.0 / (3.0 * LS * LS * NZ)), (128, 128))
    gauge_copy.wait()
    for x in range(8):
        div_copy(x).wait()


def struct(*shape):
    return jax.ShapeDtypeStruct(shape, F32)


def vmem(*shape):
    return pltpu.VMEM(shape, F32)


def whole():
    return pl.BlockSpec(memory_space=pltpu.VMEM)


def in_hbm(value):
    return pltpu.with_memory_space_constraint(value, pltpu.HBM)


def params(size):
    return pltpu.CompilerParams(vmem_limit_bytes=size * MEGA)


EDGES = [(8, 16, 128), (8, 8, 128)]


def first_call(links, table):
    shapes = [struct(384, 128), struct(8, 128, 128)] + [struct(*e) for e in EDGES] + [struct(8, 128)]
    shapes += [jax.ShapeDtypeStruct(table.shape, table.dtype), struct(12, 16, 128), struct(12, 8, 128)]
    return pl.pallas_call(
        first_kernel,
        in_specs=[pl.BlockSpec(memory_space=pl.ANY)] * 2,
        out_specs=[whole()] * len(shapes),
        out_shape=shapes,
        scratch_shapes=[
            vmem(54, 8, 16, 128),
            vmem(8, 16, 128),
            vmem(8 * 152, 128),
            vmem(384, 128),
            pltpu.SemaphoreType.DMA((9,)),
        ],
        compiler_params=params(32),
        name="first_divergence",
    )(in_hbm(links), in_hbm(table))


def plane_call(own, recv, table):
    return pl.pallas_call(
        plane_kernel,
        in_specs=[pl.BlockSpec(memory_space=pltpu.SMEM)] + [whole()] * 2,
        out_specs=whole(),
        out_shape=struct(384, 128),
        scratch_shapes=[vmem(1024, 128), vmem(1024, 128)],
        compiler_params=params(32),
        name="plane_solve",
    )(own, recv, table)


def update_call(kernel, operands, shapes, extra, name, copied=0):
    scratch = [
        vmem(54, 8, 16, 128),
        pltpu.SemaphoreType.DMA((8,)),
        vmem(384, 128),
        vmem(8 * 176, 128),
        vmem(10 * PLANE, 128),
    ]
    return pl.pallas_call(
        kernel,
        in_specs=[pl.BlockSpec(memory_space=pl.ANY) if k == 2 else whole() for k in range(len(operands))],
        out_specs=[pl.BlockSpec(memory_space=pl.ANY)] * copied + [whole()] * (len(shapes) - copied),
        out_shape=shapes,
        scratch_shapes=scratch + extra,
        compiler_params=params(32),
        name=name,
    )(*operands)


def shifted(value, axis, steps):
    count = lax.axis_size(axis)
    pairs = [(source, (source + steps) % count) for source in range(count)]
    return lax.ppermute(value, axis, pairs)


def exchange(value):
    rows = value.reshape(128, 1, value.size // 128)
    rows = lax.all_to_all(rows, ("gx", "gy"), split_axis=0, concat_axis=0, tiled=True)
    return rows.reshape(value.shape)


def per_device(links):
    flat = links.reshape(54, 8, 16, 128)
    own = (lax.axis_index("gx") * 8 + lax.axis_index("gy")).astype(jnp.int32).reshape(1)
    table = jnp.asarray(TABLE)
    packed, modes, edge_x, edge_y, theta, table, face_x, face_y = first_call(flat, table)
    face_x = shifted(face_x, "gx", 1)
    face_y = shifted(face_y, "gy", 1)
    packed, own = lax.optimization_barrier((packed, own))
    values = exchange(plane_call(own, exchange(packed), table))
    edges = [struct(*e) for e in EDGES]
    shapes = [struct(384, 128), struct(8, 128, 128)] + edges + [struct(8, 128)]
    shapes += [struct(9 * 288, 128), struct(18, 8, 128)] + edges
    packed, modes, edge1_x, edge1_y, theta1, prior, prior_y, raw_x, raw_y = update_call(
        update_kernel,
        [values, modes, in_hbm(flat), table],
        shapes,
        [vmem(8 * 192, 128), vmem(8, 16, 128), vmem(8 * 152, 128)],
        "update",
    )
    packed, face_x, face_y = lax.optimization_barrier((packed, face_x, face_y))
    values = exchange(plane_call(own, exchange(packed), table))
    operands = [values, modes, in_hbm(flat), table, edge_x, edge_y, edge1_x, edge1_y, raw_x, raw_y]
    operands += [face_x, face_y, theta, theta1, prior, prior_y]
    div, gauge, sums = update_call(
        last_kernel,
        operands,
        [struct(8, 8, 16, 128), struct(2, 2, 3, 8, 16, 128), struct(128, 128)],
        [vmem(18, 16, 128), vmem(18, 8, 128), vmem(8 * 192, 128), vmem(8, 16, 128), vmem(8, 128)]
        + [vmem(8, 8, 16, 128), vmem(2, 2, 3, 8, 16, 128), pltpu.SemaphoreType.DMA((9,))],
        "last_update",
        2,
    )
    return (gauge, div, jnp.sum(exchange(sums)[:, :3], axis=0))


def solution(mesh):
    in_specs = (P(None, None, None, None, "gx", "gy", "ta"),)
    out_specs = (P(None, None, None, "gx", "gy", "ta"), P(None, "gx", "gy", "ta"), P("ta"))
    return jax.shard_map(
        per_device, mesh=mesh, in_specs=in_specs, out_specs=out_specs, check_vma=False
    )
```
